128 devices in a mesh: dp: 16 (over y, z), fsdp: 8 (over x, core).
Axes of the slice: x: 4, y: 4, z: 4, core: 2. Of those that a mesh axis runs over, the one named last changes fastest.
Arguments:
- hidden: bfloat16 [65536, 5120], P(('dp', 'fsdp')), may hold values from -24 to 24
- advantages: bfloat16 [65536], P(('dp', 'fsdp')), may hold values from -4 to 4
- queries: bfloat16 [65536, 2560], P(('dp', 'fsdp')), may hold values from -6 to 6
- upstream: bfloat16 [65536, 2560], P(('dp', 'fsdp')), may hold values from -6 to 6
- ratios: float32 [65536], P(('dp', 'fsdp')), may hold values from 0.5 to 2
- key_weight: bfloat16 [5120, 512], P('fsdp'), may hold values from -0.078125 to 0.078125
- value_weight: bfloat16 [5120, 512], P('fsdp'), may hold values from -0.078125 to 0.078125
- lengths: int32 [16, 8, 16], replicated, may hold values from 8 to 32, as said below
- keep_flags: int32 [8, 16], replicated, may hold values from 0 to 1, as said below
- destinations: int32 [16, 8, 16], replicated, may hold values from 0 to 15, as said below
- offsets: int32 [16, 8, 16], replicated, may hold values from 0 to 511, as said below
Outputs:
- attention: bfloat16 [65536, 2560], P(('dp', 'fsdp'))
- grad_key: float32 [5120, 512], P('fsdp')
- grad_value: float32 [5120, 512], P('fsdp')
The draws below stay inside these ranges and needn't reach their ends.
Inputs may be any that keep to these rules, and one draw needn't show every extreme that they name: `lengths`: in every index of fsdp some rollout of a kept prompt has exactly 32 tokens. `keep_flags`: 1 where a prompt's rollouts differ in reward; every index of fsdp has kept and dropped prompts. `destinations`: A rollout stays at its fsdp index. The rollouts of one device go to different dp indices, so every dp index receives exactly one rollout slot from every device with its fsdp index (moved only if kept). `offsets`: kept rollouts arriving at a device lie within its 512 rows, packed without gaps from row 0 in order of the sending dp index; dropped rollouts carry 512 - 1, which has no meaning.
All inputs are finite; a program needn't handle non-finite values.
Results may differ from the reference program's by a relative error of at most 0.0087.
Values may be sent and summed in bfloat16 or wider, within the bound.
No kernel may reach another device: no remote copies, remote signals or barrier semaphores. Data moves between devices by JAX's collectives and lax.ppermute only.
A program may use at most 128 MiB of HBM per device.

```python
import math
import jax
import jax.numpy as jnp
from jax import lax

D = 5120
HD = 128
HQ = 20
KVH = 4
GROUP = 16
MAXLEN = 32
ROLL_DEV = 16
PROMPTS = 16
OUT_DEV = 512
ROWS = 65536
KVW = 512
QW = 2560
N_DP = 16
N_FSDP = 8


def rollout_plan(key):
    key_len, key_keep, key_force, key_pick, key_drop, key_perm = jax.random.split(key, 6)
    lowest = max(1, MAXLEN // 4)
    lengths = jax.random.randint(key_len, (N_DP, N_FSDP, ROLL_DEV), lowest, MAXLEN + 1)
    keep_flags = (jax.random.randint(key_keep, (N_FSDP, PROMPTS), 0, 4) > 0).astype(jnp.int32)
    force_dp = jax.random.randint(key_force, (N_FSDP,), 0, N_DP)
    force_slot = jax.random.randint(key_pick, (N_FSDP,), 0, ROLL_DEV)
    dp_ids = jnp.arange(N_DP)[:, None, None]
    slot_ids = jnp.arange(ROLL_DEV)[None, None, :]
    forced = (dp_ids == force_dp[None, :, None]) & (slot_ids == force_slot[None, :, None])
    lengths = jnp.where(forced, MAXLEN, lengths)
    force_prompt = (force_dp * ROLL_DEV + force_slot) // GROUP
    drop_prompt = (force_prompt + 1 + jax.random.randint(key_drop, (N_FSDP,), 0, PROMPTS - 1)) % PROMPTS
    prompt_ids = jnp.arange(PROMPTS)[None, :]
    keep_flags = jnp.where(prompt_ids == drop_prompt[:, None], 0, keep_flags)
    keep_flags = jnp.where(prompt_ids == force_prompt[:, None], 1, keep_flags)
    orders = jax.vmap(lambda sub: jax.random.permutation(sub, N_DP))(jax.random.split(key_perm, N_FSDP))
    diagonal = (dp_ids + slot_ids) % N_DP
    destinations = orders[jnp.arange(N_FSDP)[None, :, None], diagonal]
    prompt_of = (jnp.arange(N_DP * ROLL_DEV) // GROUP).reshape(N_DP, ROLL_DEV)
    kept_flag = jnp.transpose(jnp.take(keep_flags, prompt_of, axis=1), (1, 0, 2))
    kept_length = lengths * kept_flag
    back_index = jnp.broadcast_to((jnp.arange(N_DP)[None, None, :] - dp_ids) % N_DP, kept_length.shape)
    by_target = jnp.take_along_axis(kept_length, back_index, axis=2)
    before = jnp.cumsum(by_target, axis=0) - by_target
    offsets = jnp.take_along_axis(before, jnp.broadcast_to(diagonal, kept_length.shape), axis=2)
    offsets = jnp.where(kept_length > 0, offsets, OUT_DEV - 1)
    return (lengths.astype(jnp.int32), keep_flags.astype(jnp.int32), destinations.astype(jnp.int32), offsets.astype(jnp.int32))


def draw_lengths(key, part):
    return rollout_plan(key)[0]


def draw_keep_flags(key, part):
    return rollout_plan(key)[1]


def draw_destinations(key, part):
    return rollout_plan(key)[2]


def draw_offsets(key, part):
    return rollout_plan(key)[3]


def strengthened(drawn, own_key, source, target, parts, factor):
    owner, partner = [(jnp.arange(drawn.shape[axis_at]) // (drawn.shape[axis_at] // parts)).reshape([-1 if axis == axis_at else 1 for axis in range(drawn.ndim)]) for axis_at in (source, target)]
    chosen = jax.random.permutation(own_key, parts)[partner]
    strong = (owner == chosen) | (owner == (partner + parts // 2) % parts)
    return jnp.where(strong, factor * drawn, drawn)


def steps_of(stream_key, dims, cuts, smallest, high):
    factor_of, own = 1.0, jax.random.fold_in(stream_key, 6)
    for dim, shards_of in cuts:
        steps = jnp.exp(jax.random.uniform(jax.random.fold_in(own, dim), (shards_of,), jnp.float32, smallest / len(cuts), high / len(cuts)))
        factor_of = factor_of * jnp.repeat(steps, dims[dim] // shards_of).reshape([-1 if axis == dim else 1 for axis in range(len(dims))])
    return factor_of


def scatter_about(key, shape, width, most, cuts=(), kind=jnp.bfloat16):
    array = jax.random.normal(key, shape, jnp.float32) * width
    if len(cuts) > 0:
        array = steps_of(key, shape, cuts, -0.22, 0.18) * array
    return jnp.clip(array, min=-most, max=most).astype(kind)


def gaussian_with(stream_key, extent, width, most, cuts, heavy, kind=jnp.bfloat16):
    result = width * jax.random.normal(stream_key, extent, jnp.float32)
    if cuts:
        result = result * steps_of(stream_key, extent, cuts, -0.22, 0.18)
    return jnp.clip(strengthened(result, jax.random.fold_in(stream_key, 3), *heavy), -most, most).astype(kind)


def setup_inputs(seed: int = 0) -> dict:
    seeds = jax.random.split(jax.random.key(seed), 12)
    return {
        "hidden": gaussian_with(seeds[0], (ROWS, D), 1.0, 24.0, ((0, 128),), (0, 1, 128, 5.5)),
        "advantages": scatter_about(seeds[1], (ROWS,), 1.0, 4.0, ((0, 128),)),
        "queries": scatter_about(seeds[2], (ROWS, QW), 1.0, 6.0, ((0, 128),)),
        "upstream": scatter_about(seeds[3], (ROWS, QW), 1.0, 6.0, ((0, 128),)),
        "ratios": jnp.clip(jnp.exp(math.log(2.0) - 1.3862944 * jax.random.uniform(seeds[4], (ROWS,), jnp.float32) ** steps_of(seeds[4], (ROWS,), ((0, 128),), -0.2, 0.2)), 0.5, 2.0),
        "key_weight": scatter_about(seeds[5], (D, KVW), D ** -0.5, 0.078125, ((0, 8),)),
        "value_weight": scatter_about(seeds[6], (D, KVW), D ** -0.5, 0.078125, ((0, 8),)),
        "lengths": draw_lengths(jax.random.fold_in(seeds[11], 71), 0),
        "keep_flags": draw_keep_flags(jax.random.fold_in(seeds[11], 71), 0),
        "destinations": draw_destinations(jax.random.fold_in(seeds[11], 71), 0),
        "offsets": draw_offsets(jax.random.fold_in(seeds[11], 71), 0),
    }


rope_base = 1000000.0
loss_scale = 256.0
clip_low = 0.8
clip_high = 1.28

def rope_tables(position, head_width):
    half_width = head_width // 2
    frequency = rope_base ** (-(jnp.arange(half_width).astype(jnp.float32) * (2.0 / head_width)))
    angle = position.astype(jnp.float32)[:, None] * frequency[None, :]
    return (jnp.cos(angle)[:, None, :], jnp.sin(angle)[:, None, :])

def rotate(values, cosine, sine):
    half_width = values.shape[-1] // 2
    first = values[..., :half_width]
    second = values[..., half_width:]
    return jnp.concatenate([first * cosine - second * sine, second * cosine + first * sine], axis=-1)

def unrotate(values, cosine, sine):
    half_width = values.shape[-1] // 2
    first = values[..., :half_width]
    second = values[..., half_width:]
    return jnp.concatenate([first * cosine + second * sine, second * cosine - first * sine], axis=-1)

def kept_sizes(lengths, keep_flags):
    prompt_of = (jnp.arange(N_DP * ROLL_DEV) // GROUP).astype(jnp.int32).reshape(N_DP, ROLL_DEV)
    kept_flag = jnp.take(keep_flags, prompt_of, axis=1)
    return lengths * jnp.transpose(kept_flag, (1, 0, 2))

def attend_group(query_group, key_rows, value_rows, grad_group, allowed, empty_row, score_scale):
    query_wide = query_group.astype(jnp.float32)
    key_wide = key_rows.astype(jnp.float32)
    value_wide = value_rows.astype(jnp.float32)
    grad_wide = grad_group.astype(jnp.float32)
    scores = jnp.einsum('ugd,vd->guv', query_wide, key_wide) * score_scale
    raw_weights = jnp.where(allowed[None, :, :], jnp.exp(scores), 0.0)
    normed = raw_weights / (lax.optimization_barrier(jnp.sum(raw_weights, axis=-1, keepdims=True)) + empty_row[None, :, None])
    normed_low = normed.astype(jnp.bfloat16)
    output = jnp.einsum('guv,vd->ugd', normed_low.astype(jnp.float32), value_wide)
    grad_normed = jnp.einsum('ugd,vd->guv', grad_wide, value_wide)
    row_delta = lax.optimization_barrier(jnp.sum(normed * grad_normed, axis=-1, keepdims=True))
    grad_scores = (normed * (grad_normed - row_delta) * score_scale).astype(jnp.bfloat16)
    key_grad = jnp.einsum('guv,ugd->vd', grad_scores.astype(jnp.float32), query_wide)
    value_grad = jnp.einsum('guv,ugd->vd', normed_low.astype(jnp.float32), grad_wide)
    return (output.astype(jnp.bfloat16), key_grad, value_grad)

def reference(hidden, advantages, queries, upstream, ratios, key_weight, value_weight, lengths, keep_flags, destinations, offsets):
    kv_width = KVH * HD
    group_heads = HQ // KVH
    score_scale = 1.0 / math.sqrt(HD)
    kept_all = kept_sizes(lengths, keep_flags)
    token_count = jnp.sum(kept_all.astype(jnp.float32))
    both_weights = jnp.concatenate([key_weight, value_weight], axis=1)
    row_ids = jnp.arange(OUT_DEV).astype(jnp.int32)
    source_ids = jnp.arange(N_DP).astype(jnp.int32)
    slot_ids = jnp.arange(ROLL_DEV).astype(jnp.int32)

    def one_device(total, device):
        dest_dp = device // N_FSDP
        group = device % N_FSDP
        kept_group = jnp.take(kept_all, group, axis=1)
        dest_group = jnp.take(destinations, group, axis=1)
        offset_group = jnp.take(offsets, group, axis=1)
        incoming = (dest_group == dest_dp) & (kept_group > 0)
        in_offset = lax.optimization_barrier(jnp.sum(jnp.where(incoming, offset_group, 0), axis=1))
        in_length = lax.optimization_barrier(jnp.sum(jnp.where(incoming, kept_group, 0), axis=1))
        in_slot = lax.optimization_barrier(jnp.sum(jnp.where(incoming, slot_ids[None, :], 0), axis=1))
        relative = row_ids[:, None] - in_offset[None, :]
        inside = (relative >= 0) & (relative < in_length[None, :])
        filled = jnp.any(inside, axis=1)
        first_row = ((source_ids * N_FSDP + group) * ROLL_DEV + in_slot) * MAXLEN
        source_row = lax.optimization_barrier(jnp.sum(jnp.where(inside, first_row[None, :] + relative, 0), axis=1)).astype(jnp.int32)
        position = lax.optimization_barrier(jnp.sum(jnp.where(inside, relative, 0), axis=1))
        owner = lax.optimization_barrier(jnp.sum(jnp.where(inside, source_ids[None, :], 0), axis=1))
        placed = jnp.where(filled[:, None], jnp.take(hidden, source_row, axis=0), jnp.zeros((), jnp.bfloat16))
        placed_adv = jnp.where(filled, jnp.take(advantages, source_row), jnp.zeros((), jnp.bfloat16))
        projected = jnp.dot(placed, both_weights, preferred_element_type=jnp.float32)
        cosine, sine = rope_tables(position, HD)
        keys = rotate(projected[:, :kv_width].reshape(OUT_DEV, KVH, HD), cosine, sine).astype(jnp.bfloat16)
        values = projected[:, kv_width:].reshape(OUT_DEV, KVH, HD).astype(jnp.bfloat16)
        row_start = device * OUT_DEV
        query_rows = lax.dynamic_slice_in_dim(queries, row_start, OUT_DEV, 0).reshape(OUT_DEV, KVH, group_heads, HD)
        upstream_rows = lax.dynamic_slice_in_dim(upstream, row_start, OUT_DEV, 0)
        ratio_rows = lax.dynamic_slice_in_dim(ratios, row_start, OUT_DEV, 0)
        adv_wide = placed_adv.astype(jnp.float32)
        clipped = (adv_wide > 0) & (ratio_rows > clip_high) | (adv_wide < 0) & (ratio_rows < clip_low)
        coefficient = jnp.where(clipped, 0.0, -loss_scale * adv_wide * ratio_rows) / token_count
        out_grad = (coefficient[:, None] * upstream_rows.astype(jnp.float32)).astype(jnp.bfloat16)
        out_grad = out_grad.reshape(OUT_DEV, KVH, group_heads, HD)
        allowed = (owner[:, None] == owner[None, :]) & filled[:, None] & filled[None, :] & (row_ids[None, :] <= row_ids[:, None])
        empty_row = jnp.where(filled, 0.0, 1.0)
        outputs_all = []
        key_grads = []
        value_grads = []
        for head in range(KVH):
            output, key_grad, value_grad = attend_group(query_rows[:, head], keys[:, head], values[:, head], out_grad[:, head], allowed, empty_row, score_scale)
            outputs_all.append(output)
            key_grads.append(key_grad)
            value_grads.append(value_grad)
        attention_rows = jnp.stack(outputs_all, axis=1).reshape(OUT_DEV, HQ * HD)
        key_back = unrotate(jnp.stack(key_grads, axis=1), cosine, sine).reshape(OUT_DEV, kv_width)
        value_back = jnp.stack(value_grads, axis=1).reshape(OUT_DEV, kv_width)
        kv_grad = jnp.concatenate([key_back, value_back], axis=1).astype(jnp.bfloat16)
        partial_grad = jnp.dot(placed.T, kv_grad, preferred_element_type=jnp.float32)
        return (total + partial_grad, attention_rows)
    zero_grad = jnp.zeros((D, 2 * kv_width), jnp.float32)
    total, blocks = lax.scan(one_device, zero_grad, jnp.arange(N_DP * N_FSDP).astype(jnp.int32))
    attention = blocks.reshape(N_DP * N_FSDP * OUT_DEV, HQ * HD)
    return (attention, total[:, :kv_width], total[:, kv_width:])
```

```python
import math

import jax
import jax.numpy as jnp
import numpy as np
from jax import lax
from jax.experimental import pallas as pl
from jax.experimental.pallas import tpu as pltpu
from jax.sharding import Mesh
from jax.sharding import PartitionSpec as P

HD = 128
GROUP = 16
SLOT = 32

rope_base = 1000000.0
loss_scale = 256.0
clip_low = 0.8
clip_high = 1.28

DP = ("y", "z")
FSDP = ("x", "core")
ALL = DP + FSDP
BF = jnp.bfloat16
F32 = jnp.float32


def row_blocks(rows):
    step = HD - SLOT
    blocks = []
    for first in range(0, rows, step):
        size = min(step, rows - first)
        blocks.append((first, size, min(first, rows + SLOT - HD)))
    return blocks


def slot_tables():
    frequency = rope_base ** (-(np.arange(HD // 2) * (2.0 / HD)))
    angle = np.arange(SLOT)[:, None] * frequency[None, :]
    cosine, sine = np.cos(angle), np.sin(angle)
    return (
        np.concatenate([cosine, cosine], axis=1).astype(np.float32),
        np.concatenate([-sine, sine], axis=1).astype(np.float32),
    )


def row_tables(position):
    half = HD // 2
    frequency = rope_base ** (-(jnp.arange(half).astype(F32) * (2.0 / HD)))
    angle = position.astype(F32)[:, None] * frequency[None, :]
    cosine, sine = jnp.cos(angle), jnp.sin(angle)
    return (
        jnp.concatenate([cosine, cosine], axis=1),
        jnp.concatenate([-sine, sine], axis=1),
    )


def kept_sizes(lengths, keep_flags):
    dp_count, fsdp_count, slot_count = lengths.shape
    prompts = keep_flags.shape[1]
    prompt_of = (jnp.arange(dp_count * slot_count, dtype=jnp.int32) // GROUP).reshape(
        dp_count, 1, slot_count, 1
    )
    matches = prompt_of == jnp.arange(prompts, dtype=jnp.int32).reshape(1, 1, 1, prompts)
    kept_flag = jnp.sum(jnp.where(matches, keep_flags[None, :, None, :], 0), axis=-1)
    return lengths * kept_flag


def project_kernel(dest_ref, hidden_ref, weight_ref, cos_ref, sin_ref, out_ref, acc_ref):
    step = pl.program_id(0)
    part = jnp.dot(hidden_ref[...], weight_ref[...], preferred_element_type=F32)

    @pl.when(step == 0)
    def _():
        acc_ref[...] = part

    @pl.when(step > 0)
    def _():
        acc_ref[...] += part

    @pl.when(step == pl.num_programs(0) - 1)
    def _():
        kv_width = acc_ref.shape[1] // 2
        for slot in range(acc_ref.shape[0] // SLOT):
            rows = pl.ds(pl.multiple_of(dest_ref[slot] * SLOT, SLOT), SLOT)
            here = pl.ds(slot * SLOT, SLOT)
            for head in range(kv_width // HD):
                columns = pl.ds(head * HD, HD)
                key = acc_ref[here, columns]
                turned = key * cos_ref[...] + pltpu.roll(key, HD // 2, 1) * sin_ref[...]
                out_ref[rows, columns] = turned.astype(BF)
            values = pl.ds(kv_width, kv_width)
            out_ref[rows, values] = acc_ref[here, values].astype(BF)


def project(hidden, weights, dest_mine):
    rows, width = hidden.shape
    columns = weights.shape[1]
    depth = 512
    cosine, signed_sine = slot_tables()
    return pl.pallas_call(
        project_kernel,
        grid=(width // depth,),
        in_specs=[
            pl.BlockSpec(memory_space=pltpu.SMEM),
            pl.BlockSpec((rows, depth), lambda k: (0, k)),
            pl.BlockSpec((depth, columns), lambda k: (k, 0)),
            pl.BlockSpec((SLOT, HD), lambda k: (0, 0)),
            pl.BlockSpec((SLOT, HD), lambda k: (0, 0)),
        ],
        out_specs=pl.BlockSpec((rows, columns), lambda k: (0, 0)),
        out_shape=jax.ShapeDtypeStruct((rows, columns), BF),
        scratch_shapes=[pltpu.VMEM((rows, columns), F32)],
        compiler_params=pltpu.CompilerParams(vmem_limit_bytes=32 * 1024 * 1024),
        cost_estimate=pl.CostEstimate(
            flops=2 * rows * width * columns,
            bytes_accessed=2 * (rows * width + width * columns + rows * columns),
            transcendentals=0,
        ),
    )(dest_mine, hidden, weights, jnp.asarray(cosine), jnp.asarray(signed_sine))


def attend_kernel(
    place_ref,
    back_ref,
    keys_ref,
    values_ref,
    query_ref,
    upstream_ref,
    coef_ref,
    mask_ref,
    empty_ref,
    cos_ref,
    sin_ref,
    out_ref,
    kv_grad_ref,
    key_pad,
    value_pad,
    key_grad,
    value_grad,
):
    head = pl.program_id(0)
    rows = query_ref.shape[0]
    group = query_ref.shape[1] // HD
    kv_width = kv_grad_ref.shape[1] // 2
    scale = 1.0 / math.sqrt(HD)
    place = place_ref[...]
    lead = pl.ds(0, SLOT)
    body = pl.ds(SLOT, rows)
    key_pad[lead, :] = jnp.zeros((SLOT, HD), BF)
    value_pad[lead, :] = jnp.zeros((SLOT, HD), BF)
    key_pad[body, :] = jnp.dot(place, keys_ref[...], preferred_element_type=F32).astype(BF)
    value_pad[body, :] = jnp.dot(place, values_ref[...], preferred_element_type=F32).astype(BF)
    key_grad[...] = jnp.zeros_like(key_grad)
    value_grad[...] = jnp.zeros_like(value_grad)
    for first, size, window in row_blocks(rows):
        here = pl.ds(first, size)
        span = pl.ds(window, HD)
        coef = coef_ref[here, :]
        allowed = mask_ref[here, :] > 0.0
        empty = empty_ref[here, :]
        allowed = jnp.broadcast_to(allowed[None], (group, size, HD)).reshape(group * size, HD)
        empty = jnp.broadcast_to(empty[None], (group, size, 1)).reshape(group * size, 1)
        query = jnp.concatenate(
            [query_ref[here, pl.ds(g * HD, HD)] for g in range(group)], axis=0
        )
        grad = jnp.concatenate(
            [
                (coef * upstream_ref[here, pl.ds(g * HD, HD)].astype(F32)).astype(BF)
                for g in range(group)
            ],
            axis=0,
        )
        key = key_pad[span, :]
        value = value_pad[span, :]
        across = (((1,), (1,)), ((), ()))
        along = (((0,), (0,)), ((), ()))
        scores = lax.dot_general(query, key, across, preferred_element_type=F32) * scale
        raw = jnp.where(allowed, jnp.exp(scores), 0.0)
        normed = raw / (jnp.sum(raw, axis=-1, keepdims=True) + empty)
        normed_low = normed.astype(BF)
        output = jnp.dot(normed_low, value, preferred_element_type=F32).astype(BF)
        for g in range(group):
            out_ref[here, pl.ds(g * HD, HD)] = output[g * size : (g + 1) * size]
        grad_normed = lax.dot_general(grad, value, across, preferred_element_type=F32)
        delta = jnp.sum(normed * grad_normed, axis=-1, keepdims=True)
        grad_scores = (normed * (grad_normed - delta) * scale).astype(BF)
        key_grad[span, :] += lax.dot_general(
            grad_scores, query, along, preferred_element_type=F32
        )
        value_grad[span, :] += lax.dot_general(
            normed_low, grad, along, preferred_element_type=F32
        )
    turned = key_grad[body, :]
    key_back = turned * cos_ref[...] - pltpu.roll(turned, HD // 2, 1) * sin_ref[...]
    back = back_ref[...]
    key_columns = pl.ds(pl.multiple_of(head * HD, HD), HD)
    value_columns = pl.ds(pl.multiple_of(kv_width + head * HD, HD), HD)
    kv_grad_ref[:, key_columns] = jnp.dot(
        back, key_back.astype(BF), preferred_element_type=F32
    ).astype(BF)
    kv_grad_ref[:, value_columns] = jnp.dot(
        back, value_grad[body, :].astype(BF), preferred_element_type=F32
    ).astype(BF)


def attend(place, back, kv, queries, upstream, coefficient, mask, empty, cosine, signed_sine):
    rows, kv_columns = kv.shape
    heads = kv_columns // (2 * HD)
    width = queries.shape[1] // heads
    whole = lambda shape: pl.BlockSpec(shape, lambda h: (0, 0))
    return pl.pallas_call(
        attend_kernel,
        grid=(heads,),
        in_specs=[
            whole((rows, rows)),
            whole((rows, rows)),
            pl.BlockSpec((rows, HD), lambda h: (0, h)),
            pl.BlockSpec((rows, HD), lambda h: (0, heads + h)),
            pl.BlockSpec((rows, width), lambda h: (0, h)),
            pl.BlockSpec((rows, width), lambda h: (0, h)),
            whole((rows, 1)),
            whole((rows, HD)),
            whole((rows, 1)),
            whole((rows, HD)),
            whole((rows, HD)),
        ],
        out_specs=[
            pl.BlockSpec((rows, width), lambda h: (0, h)),
            whole((rows, kv_columns)),
        ],
        out_shape=[
            jax.ShapeDtypeStruct(queries.shape, BF),
            jax.ShapeDtypeStruct((rows, kv_columns), BF),
        ],
        scratch_shapes=[
            pltpu.VMEM((rows + SLOT, HD), BF),
            pltpu.VMEM((rows + SLOT, HD), BF),
            pltpu.VMEM((rows + SLOT, HD), F32),
            pltpu.VMEM((rows + SLOT, HD), F32),
        ],
        compiler_params=pltpu.CompilerParams(vmem_limit_bytes=40 * 1024 * 1024),
        cost_estimate=pl.CostEstimate(
            flops=10 * rows * queries.shape[1] * HD,
            bytes_accessed=2 * (3 * rows * queries.shape[1] + 2 * rows * kv_columns),
            transcendentals=rows * queries.shape[1],
        ),
    )(place, back, kv, kv, queries, upstream, coefficient, mask, empty, cosine, signed_sine)


def weight_grad_kernel(dest_ref, hidden_ref, grad_ref, out_ref, ordered):
    @pl.when(pl.program_id(0) == 0)
    def _():
        for slot in range(ordered.shape[0] // SLOT):
            rows = pl.ds(pl.multiple_of(dest_ref[slot] * SLOT, SLOT), SLOT)
            ordered[pl.ds(slot * SLOT, SLOT), :] = grad_ref[rows, :]

    out_ref[...] = lax.dot_general(
        hidden_ref[...], ordered[...], (((0,), (0,)), ((), ())), preferred_element_type=F32
    ).astype(BF)


def weight_grad(hidden, kv_grad, dest_mine):
    rows, width = hidden.shape
    columns = kv_grad.shape[1]
    piece = 640
    return pl.pallas_call(
        weight_grad_kernel,
        grid=(width // piece,),
        in_specs=[
            pl.BlockSpec(memory_space=pltpu.SMEM),
            pl.BlockSpec((rows, piece), lambda i: (0, i)),
            pl.BlockSpec((rows, columns), lambda i: (0, 0)),
        ],
        out_specs=pl.BlockSpec((piece, columns), lambda i: (i, 0)),
        out_shape=jax.ShapeDtypeStruct((width, columns), BF),
        scratch_shapes=[pltpu.VMEM((rows, columns), BF)],
        compiler_params=pltpu.CompilerParams(vmem_limit_bytes=32 * 1024 * 1024),
        cost_estimate=pl.CostEstimate(
            flops=2 * rows * width * columns,
            bytes_accessed=2 * (rows * width + width * columns + rows * columns),
            transcendentals=0,
        ),
    )(dest_mine, hidden, kv_grad)


def on_device(
    hidden,
    advantages,
    queries,
    upstream,
    ratios,
    key_weight,
    value_weight,
    lengths,
    keep_flags,
    destinations,
    offsets,
):
    dp_count, fsdp_count, slot_count = lengths.shape
    rows_here, model_width = hidden.shape
    kv_width = key_weight.shape[1]
    dp_index = lax.axis_index(DP)
    fsdp_index = lax.axis_index(FSDP)
    weights = lax.all_gather(
        jnp.concatenate([key_weight, value_weight], axis=1), FSDP, axis=0, tiled=True
    )
    kept_all = kept_sizes(lengths, keep_flags)
    token_count = jnp.sum(kept_all.astype(F32))
    kept_group = lax.dynamic_index_in_dim(kept_all, fsdp_index, 1, keepdims=False)
    dest_group = lax.dynamic_index_in_dim(destinations, fsdp_index, 1, keepdims=False)
    offset_group = lax.dynamic_index_in_dim(offsets, fsdp_index, 1, keepdims=False)
    dest_mine = lax.dynamic_index_in_dim(dest_group, dp_index, 0, keepdims=False)
    peer_ids = jnp.arange(dp_count, dtype=jnp.int32)
    slot_ids = jnp.arange(slot_count, dtype=jnp.int32)
    row_ids = jnp.arange(rows_here, dtype=jnp.int32)
    incoming = (dest_group == dp_index) & (kept_group > 0)
    in_offset = jnp.sum(jnp.where(incoming, offset_group, 0), axis=1)
    in_length = jnp.sum(jnp.where(incoming, kept_group, 0), axis=1)
    relative = row_ids[:, None] - in_offset[None, :]
    inside = (relative >= 0) & (relative < in_length[None, :])
    filled = jnp.any(inside, axis=1)
    recv_index = jnp.sum(jnp.where(inside, peer_ids[None, :] * SLOT + relative, 0), axis=1)
    position = jnp.sum(jnp.where(inside, relative, 0), axis=1)
    start = row_ids - position
    chosen = jnp.where(filled, recv_index, -1)
    place = (chosen[:, None] == row_ids[None, :]).astype(BF)
    back = (row_ids[:, None] == chosen[None, :]).astype(BF)
    cosine, signed_sine = row_tables(position)
    window = np.zeros((rows_here,), np.int32)
    for first, size, at in row_blocks(rows_here):
        window[first : first + size] = at - SLOT
    seen = jnp.asarray(window)[:, None] + jnp.arange(HD, dtype=jnp.int32)[None, :]
    mask = (
        filled[:, None] & (seen >= start[:, None]) & (seen <= row_ids[:, None])
    ).astype(F32)
    empty = jnp.where(filled, 0.0, 1.0).astype(F32)[:, None]

    order = dest_mine[None, :] == peer_ids[:, None]
    send_slots = jnp.sum(jnp.where(order, slot_ids[None, :], 0), axis=1)
    send_adv = jnp.take(advantages.reshape(slot_count, SLOT), send_slots, axis=0)
    got_adv = lax.all_to_all(send_adv, DP, split_axis=0, concat_axis=0, tiled=True)
    placed_adv = jnp.where(
        filled, jnp.take(got_adv.reshape(-1), recv_index), jnp.zeros((), BF)
    ).astype(F32)
    clipped = (placed_adv > 0) & (ratios > clip_high) | (placed_adv < 0) & (ratios < clip_low)
    coefficient = jnp.where(clipped, 0.0, -loss_scale * placed_adv * ratios) / token_count

    sent = project(hidden, weights, dest_mine)
    got = lax.all_to_all(
        sent.reshape(dp_count, SLOT, 2 * kv_width), DP, split_axis=0, concat_axis=0, tiled=True
    ).reshape(rows_here, 2 * kv_width)
    attention, kv_grad = attend(
        place, back, got, queries, upstream, coefficient[:, None], mask, empty, cosine, signed_sine
    )
    returned = lax.all_to_all(
        kv_grad.reshape(dp_count, SLOT, 2 * kv_width), DP, split_axis=0, concat_axis=0, tiled=True
    ).reshape(rows_here, 2 * kv_width)
    partial = weight_grad(hidden, returned, dest_mine)
    shares = lax.psum_scatter(partial, FSDP, scatter_dimension=0, tiled=True)
    share_rows = shares.shape[0]
    pieces = lax.all_to_all(
        shares.reshape(dp_count, share_rows // dp_count, 2 * kv_width),
        DP,
        split_axis=0,
        concat_axis=0,
        tiled=True,
    )
    total = jnp.sum(pieces.astype(F32), axis=0).astype(BF)
    spread = lax.all_to_all(
        jnp.broadcast_to(total[None], (dp_count,) + total.shape),
        DP,
        split_axis=0,
        concat_axis=0,
        tiled=True,
    )
    grad = spread.reshape(share_rows, 2 * kv_width).astype(F32)
    return (attention, grad[:, :kv_width], grad[:, kv_width:])


def solution(mesh):
    chips = {"y": 4, "z": 4, "x": 4, "core": 2}
    fine = Mesh(mesh.devices.reshape(tuple(chips.values())), tuple(chips))
    in_specs = (
        P(ALL, None),
        P(ALL),
        P(ALL, None),
        P(ALL, None),
        P(ALL),
        P(FSDP, None),
        P(FSDP, None),
        P(),
        P(),
        P(),
        P(),
    )
    out_specs = (P(ALL, None), P(FSDP, None), P(FSDP, None))
    return jax.shard_map(
        on_device, mesh=fine, in_specs=in_specs, out_specs=out_specs, check_vma=False
    )
```

```python
import math

import jax
import jax.numpy as jnp
import numpy as np
from jax import lax
from jax.experimental import pallas as pl
from jax.experimental.pallas import tpu as pltpu
from jax.sharding import Mesh
from jax.sharding import PartitionSpec as P

HD = 128
GROUP = 16
SLOT = 32
RING = 4
VMEM_LIMIT = 56 * 1024 * 1024

rope_base = 1000000.0
loss_scale = 256.0
clip_low = 0.8
clip_high = 1.28

DP = ("y", "z")
FSDP = ("x", "core")
ALL = DP + FSDP
BF = jnp.bfloat16
F32 = jnp.float32
LANES = 128


def row_blocks(rows):
    step = HD - SLOT
    blocks = []
    for first in range(0, rows, step):
        size = min(step, rows - first)
        blocks.append((first, size, min(first, rows + SLOT - HD)))
    return blocks


def slot_tables():
    frequency = rope_base ** (-(np.arange(HD // 2) * (2.0 / HD)))
    angle = np.arange(SLOT)[:, None] * frequency[None, :]
    cosine, sine = np.cos(angle), np.sin(angle)
    return (
        np.concatenate([cosine, cosine], axis=1).astype(np.float32),
        np.concatenate([-sine, sine], axis=1).astype(np.float32),
    )


def row_tables(position):
    half = HD // 2
    frequency = rope_base ** (-(jnp.arange(half).astype(F32) * (2.0 / HD)))
    angle = position.astype(F32)[:, None] * frequency[None, :]
    cosine, sine = jnp.cos(angle), jnp.sin(angle)
    return (
        jnp.concatenate([cosine, cosine], axis=1),
        jnp.concatenate([-sine, sine], axis=1),
    )


def kept_sizes(lengths, keep_flags):
    dp_count, fsdp_count, slot_count = lengths.shape
    prompts = keep_flags.shape[1]
    prompt_of = (jnp.arange(dp_count * slot_count, dtype=jnp.int32) // GROUP).reshape(
        dp_count, 1, slot_count, 1
    )
    matches = prompt_of == jnp.arange(prompts, dtype=jnp.int32).reshape(1, 1, 1, prompts)
    kept_flag = jnp.sum(jnp.where(matches, keep_flags[None, :, None, :], 0), axis=-1)
    return lengths * kept_flag


def params():
    return pltpu.CompilerParams(vmem_limit_bytes=VMEM_LIMIT)


def cost(flops, count):
    return pl.CostEstimate(flops=int(flops), bytes_accessed=int(2 * count), transcendentals=0)


def order_kernel(ids_ref, hidden_ref, adv_ref, mine_ref, theirs_ref):
    core = ids_ref[16]
    piece = theirs_ref.shape[1] // RING
    for block in range(RING):
        here = pl.ds(block * piece, piece)
        mine = pl.ds(pl.multiple_of((2 * block + core) * piece, LANES), piece)
        theirs = pl.ds(pl.multiple_of((2 * block + 1 - core) * piece, LANES), piece)
        mine_ref[:, here] = hidden_ref[:, mine]
        theirs_ref[:, here] = hidden_ref[:, theirs]
    mine_ref[:, pl.ds(RING * piece, LANES)] = adv_ref[...]


def order(ids, hidden, adv):
    rows, width = hidden.shape
    half = width // 2
    return pl.pallas_call(
        order_kernel,
        grid_spec=pltpu.PrefetchScalarGridSpec(
            num_scalar_prefetch=1,
            grid=(rows // SLOT,),
            in_specs=[
                pl.BlockSpec((SLOT, width), lambda s, ids: (s, 0)),
                pl.BlockSpec((SLOT, LANES), lambda s, ids: (s, 0)),
            ],
            out_specs=[
                pl.BlockSpec((SLOT, half + LANES), lambda s, ids: (ids[s], 0)),
                pl.BlockSpec((SLOT, half), lambda s, ids: (ids[s], 0)),
            ],
        ),
        out_shape=[
            jax.ShapeDtypeStruct((rows, half + LANES), BF),
            jax.ShapeDtypeStruct((rows, half), BF),
        ],
        compiler_params=params(),
        cost_estimate=cost(0, 2 * rows * width),
    )(ids, hidden, adv)


def project_kernel(
    ids_ref, theirs_ref, mine_ref, weight_ref, cos_ref, sin_ref, out_ref, acc_ref
):
    step = pl.program_id(0)

    @pl.when(step == 0)
    def _():
        acc_ref[...] = jnp.dot(theirs_ref[...], weight_ref[...], preferred_element_type=F32)

    @pl.when((step > 0) & (step < RING))
    def _():
        acc_ref[...] += jnp.dot(theirs_ref[...], weight_ref[...], preferred_element_type=F32)

    @pl.when(step >= RING)
    def _():
        acc_ref[...] += jnp.dot(mine_ref[...], weight_ref[...], preferred_element_type=F32)

    @pl.when(step == 2 * RING - 1)
    def _():
        kv_width = acc_ref.shape[1] // 2
        for slot in range(acc_ref.shape[0] // SLOT):
            here = pl.ds(slot * SLOT, SLOT)
            for head in range(kv_width // HD):
                columns = pl.ds(head * HD, HD)
                key = acc_ref[here, columns]
                turned = key * cos_ref[...] + pltpu.roll(key, HD // 2, 1) * sin_ref[...]
                out_ref[here, columns] = turned.astype(BF)
            values = pl.ds(kv_width, kv_width)
            out_ref[here, values] = acc_ref[here, values].astype(BF)


def project(ids, theirs, mine, weights):
    rows = theirs.shape[0]
    width, columns = weights.shape
    piece = width // (2 * RING)
    cosine, signed_sine = slot_tables()

    def weight_block(k, ids):
        core = ids[16]
        first = 2 * k + 1 - core
        second = 2 * (k - RING) + core
        return (jnp.where(k < RING, first, second), 0)

    return pl.pallas_call(
        project_kernel,
        grid_spec=pltpu.PrefetchScalarGridSpec(
            num_scalar_prefetch=1,
            grid=(2 * RING,),
            in_specs=[
                pl.BlockSpec((rows, piece), lambda k, ids: (0, jnp.minimum(k, RING - 1))),
                pl.BlockSpec((rows, piece), lambda k, ids: (0, jnp.maximum(k - RING, 0))),
                pl.BlockSpec((piece, columns), weight_block),
                pl.BlockSpec((SLOT, HD), lambda k, ids: (0, 0)),
                pl.BlockSpec((SLOT, HD), lambda k, ids: (0, 0)),
            ],
            out_specs=pl.BlockSpec((rows, columns), lambda k, ids: (0, 0)),
            scratch_shapes=[pltpu.VMEM((rows, columns), F32)],
        ),
        out_shape=jax.ShapeDtypeStruct((rows, columns), BF),
        compiler_params=params(),
        cost_estimate=cost(
            2 * rows * width * columns, rows * width + width * columns + rows * columns
        ),
    )(ids, theirs, mine, weights, jnp.asarray(cosine), jnp.asarray(signed_sine))


def attend_kernel(
    place_ref,
    back_ref,
    keys_ref,
    values_ref,
    query_ref,
    upstream_ref,
    adv_ref,
    ratio_ref,
    count_ref,
    mask_ref,
    empty_ref,
    cos_ref,
    sin_ref,
    out_ref,
    kv_grad_ref,
    key_pad,
    value_pad,
    key_grad,
    value_grad,
    coef_ref,
):
    head = pl.program_id(0)
    rows = query_ref.shape[0]
    group = query_ref.shape[1] // HD
    kv_width = kv_grad_ref.shape[1] // 2
    scale = 1.0 / math.sqrt(HD)
    place = place_ref[...]
    lead = pl.ds(0, SLOT)
    body = pl.ds(SLOT, rows)

    @pl.when(head == 0)
    def _():
        adv = jnp.dot(place, adv_ref[...], preferred_element_type=F32)
        ratio = ratio_ref[...]
        clipped = (adv > 0) & (ratio > clip_high) | (adv < 0) & (ratio < clip_low)
        coef_ref[...] = jnp.where(clipped, 0.0, -loss_scale * adv * ratio) / count_ref[0]

    key_pad[lead, :] = jnp.zeros((SLOT, HD), BF)
    value_pad[lead, :] = jnp.zeros((SLOT, HD), BF)
    key_pad[body, :] = jnp.dot(place, keys_ref[...], preferred_element_type=F32).astype(BF)
    value_pad[body, :] = jnp.dot(place, values_ref[...], preferred_element_type=F32).astype(BF)
    key_grad[...] = jnp.zeros_like(key_grad)
    value_grad[...] = jnp.zeros_like(value_grad)
    for first, size, window in row_blocks(rows):
        here = pl.ds(first, size)
        span = pl.ds(window, HD)
        coef = coef_ref[here, :]
        allowed = mask_ref[here, :] > 0.0
        empty = empty_ref[here, :]
        allowed = jnp.broadcast_to(allowed[None], (group, size, HD)).reshape(group * size, HD)
        empty = jnp.broadcast_to(empty[None], (group, size, 1)).reshape(group * size, 1)
        query = jnp.concatenate(
            [query_ref[here, pl.ds(g * HD, HD)] for g in range(group)], axis=0
        )
        grad = jnp.concatenate(
            [
                (coef * upstream_ref[here, pl.ds(g * HD, HD)].astype(F32)).astype(BF)
                for g in range(group)
            ],
            axis=0,
        )
        key = key_pad[span, :]
        value = value_pad[span, :]
        across = (((1,), (1,)), ((), ()))
        along = (((0,), (0,)), ((), ()))
        scores = lax.dot_general(query, key, across, preferred_element_type=F32) * scale
        raw = jnp.where(allowed, jnp.exp(scores), 0.0)
        normed = raw / (jnp.sum(raw, axis=-1, keepdims=True) + empty)
        normed_low = normed.astype(BF)
        output = jnp.dot(normed_low, value, preferred_element_type=F32).astype(BF)
        for g in range(group):
            out_ref[here, pl.ds(g * HD, HD)] = output[g * size : (g + 1) * size]
        grad_normed = lax.dot_general(grad, value, across, preferred_element_type=F32)
        delta = jnp.sum(normed * grad_normed, axis=-1, keepdims=True)
        grad_scores = (normed * (grad_normed - delta) * scale).astype(BF)
        key_grad[span, :] += lax.dot_general(
            grad_scores, query, along, preferred_element_type=F32
        )
        value_grad[span, :] += lax.dot_general(
            normed_low, grad, along, preferred_element_type=F32
        )
    turned = key_grad[body, :]
    key_back = turned * cos_ref[...] - pltpu.roll(turned, HD // 2, 1) * sin_ref[...]
    back = back_ref[...]
    key_columns = pl.ds(pl.multiple_of(head * HD, HD), HD)
    value_columns = pl.ds(pl.multiple_of(kv_width + head * HD, HD), HD)
    kv_grad_ref[:, key_columns] = jnp.dot(
        back, key_back.astype(BF), preferred_element_type=F32
    ).astype(BF)
    kv_grad_ref[:, value_columns] = jnp.dot(
        back, value_grad[body, :].astype(BF), preferred_element_type=F32
    ).astype(BF)


def attend(place, back, kv, queries, upstream, mine, ratios, count, mask, empty, cosine, sine):
    rows, kv_columns = kv.shape
    heads = kv_columns // (2 * HD)
    width = queries.shape[1] // heads
    adv_block = mine.shape[1] // LANES - 1
    whole = lambda shape: pl.BlockSpec(shape, lambda h: (0, 0))
    return pl.pallas_call(
        attend_kernel,
        grid=(heads,),
        in_specs=[
            whole((rows, rows)),
            whole((rows, rows)),
            pl.BlockSpec((rows, HD), lambda h: (0, h)),
            pl.BlockSpec((rows, HD), lambda h: (0, heads + h)),
            pl.BlockSpec((rows, width), lambda h: (0, h)),
            pl.BlockSpec((rows, width), lambda h: (0, h)),
            pl.BlockSpec((rows, LANES), lambda h: (0, adv_block)),
            whole((rows, 1)),
            pl.BlockSpec(memory_space=pltpu.SMEM),
            whole((rows, HD)),
            whole((rows, 1)),
            whole((rows, HD)),
            whole((rows, HD)),
        ],
        out_specs=[
            pl.BlockSpec((rows, width), lambda h: (0, h)),
            whole((rows, kv_columns)),
        ],
        out_shape=[
            jax.ShapeDtypeStruct(queries.shape, BF),
            jax.ShapeDtypeStruct((rows, kv_columns), BF),
        ],
        scratch_shapes=[
            pltpu.VMEM((rows + SLOT, HD), BF),
            pltpu.VMEM((rows + SLOT, HD), BF),
            pltpu.VMEM((rows + SLOT, HD), F32),
            pltpu.VMEM((rows + SLOT, HD), F32),
            pltpu.VMEM((rows, LANES), F32),
        ],
        compiler_params=params(),
        cost_estimate=cost(
            10 * rows * queries.shape[1] * HD, 3 * rows * queries.shape[1] + 2 * rows * kv_columns
        ),
    )(place, back, kv, kv, queries, upstream, mine, ratios, count, mask, empty, cosine, sine)


def pair_product(mine_ref, sibling_ref, own_ref, other_ref):
    along = (((0,), (0,)), ((), ()))
    return lax.dot_general(
        mine_ref[...], own_ref[...], along, preferred_element_type=F32
    ) + lax.dot_general(sibling_ref[...], other_ref[...], along, preferred_element_type=F32)


def grad_by_block_kernel(ids_ref, mine_ref, sibling_ref, own_ref, other_ref, *out_refs):
    product = pair_product(mine_ref, sibling_ref, own_ref, other_ref).astype(BF)
    for k in range(RING):

        @pl.when(pl.program_id(0) == k)
        def _(k=k):
            out_refs[k][...] = product


def grad_by_quarter_kernel(at, ids_ref, mine_ref, sibling_ref, own_ref, other_ref, *refs):
    out_refs, acc_ref = refs[:-1], refs[-1]
    acc_ref[...] = pair_product(mine_ref, sibling_ref, own_ref, other_ref)
    size = acc_ref.shape[0] // RING
    for k in range(RING):
        quarter = lax.rem(ids_ref[at] + k, RING)
        rows = pl.ds(pl.multiple_of(quarter * size, 8), size)
        out_refs[k][0] = acc_ref[rows, :].astype(BF)


def grad_part(ids, mine, sibling, own, other, at):
    rows, columns = own.shape
    piece = sibling.shape[1] // RING
    by_block = at == 17
    if by_block:
        block = lambda k, ids: (0, lax.rem(ids[17] + k, RING))
        kernel = grad_by_block_kernel
        out_spec = pl.BlockSpec((piece, columns), lambda k, ids: (0, 0))
        out_shape = jax.ShapeDtypeStruct((piece, columns), BF)
        scratch = []
    else:
        block = lambda k, ids: (0, k)
        kernel = lambda *refs: grad_by_quarter_kernel(at, *refs)
        size = piece // RING
        out_spec = pl.BlockSpec((1, size, columns), lambda k, ids: (k, 0, 0))
        out_shape = jax.ShapeDtypeStruct((RING, size, columns), BF)
        scratch = [pltpu.VMEM((piece, columns), F32)]
    return pl.pallas_call(
        kernel,
        grid_spec=pltpu.PrefetchScalarGridSpec(
            num_scalar_prefetch=1,
            grid=(RING,),
            in_specs=[
                pl.BlockSpec((rows, piece), block),
                pl.BlockSpec((rows, piece), block),
                pl.BlockSpec((rows, columns), lambda k, ids: (0, 0)),
                pl.BlockSpec((rows, columns), lambda k, ids: (0, 0)),
            ],
            out_specs=[out_spec] * RING,
            scratch_shapes=scratch,
        ),
        out_shape=[out_shape] * RING,
        compiler_params=params(),
        cost_estimate=cost(
            4 * rows * columns * RING * piece, RING * piece * (2 * rows + columns)
        ),
    )(ids, mine, sibling, own, other)


def total(parts):
    own, after, opposite, before = [part.astype(F32) for part in parts]
    return (own + opposite) + (after + before)


def sum_one_kernel(ids_ref, *refs):
    a, b, c = refs[0:4], refs[4:8], refs[8:12]
    a_out, bc_out = refs[12:16], refs[16:20]
    a_sum, b_sum, c_sum = refs[20:23]
    a_sum[...] = total([r[...] for r in a])
    b_sum[...] = total([r[...] for r in b])
    c_sum[...] = total([r[...] for r in c])
    size = a_out[0].shape[0]
    split = b_sum.shape[2]
    for k in range(RING):
        quarter = lax.rem(ids_ref[18] + k, RING)
        a_out[k][...] = a_sum[pl.ds(pl.multiple_of(quarter * size, 8), size), :].astype(BF)
        block = lax.rem(ids_ref[17] + k, RING)
        bc_out[k][:, pl.ds(0, split)] = b_sum[block].astype(BF)
        bc_out[k][:, pl.ds(split, c_sum.shape[2])] = c_sum[block].astype(BF)


def sum_one(ids, a, b, c):
    rows, a_width = a[0].shape
    b_width, c_width = b[0].shape[2], c[0].shape[2]
    size = rows // RING
    return pl.pallas_call(
        sum_one_kernel,
        in_specs=[pl.BlockSpec(memory_space=pltpu.SMEM)]
        + [pl.BlockSpec(memory_space=pltpu.VMEM)] * 12,
        out_specs=[pl.BlockSpec(memory_space=pltpu.VMEM)] * 8,
        out_shape=[jax.ShapeDtypeStruct((size, a_width), BF)] * RING
        + [jax.ShapeDtypeStruct((size, b_width + c_width), BF)] * RING,
        scratch_shapes=[
            pltpu.VMEM((rows, a_width), F32),
            pltpu.VMEM((RING, size, b_width), F32),
            pltpu.VMEM((RING, size, c_width), F32),
        ],
        compiler_params=params(),
        cost_estimate=cost(0, 5 * rows * (a_width + b_width + c_width)),
    )(ids, *a, *b, *c)


def sum_two_kernel(*refs):
    a, bc = refs[0:4], refs[4:8]
    ab_out, c_out = refs[8:10]
    a_width = a[0].shape[1]
    b_width = ab_out.shape[1] - a_width
    ab_out[:, pl.ds(0, a_width)] = total([r[...] for r in a]).astype(BF)
    both = total([r[...] for r in bc]).astype(BF)
    ab_out[:, pl.ds(a_width, b_width)] = both[:, :b_width]
    c_out[...] = both[:, b_width:]


def sum_two(a, bc, b_width):
    size, a_width = a[0].shape
    c_width = bc[0].shape[1] - b_width
    return pl.pallas_call(
        sum_two_kernel,
        in_specs=[pl.BlockSpec(memory_space=pltpu.VMEM)] * 8,
        out_specs=[pl.BlockSpec(memory_space=pltpu.VMEM)] * 2,
        out_shape=[
            jax.ShapeDtypeStruct((size, a_width + b_width), BF),
            jax.ShapeDtypeStruct((size, c_width), BF),
        ],
        compiler_params=params(),
        cost_estimate=cost(0, 5 * size * (a_width + b_width + c_width)),
    )(*a, *bc)


def sum_three_kernel(*refs):
    refs[8][...] = total([r[...] for r in refs[0:4]]).astype(BF)
    refs[9][...] = total([r[...] for r in refs[4:8]]).astype(BF)


def sum_three(ab, c):
    return pl.pallas_call(
        sum_three_kernel,
        in_specs=[pl.BlockSpec(memory_space=pltpu.VMEM)] * 8,
        out_specs=[pl.BlockSpec(memory_space=pltpu.VMEM)] * 2,
        out_shape=[
            jax.ShapeDtypeStruct(ab[0].shape, BF),
            jax.ShapeDtypeStruct(c[0].shape, BF),
        ],
        compiler_params=params(),
        cost_estimate=cost(0, 5 * (ab[0].size + c[0].size)),
    )(*ab, *c)


def assemble_kernel(ids_ref, *refs):
    ab, c, key_ref, value_ref = refs[0:4], refs[4:8], refs[8], refs[9]
    size, ab_width = ab[0].shape
    c_width = c[0].shape[1]
    kv_width = key_ref.shape[1]
    for k in range(RING):
        rows = pl.ds(pl.multiple_of(lax.rem(ids_ref[18] + RING - k, RING) * size, 8), size)
        key_ref[rows, :] = ab[k][:, pl.ds(0, kv_width)].astype(F32)
        value_ref[rows, pl.ds(0, ab_width - kv_width)] = ab[k][
            :, pl.ds(kv_width, ab_width - kv_width)
        ].astype(F32)
        rows = pl.ds(pl.multiple_of(lax.rem(ids_ref[19] + RING - k, RING) * size, 8), size)
        value_ref[rows, pl.ds(ab_width - kv_width, c_width)] = c[k][...].astype(F32)


def assemble(ids, ab, c):
    size, ab_width = ab[0].shape
    kv_width = (ab_width + c[0].shape[1]) // 2
    return pl.pallas_call(
        assemble_kernel,
        in_specs=[pl.BlockSpec(memory_space=pltpu.SMEM)]
        + [pl.BlockSpec(memory_space=pltpu.VMEM)] * 8,
        out_specs=[pl.BlockSpec(memory_space=pltpu.VMEM)] * 2,
        out_shape=[jax.ShapeDtypeStruct((RING * size, kv_width), F32)] * 2,
        compiler_params=params(),
        cost_estimate=cost(0, 3 * RING * size * 2 * kv_width),
    )(ids, *ab, *c)


def shifted(value, axis, k):
    return lax.ppermute(value, axis, [(i, (i + k) % RING) for i in range(RING)])


def exchange(parts, axis):
    far = shifted(parts[2], axis, 2)
    return [parts[0], shifted(parts[1], axis, 1), far, shifted(parts[3], axis, 3)]


def swap_cores(value):
    return lax.ppermute(value, "core", [(0, 1), (1, 0)])


def on_device(
    hidden,
    advantages,
    queries,
    upstream,
    ratios,
    key_weight,
    value_weight,
    lengths,
    keep_flags,
    destinations,
    offsets,
):
    dp_count, fsdp_count, slot_count = lengths.shape
    rows_here, model_width = hidden.shape
    kv_width = key_weight.shape[1]
    dp_index = lax.axis_index(DP)
    fsdp_index = lax.axis_index(FSDP)
    weights = lax.all_gather(
        jnp.concatenate([key_weight, value_weight], axis=1), FSDP, axis=0, tiled=True
    )
    dest_group = lax.dynamic_index_in_dim(destinations, fsdp_index, 1, keepdims=False)
    dest_mine = lax.dynamic_index_in_dim(dest_group, dp_index, 0, keepdims=False)
    places = [lax.axis_index(axis) for axis in ("core", "x", "y", "z")]
    ids = jnp.concatenate([dest_mine, jnp.stack(places)]).astype(jnp.int32)

    adv = jnp.broadcast_to(advantages[:, None], (rows_here, LANES))
    mine, theirs = order(ids, hidden, adv)

    def to_receivers(value):
        slots = value.reshape(dp_count, SLOT, value.shape[1])
        got = lax.all_to_all(slots, DP, split_axis=0, concat_axis=0, tiled=True)
        return got.reshape(value.shape)

    theirs = to_receivers(theirs)
    mine = to_receivers(mine)
    sibling = swap_cores(theirs)

    kept_all = kept_sizes(lengths, keep_flags)
    token_count = jnp.sum(kept_all.astype(F32))
    kept_group = lax.dynamic_index_in_dim(kept_all, fsdp_index, 1, keepdims=False)
    offset_group = lax.dynamic_index_in_dim(offsets, fsdp_index, 1, keepdims=False)
    peer_ids = jnp.arange(dp_count, dtype=jnp.int32)
    row_ids = jnp.arange(rows_here, dtype=jnp.int32)
    incoming = (dest_group == dp_index) & (kept_group > 0)
    in_offset = jnp.sum(jnp.where(incoming, offset_group, 0), axis=1)
    in_length = jnp.sum(jnp.where(incoming, kept_group, 0), axis=1)
    relative = row_ids[:, None] - in_offset[None, :]
    inside = (relative >= 0) & (relative < in_length[None, :])
    filled = jnp.any(inside, axis=1)
    recv_index = jnp.sum(jnp.where(inside, peer_ids[None, :] * SLOT + relative, 0), axis=1)
    position = jnp.sum(jnp.where(inside, relative, 0), axis=1)
    start = row_ids - position
    chosen = jnp.where(filled, recv_index, -1)
    place = (chosen[:, None] == row_ids[None, :]).astype(BF)
    back = (row_ids[:, None] == chosen[None, :]).astype(BF)
    cosine, signed_sine = row_tables(position)
    window = np.zeros((rows_here,), np.int32)
    for first, size, at in row_blocks(rows_here):
        window[first : first + size] = at - SLOT
    seen = jnp.asarray(window)[:, None] + jnp.arange(HD, dtype=jnp.int32)[None, :]
    mask = (
        filled[:, None] & (seen >= start[:, None]) & (seen <= row_ids[:, None])
    ).astype(F32)
    empty = jnp.where(filled, 0.0, 1.0).astype(F32)[:, None]

    kv = project(ids, theirs, mine, weights)
    attention, own = attend(
        place,
        back,
        kv,
        queries,
        upstream,
        mine,
        ratios[:, None],
        token_count[None],
        mask,
        empty,
        cosine,
        signed_sine,
    )
    other = swap_cores(own)
    cuts = (0, 3 * HD, 6 * HD, 2 * kv_width)

    def part(at, first, last):
        return grad_part(ids, mine, sibling, own[:, first:last], other[:, first:last], at)

    a = exchange(part(17, cuts[0], cuts[1]), "x")
    b = exchange(part(18, cuts[1], cuts[2]), "y")
    c = exchange(part(19, cuts[2], cuts[3]), "z")
    sums = sum_one(ids, a, b, c)
    a = exchange(sums[:RING], "y")
    bc = exchange(sums[RING:], "x")
    ab, c = sum_two(a, bc, cuts[2] - cuts[1])
    ab = exchange([ab] * RING, "z")
    c = exchange([c] * RING, "y")
    ab, c = sum_three(ab, c)
    ab = exchange([ab] * RING, "y")
    c = exchange([c] * RING, "z")
    grad_key, grad_value = assemble(ids, ab, c)
    return (attention, grad_key, grad_value)


def solution(mesh):
    chips = {"y": RING, "z": RING, "x": RING, "core": 2}
    fine = Mesh(mesh.devices.reshape(tuple(chips.values())), tuple(chips))
    in_specs = (
        P(ALL, None),
        P(ALL),
        P(ALL, None),
        P(ALL, None),
        P(ALL),
        P(FSDP, None),
        P(FSDP, None),
        P(),
        P(),
        P(),
        P(),
    )
    out_specs = (P(ALL, None), P(FSDP, None), P(FSDP, None))
    return jax.shard_map(
        on_device, mesh=fine, in_specs=in_specs, out_specs=out_specs, check_vma=False
    )
```

```python
import math

import jax
import jax.numpy as jnp
import numpy as np
from jax import lax
from jax.experimental import pallas as pl
from jax.experimental.pallas import tpu as pltpu
from jax.sharding import Mesh
from jax.sharding import PartitionSpec as P

HD = 128
SLOT = 32
RING = 4
SPLIT = 384
VMEM_LIMIT = 56 * 1024 * 1024

rope_base = 1000000.0
loss_scale = 256.0
clip_low = 0.8
clip_high = 1.28

DP = ("y", "z")
FSDP = ("x", "core")
ALL = DP + FSDP
BF = jnp.bfloat16
F32 = jnp.float32
LANES = 128
CORE, X, DP_AT, FSDP_AT = 16, 17, 18, 19


def row_blocks(rows):
    step = HD - SLOT
    blocks = []
    for first in range(0, rows, step):
        size = min(step, rows - first)
        blocks.append((first, size, min(first, rows + SLOT - HD)))
    return blocks


def slot_tables(rows=SLOT):
    frequency = rope_base ** (-(np.arange(HD // 2) * (2.0 / HD)))
    angle = np.arange(SLOT)[:, None] * frequency[None, :]
    cosine, sine = np.cos(angle), np.sin(angle)
    after = ((0, rows - SLOT), (0, 0))
    return (
        np.pad(np.concatenate([cosine, cosine], axis=1), after).astype(np.float32),
        np.pad(np.concatenate([-sine, sine], axis=1), after).astype(np.float32),
    )


def params():
    return pltpu.CompilerParams(vmem_limit_bytes=VMEM_LIMIT)


def cost(flops, count):
    return pl.CostEstimate(flops=int(flops), bytes_accessed=int(2 * count), transcendentals=0)


def order_kernel(ids_ref, hidden_ref, adv_ref, out_ref):
    step = pl.program_id(0)
    last = pl.num_programs(0) - 1
    for slot in range(hidden_ref.shape[0] // SLOT):
        here = pl.ds(slot * SLOT, SLOT)
        there = pl.ds(pl.multiple_of(ids_ref[slot] * SLOT, SLOT), SLOT)

        @pl.when(step < last)
        def _(here=here, there=there):
            out_ref[there, :] = hidden_ref[here, :]

        @pl.when(step == last)
        def _(here=here, there=there):
            out_ref[there, pl.ds(0, LANES)] = adv_ref[here, :]


def order(ids, hidden, adv):
    rows, width = hidden.shape
    pieces = 2 * RING
    piece = width // pieces

    def out_block(f, ids):
        mine = lax.rem(f, 2) == ids[CORE]
        block = jnp.where(mine, f // 2, RING + f // 2)
        return (0, jnp.where(f < pieces, block, pieces))

    return pl.pallas_call(
        order_kernel,
        grid_spec=pltpu.PrefetchScalarGridSpec(
            num_scalar_prefetch=1,
            grid=(pieces + 1,),
            in_specs=[
                pl.BlockSpec((rows, piece), lambda f, ids: (0, jnp.minimum(f, pieces - 1))),
                pl.BlockSpec((rows, LANES), lambda f, ids: (0, 0)),
            ],
            out_specs=pl.BlockSpec((rows, piece), out_block),
        ),
        out_shape=jax.ShapeDtypeStruct((rows, width + LANES), BF),
        compiler_params=params(),
        cost_estimate=cost(0, 2 * rows * width),
    )(ids, hidden, adv)


def project_kernel(ids_ref, rows_ref, weight_ref, cos_ref, sin_ref, out_ref, copy_ref, acc_ref):
    step = pl.program_id(0)
    last = pl.num_programs(0) - 1
    rows = rows_ref[...]
    weights = weight_ref[...].reshape(rows.shape[1], acc_ref.shape[1])
    part = jnp.dot(rows, weights, preferred_element_type=F32)

    @pl.when(step >= 2)
    def _():
        copy_ref[...] = rows

    @pl.when(step == 0)
    def _():
        acc_ref[...] = part

    @pl.when(step > 0)
    def _():
        acc_ref[...] += part

    @pl.when(step == last)
    def _():
        kv_width = acc_ref.shape[1] // 2
        for slot in range(acc_ref.shape[0] // SLOT):
            here = pl.ds(slot * SLOT, SLOT)
            for head in range(kv_width // HD):
                columns = pl.ds(head * HD, HD)
                key = acc_ref[here, columns]
                turned = key * cos_ref[...] + pltpu.roll(key, HD // 2, 1) * sin_ref[...]
                out_ref[here, columns] = turned.astype(BF)
            values = pl.ds(kv_width, kv_width)
            out_ref[here, values] = acc_ref[here, values].astype(BF)


def project(ids, got, weights):
    rows = got.shape[0]
    width, columns = weights.shape
    piece = width // (2 * RING)
    cosine, signed_sine = slot_tables()
    by_owner = weights.reshape(RING, 2, piece, columns)

    def weight_block(k, ids):
        core = jnp.where(k < 2, ids[CORE], 1 - ids[CORE])
        return (lax.rem(k, 2), core, 0, 0)

    return pl.pallas_call(
        project_kernel,
        grid_spec=pltpu.PrefetchScalarGridSpec(
            num_scalar_prefetch=1,
            grid=(RING,),
            in_specs=[
                pl.BlockSpec((rows, 2 * piece), lambda k, ids: (0, k)),
                pl.BlockSpec((2, 1, piece, columns), weight_block),
                pl.BlockSpec((SLOT, HD), lambda k, ids: (0, 0)),
                pl.BlockSpec((SLOT, HD), lambda k, ids: (0, 0)),
            ],
            out_specs=[
                pl.BlockSpec((rows, columns), lambda k, ids: (0, 0)),
                pl.BlockSpec((rows, 2 * piece), lambda k, ids: (0, jnp.maximum(k - 2, 0))),
            ],
            scratch_shapes=[pltpu.VMEM((rows, columns), F32)],
        ),
        out_shape=[
            jax.ShapeDtypeStruct((rows, columns), BF),
            jax.ShapeDtypeStruct((rows, width // 2), BF),
        ],
        compiler_params=params(),
        cost_estimate=cost(
            2 * rows * width * columns, rows * width + width * columns + rows * columns
        ),
    )(ids, got, by_owner, jnp.asarray(cosine), jnp.asarray(signed_sine))


def place_rows(ids_ref, lengths_ref, keep_ref, dest_ref, offsets_ref, place, back, mask, empty):
    rows = place.shape[0]
    dp_count, fsdp_count, slots = lengths_ref.shape
    group = ids_ref[FSDP_AT]

    def of_group(ref):
        picked = lax.broadcasted_iota(jnp.int32, (dp_count, fsdp_count, slots), 1) == group
        return jnp.sum(jnp.where(picked, ref[...], 0), axis=1)

    keep = keep_ref[...]
    same = lax.broadcasted_iota(jnp.int32, (dp_count, dp_count), 0) == lax.broadcasted_iota(
        jnp.int32, (dp_count, dp_count), 1
    )
    picked = lax.broadcasted_iota(jnp.int32, keep.shape, 0) == group
    keep_row = jnp.sum(jnp.where(picked, keep, 0), axis=0, keepdims=True)
    keep_column = jnp.sum(jnp.where(same, keep_row, 0), axis=1, keepdims=True)
    count = jnp.float32(0.0)
    for source in range(dp_count):
        kept = lengths_ref[source] * keep[:, source : source + 1]
        count += jnp.sum(kept.astype(F32))
    kept = of_group(lengths_ref) * keep_column
    incoming = (of_group(dest_ref) == ids_ref[DP_AT]) & (kept > 0)
    offset = jnp.sum(jnp.where(incoming, of_group(offsets_ref), 0), axis=1, keepdims=True)
    length = jnp.sum(jnp.where(incoming, kept, 0), axis=1, keepdims=True)

    offset_row = jnp.sum(jnp.where(same, offset, 0), axis=0, keepdims=True)
    length_row = jnp.sum(jnp.where(same, length, 0), axis=0, keepdims=True)
    source = lax.broadcasted_iota(jnp.int32, (rows, dp_count), 1)
    relative = lax.broadcasted_iota(jnp.int32, (rows, dp_count), 0) - offset_row
    inside = (relative >= 0) & (relative < length_row)
    filled = jnp.sum(jnp.where(inside, 1, 0), axis=1, keepdims=True) > 0
    position = jnp.sum(jnp.where(inside, relative, 0), axis=1, keepdims=True)
    origin = jnp.sum(jnp.where(inside, source * SLOT + relative, 0), axis=1, keepdims=True)
    origin = jnp.where(filled, origin, -1)
    wide = lax.broadcasted_iota(jnp.int32, (rows, rows), 1)
    place[...] = jnp.where(wide == origin, 1.0, 0.0).astype(BF)
    empty[...] = jnp.where(filled, 0.0, 1.0)

    slot_row = lax.broadcasted_iota(jnp.int32, (rows, dp_count), 0)
    owned = slot_row // SLOT == source
    token = slot_row - source * SLOT
    target = jnp.sum(
        jnp.where(owned & (token < length_row), offset_row + token + 1, 0), axis=1, keepdims=True
    )
    back[...] = jnp.where(wide == target - 1, 1.0, 0.0).astype(BF)

    row = lax.broadcasted_iota(jnp.int32, (rows, HD), 0)
    lane = lax.broadcasted_iota(jnp.int32, (rows, HD), 1)
    first = row - position
    window = jnp.zeros((rows, HD), jnp.int32)
    for start, size, at in row_blocks(rows):
        window = jnp.where(row >= start, at - SLOT, window)
    seen = window + lane
    mask[...] = jnp.where(filled & (seen >= first) & (seen <= row), 1.0, 0.0)
    return count, position


def attend_kernel(
    ids_ref,
    lengths_ref,
    keep_ref,
    dest_ref,
    offsets_ref,
    keys_ref,
    values_ref,
    query_ref,
    upstream_ref,
    adv_ref,
    ratio_ref,
    cos_table_ref,
    sin_table_ref,
    out_ref,
    kv_grad_ref,
    key_pad,
    value_pad,
    key_grad,
    value_grad,
    coef_ref,
    place_ref,
    back_ref,
    mask_ref,
    empty_ref,
    cos_ref,
    sin_ref,
):
    head = pl.program_id(0)
    rows = query_ref.shape[0]
    group = query_ref.shape[1] // HD
    kv_width = kv_grad_ref.shape[1] // 2
    scale = 1.0 / math.sqrt(HD)
    lead = pl.ds(0, SLOT)
    body = pl.ds(SLOT, rows)

    @pl.when(head == 0)
    def _():
        count, position = place_rows(
            ids_ref,
            lengths_ref,
            keep_ref,
            dest_ref,
            offsets_ref,
            place_ref,
            back_ref,
            mask_ref,
            empty_ref,
        )
        at = lax.broadcasted_iota(jnp.int32, (rows, HD), 1) == position
        at = jnp.where(at, 1.0, 0.0)
        exact = lax.Precision.HIGHEST
        cos_ref[...] = jnp.dot(
            at, cos_table_ref[...], preferred_element_type=F32, precision=exact
        )
        sin_ref[...] = jnp.dot(
            at, sin_table_ref[...], preferred_element_type=F32, precision=exact
        )
        adv = jnp.dot(place_ref[...], adv_ref[...], preferred_element_type=F32)
        ratio = ratio_ref[...]
        clipped = (adv > 0) & (ratio > clip_high) | (adv < 0) & (ratio < clip_low)
        coef_ref[...] = jnp.where(clipped, 0.0, -loss_scale * adv * ratio) / count

    place = place_ref[...]
    key_pad[lead, :] = jnp.zeros((SLOT, HD), BF)
    value_pad[lead, :] = jnp.zeros((SLOT, HD), BF)
    key_pad[body, :] = jnp.dot(place, keys_ref[...], preferred_element_type=F32).astype(BF)
    value_pad[body, :] = jnp.dot(place, values_ref[...], preferred_element_type=F32).astype(BF)
    key_grad[...] = jnp.zeros_like(key_grad)
    value_grad[...] = jnp.zeros_like(value_grad)
    for first, size, window in row_blocks(rows):
        here = pl.ds(first, size)
        span = pl.ds(window, HD)
        coef = coef_ref[here, :]
        allowed = mask_ref[here, :] > 0.0
        empty = empty_ref[here, :]
        allowed = jnp.broadcast_to(allowed[None], (group, size, HD)).reshape(group * size, HD)
        empty = jnp.broadcast_to(empty[None], (group, size, 1)).reshape(group * size, 1)
        query = jnp.concatenate(
            [query_ref[here, pl.ds(g * HD, HD)] for g in range(group)], axis=0
        )
        grad = jnp.concatenate(
            [
                (coef * upstream_ref[here, pl.ds(g * HD, HD)].astype(F32)).astype(BF)
                for g in range(group)
            ],
            axis=0,
        )
        key = key_pad[span, :]
        value = value_pad[span, :]
        across = (((1,), (1,)), ((), ()))
        along = (((0,), (0,)), ((), ()))
        scores = lax.dot_general(query, key, across, preferred_element_type=F32) * scale
        raw = jnp.where(allowed, jnp.exp(scores), 0.0)
        normed = raw / (jnp.sum(raw, axis=-1, keepdims=True) + empty)
        normed_low = normed.astype(BF)
        output = jnp.dot(normed_low, value, preferred_element_type=F32).astype(BF)
        for g in range(group):
            out_ref[here, pl.ds(g * HD, HD)] = output[g * size : (g + 1) * size]
        grad_normed = lax.dot_general(grad, value, across, preferred_element_type=F32)
        delta = jnp.sum(normed * grad_normed, axis=-1, keepdims=True)
        grad_scores = (normed * (grad_normed - delta) * scale).astype(BF)
        key_grad[span, :] += lax.dot_general(
            grad_scores, query, along, preferred_element_type=F32
        )
        value_grad[span, :] += lax.dot_general(
            normed_low, grad, along, preferred_element_type=F32
        )
    turned = key_grad[body, :]
    key_back = turned * cos_ref[...] - pltpu.roll(turned, HD // 2, 1) * sin_ref[...]
    back = back_ref[...]
    key_columns = pl.ds(pl.multiple_of(head * HD, HD), HD)
    value_columns = pl.ds(pl.multiple_of(kv_width + head * HD, HD), HD)
    kv_grad_ref[:, key_columns] = jnp.dot(
        back, key_back.astype(BF), preferred_element_type=F32
    ).astype(BF)
    kv_grad_ref[:, value_columns] = jnp.dot(
        back, value_grad[body, :].astype(BF), preferred_element_type=F32
    ).astype(BF)


def attend(ids, plan, kv, queries, upstream, got, ratios):
    rows, kv_columns = kv.shape
    heads = kv_columns // (2 * HD)
    width = queries.shape[1] // heads
    adv_block = got.shape[1] // LANES - 1
    tables = [jnp.asarray(table) for table in slot_tables(HD)]
    whole = lambda array: pl.BlockSpec(array.shape, lambda h: (0,) * array.ndim)
    return pl.pallas_call(
        attend_kernel,
        grid=(heads,),
        in_specs=[pl.BlockSpec(memory_space=pltpu.SMEM)]
        + [whole(array) for array in plan]
        + [
            pl.BlockSpec((rows, HD), lambda h: (0, h)),
            pl.BlockSpec((rows, HD), lambda h: (0, heads + h)),
            pl.BlockSpec((rows, width), lambda h: (0, h)),
            pl.BlockSpec((rows, width), lambda h: (0, h)),
            pl.BlockSpec((rows, LANES), lambda h: (0, adv_block)),
            whole(ratios),
            whole(tables[0]),
            whole(tables[1]),
        ],
        out_specs=[
            pl.BlockSpec((rows, width), lambda h: (0, h)),
            pl.BlockSpec((rows, kv_columns), lambda h: (0, 0)),
        ],
        out_shape=[
            jax.ShapeDtypeStruct(queries.shape, BF),
            jax.ShapeDtypeStruct((rows, kv_columns), BF),
        ],
        scratch_shapes=[
            pltpu.VMEM((rows + SLOT, HD), BF),
            pltpu.VMEM((rows + SLOT, HD), BF),
            pltpu.VMEM((rows + SLOT, HD), F32),
            pltpu.VMEM((rows + SLOT, HD), F32),
            pltpu.VMEM((rows, LANES), F32),
            pltpu.VMEM((rows, rows), BF),
            pltpu.VMEM((rows, rows), BF),
            pltpu.VMEM((rows, HD), F32),
            pltpu.VMEM((rows, 1), F32),
            pltpu.VMEM((rows, HD), F32),
            pltpu.VMEM((rows, HD), F32),
        ],
        compiler_params=params(),
        cost_estimate=cost(
            10 * rows * queries.shape[1] * HD, 3 * rows * queries.shape[1] + 2 * rows * kv_columns
        ),
    )(ids, *plan, kv, kv, queries, upstream, got, ratios, *tables)


def pair_product(columns, mine_ref, sibling_ref, own_ref, other_ref):
    along = (((0,), (0,)), ((), ()))
    return lax.dot_general(
        mine_ref[:, columns], own_ref[...], along, preferred_element_type=F32
    ) + lax.dot_general(
        sibling_ref[:, columns], other_ref[...], along, preferred_element_type=F32
    )


def grad_first_kernel(ids_ref, mine_ref, sibling_ref, own_ref, other_ref, *out_refs):
    columns = pl.ds(0, SPLIT)
    product = pair_product(columns, mine_ref, sibling_ref, own_ref, other_ref).astype(BF)
    for k in range(RING):

        @pl.when(pl.program_id(0) == k)
        def _(k=k):
            out_refs[k][...] = product


def grad_rest_kernel(ids_ref, mine_ref, sibling_ref, own_ref, other_ref, out_ref):
    columns = pl.ds(SPLIT, mine_ref.shape[1] - SPLIT)
    product = pair_product(columns, mine_ref, sibling_ref, own_ref, other_ref).astype(BF)
    size = out_ref.shape[2]
    for place in range(out_ref.shape[0]):
        out_ref[place, 0] = product[place * size : (place + 1) * size]


def grad_part(ids, got, sibling, own, other, places=0):
    rows, columns = own.shape
    piece = sibling.shape[1] // RING
    if places:
        block = lambda k, ids: (0, k)
        kernel = grad_rest_kernel
        count = piece - SPLIT
        size = count // places
        out_specs = pl.BlockSpec((places, 1, size, columns), lambda k, ids: (0, k, 0, 0))
        out_shape = jax.ShapeDtypeStruct((places, RING, size, columns), BF)
    else:
        block = lambda k, ids: (0, lax.rem(ids[X] + k, RING))
        kernel = grad_first_kernel
        count = SPLIT
        out_specs = [pl.BlockSpec((count, columns), lambda k, ids: (0, 0))] * RING
        out_shape = [jax.ShapeDtypeStruct((count, columns), BF)] * RING
    return pl.pallas_call(
        kernel,
        grid_spec=pltpu.PrefetchScalarGridSpec(
            num_scalar_prefetch=1,
            grid=(RING,),
            in_specs=[
                pl.BlockSpec((rows, piece), block),
                pl.BlockSpec((rows, piece), block),
                pl.BlockSpec((rows, columns), lambda k, ids: (0, 0)),
                pl.BlockSpec((rows, columns), lambda k, ids: (0, 0)),
            ],
            out_specs=out_specs,
        ),
        out_shape=out_shape,
        compiler_params=params(),
        cost_estimate=cost(
            4 * rows * columns * RING * count, RING * (2 * rows * piece + count * columns)
        ),
    )(ids, got, sibling, own, other)


def sum_places_kernel(ids_ref, parts_ref, *out_refs):
    for k in range(RING):
        block = lax.rem(ids_ref[X] + k, RING)
        terms = [parts_ref[place, block].astype(F32) for place in range(parts_ref.shape[0])]
        while len(terms) > 1:
            terms = [terms[i] + terms[i + 1] for i in range(0, len(terms), 2)]
        out_refs[k][...] = terms[0].astype(BF)


def sum_places(ids, parts):
    shape = jax.ShapeDtypeStruct(parts.shape[2:], BF)
    return pl.pallas_call(
        sum_places_kernel,
        in_specs=[
            pl.BlockSpec(memory_space=pltpu.SMEM),
            pl.BlockSpec(memory_space=pltpu.VMEM),
        ],
        out_specs=[pl.BlockSpec(memory_space=pltpu.VMEM)] * RING,
        out_shape=[shape] * RING,
        compiler_params=params(),
        cost_estimate=cost(0, parts.size),
    )(ids, parts)


def total(parts):
    own, after, opposite, before = [part.astype(F32) for part in parts]
    return (own + opposite) + (after + before)


def shifted(value, k):
    return lax.ppermute(value, "x", [(i, (i + k) % RING) for i in range(RING)])


def exchange(parts):
    far = shifted(parts[2], 2)
    return [parts[0], shifted(parts[1], 1), far, shifted(parts[3], 3)]


def swap_cores(value):
    return lax.ppermute(value, "core", [(0, 1), (1, 0)])


def over_dp(value):
    return lax.all_to_all(value, DP, split_axis=0, concat_axis=0, tiled=True)


def on_device(
    hidden,
    advantages,
    queries,
    upstream,
    ratios,
    key_weight,
    value_weight,
    lengths,
    keep_flags,
    destinations,
    offsets,
):
    dp_count = lengths.shape[0]
    rows_here, model_width = hidden.shape
    kv_width = key_weight.shape[1]
    dp_index = lax.axis_index(DP)
    fsdp_index = lax.axis_index(FSDP)
    weights = lax.all_gather(
        jnp.concatenate([key_weight, value_weight], axis=1), FSDP, axis=0, tiled=True
    )
    dest_group = lax.dynamic_index_in_dim(destinations, fsdp_index, 1, keepdims=False)
    dest_mine = lax.dynamic_index_in_dim(dest_group, dp_index, 0, keepdims=False)
    places = [lax.axis_index("core"), lax.axis_index("x"), dp_index, fsdp_index]
    ids = jnp.concatenate([dest_mine, jnp.stack(places)]).astype(jnp.int32)
    adv = jnp.broadcast_to(advantages[:, None], (rows_here, LANES))
    adv, ratios = lax.optimization_barrier((adv, ratios[:, None]))
    sent = order(ids, hidden, adv)
    got = over_dp(sent.reshape(dp_count, SLOT, sent.shape[1])).reshape(sent.shape)
    kv, theirs = project(ids, got, weights)
    sibling = swap_cores(theirs)
    plan = (lengths, keep_flags, destinations, offsets)
    attention, own = attend(ids, plan, kv, queries, upstream, got, ratios)
    other = swap_cores(own)

    first = exchange(grad_part(ids, got, sibling, own, other))
    rest = over_dp(grad_part(ids, got, sibling, own, other, dp_count))
    rest = exchange(sum_places(ids, rest))
    first = total(first).astype(BF)
    size = SPLIT // dp_count
    first = over_dp(first.reshape(dp_count, size, 2 * kv_width))
    summed = jnp.concatenate([jnp.sum(first.astype(F32), axis=0), total(rest)], axis=0)
    spread = over_dp(jnp.broadcast_to(summed.astype(BF)[None], (dp_count,) + summed.shape))
    grad = jnp.concatenate(
        [
            spread[:, :size].reshape(SPLIT, 2 * kv_width),
            spread[:, size:].reshape(-1, 2 * kv_width),
        ],
        axis=0,
    ).astype(F32)
    return (attention, grad[:, :kv_width], grad[:, kv_width:])


def solution(mesh):
    chips = {"y": RING, "z": RING, "x": RING, "core": 2}
    fine = Mesh(mesh.devices.reshape(tuple(chips.values())), tuple(chips))
    in_specs = (
        P(ALL, None),
        P(ALL),
        P(ALL, None),
        P(ALL, None),
        P(ALL),
        P(FSDP, None),
        P(FSDP, None),
        P(),
        P(),
        P(),
        P(),
    )
    out_specs = (P(ALL, None), P(FSDP, None), P(FSDP, None))
    return jax.shard_map(
        on_device, mesh=fine, in_specs=in_specs, out_specs=out_specs, check_vma=False
    )
```

```python
import math

import jax
import jax.numpy as jnp
import numpy as np
from jax import lax
from jax.experimental import pallas as pl
from jax.experimental.pallas import tpu as pltpu
from jax.sharding import Mesh
from jax.sharding import PartitionSpec as P

HD = 128
SLOT = 32
RING = 4
SPLIT = 512
VMEM_LIMIT = 56 * 1024 * 1024

rope_base = 1000000.0
loss_scale = 256.0
clip_low = 0.8
clip_high = 1.28

DP = ("y", "z")
FSDP = ("x", "core")
ALL = DP + FSDP
BF = jnp.bfloat16
F32 = jnp.float32
LANES = 128
CORE, X = 0, 1


def row_blocks(rows):
    step = HD - SLOT
    blocks = []
    for first in range(0, rows, step):
        size = min(step, rows - first)
        blocks.append((first, size, min(first, rows + SLOT - HD)))
    return blocks


def slot_tables(rows=SLOT):
    frequency = rope_base ** (-(np.arange(HD // 2) * (2.0 / HD)))
    angle = np.arange(SLOT)[:, None] * frequency[None, :]
    cosine, sine = np.cos(angle), np.sin(angle)
    after = ((0, rows - SLOT), (0, 0))
    return (
        np.pad(np.concatenate([cosine, cosine], axis=1), after).astype(np.float32),
        np.pad(np.concatenate([-sine, sine], axis=1), after).astype(np.float32),
    )


def params():
    return pltpu.CompilerParams(vmem_limit_bytes=VMEM_LIMIT)


def cost(flops, count):
    return pl.CostEstimate(flops=int(flops), bytes_accessed=int(2 * count), transcendentals=0)


def dp_fsdp():
    dp_index = lax.axis_index("y") * RING + lax.axis_index("z")
    return dp_index, lax.axis_index("x") * 2 + lax.axis_index("core")


def order_kernel(dest_ref, hidden_ref, adv_ref, key_ref, value_ref, sent_ref, weight_ref, sems):
    dp_index, group = dp_fsdp()
    width = hidden_ref.shape[1]
    kv_width = key_ref.shape[1]
    slots = hidden_ref.shape[0] // SLOT
    pairs = []
    for slot in range(slots):
        here = pl.ds(slot * SLOT, SLOT)
        there = pl.ds(pl.multiple_of(dest_ref[dp_index, group, slot] * SLOT, SLOT), SLOT)
        pairs.append((hidden_ref.at[here, :], sent_ref.at[there, pl.ds(0, width)]))
        pairs.append((adv_ref.at[here, :], sent_ref.at[there, pl.ds(width, LANES)]))
    pairs.append((key_ref, weight_ref.at[:, pl.ds(0, kv_width)]))
    pairs.append((value_ref, weight_ref.at[:, pl.ds(kv_width, kv_width)]))
    copies = [
        pltpu.make_async_copy(source, target, sems.at[i])
        for i, (source, target) in enumerate(pairs)
    ]
    for copy in copies:
        copy.start()
    for copy in copies:
        copy.wait()


def order(destinations, hidden, adv, key_weight, value_weight):
    rows, width = hidden.shape
    depth, kv_width = key_weight.shape
    anywhere = pl.BlockSpec(memory_space=pl.ANY)
    return pl.pallas_call(
        order_kernel,
        in_specs=[pl.BlockSpec(memory_space=pltpu.SMEM)] + [anywhere] * 4,
        out_specs=[anywhere] * 2,
        out_shape=[
            jax.ShapeDtypeStruct((rows, width + LANES), BF),
            jax.ShapeDtypeStruct((depth, 2 * kv_width), BF),
        ],
        scratch_shapes=[pltpu.SemaphoreType.DMA((2 * (rows // SLOT) + 2,))],
        compiler_params=params(),
        cost_estimate=cost(0, 2 * rows * width),
    )(destinations, hidden, adv, key_weight, value_weight)


def place_rows(lengths_ref, keep_ref, dest_ref, offsets_ref, place, mask, empty):
    rows = place.shape[0]
    dp_count, fsdp_count, slots = lengths_ref.shape
    dp_index, group = dp_fsdp()

    def of_group(ref):
        picked = lax.broadcasted_iota(jnp.int32, (dp_count, fsdp_count, slots), 1) == group
        return jnp.sum(jnp.where(picked, ref[...], 0), axis=1)

    keep = keep_ref[...]
    same = lax.broadcasted_iota(jnp.int32, (dp_count, dp_count), 0) == lax.broadcasted_iota(
        jnp.int32, (dp_count, dp_count), 1
    )
    picked = lax.broadcasted_iota(jnp.int32, keep.shape, 0) == group
    keep_row = jnp.sum(jnp.where(picked, keep, 0), axis=0, keepdims=True)
    keep_column = jnp.sum(jnp.where(same, keep_row, 0), axis=1, keepdims=True)
    count = jnp.float32(0.0)
    for source in range(dp_count):
        kept = lengths_ref[source] * keep[:, source : source + 1]
        count += jnp.sum(kept.astype(F32))
    kept = of_group(lengths_ref) * keep_column
    incoming = (of_group(dest_ref) == dp_index) & (kept > 0)
    offset = jnp.sum(jnp.where(incoming, of_group(offsets_ref), 0), axis=1, keepdims=True)
    length = jnp.sum(jnp.where(incoming, kept, 0), axis=1, keepdims=True)

    offset_row = jnp.sum(jnp.where(same, offset, 0), axis=0, keepdims=True)
    length_row = jnp.sum(jnp.where(same, length, 0), axis=0, keepdims=True)
    source = lax.broadcasted_iota(jnp.int32, (rows, dp_count), 1)
    relative = lax.broadcasted_iota(jnp.int32, (rows, dp_count), 0) - offset_row
    inside = (relative >= 0) & (relative < length_row)
    filled = jnp.sum(jnp.where(inside, 1, 0), axis=1, keepdims=True) > 0
    position = jnp.sum(jnp.where(inside, relative, 0), axis=1, keepdims=True)
    origin = jnp.sum(jnp.where(inside, source * SLOT + relative, 0), axis=1, keepdims=True)
    origin = jnp.where(filled, origin, -1)
    wide = lax.broadcasted_iota(jnp.int32, (rows, rows), 1)
    place[...] = jnp.where(wide == origin, 1.0, 0.0).astype(BF)
    empty[...] = jnp.where(filled, 0.0, 1.0)

    row = lax.broadcasted_iota(jnp.int32, (rows, HD), 0)
    lane = lax.broadcasted_iota(jnp.int32, (rows, HD), 1)
    first = row - position
    window = jnp.zeros((rows, HD), jnp.int32)
    for start, size, at in row_blocks(rows):
        window = jnp.where(row >= start, at - SLOT, window)
    seen = window + lane
    mask[...] = jnp.where(filled & (seen >= first) & (seen <= row), 1.0, 0.0)
    return count, position


def attend_kernel(
    lengths_ref,
    keep_ref,
    dest_ref,
    offsets_ref,
    rows_ref,
    weight_ref,
    query_ref,
    upstream_ref,
    adv_ref,
    ratio_ref,
    cos_table_ref,
    sin_table_ref,
    out_ref,
    kv_grad_ref,
    acc_ref,
    kv_ref,
    kv_pad,
    key_grad,
    value_grad,
    coef_ref,
    place_ref,
    mask_ref,
    empty_ref,
    cos_ref,
    sin_ref,
):
    step = pl.program_id(0)
    rows = query_ref.shape[0]
    kv_width = acc_ref.shape[1] // 2

    @pl.when(step < RING)
    def _():
        part = jnp.dot(rows_ref[...], weight_ref[...], preferred_element_type=F32)

        @pl.when(step == 0)
        def _():
            acc_ref[...] = part

        @pl.when(step > 0)
        def _():
            acc_ref[...] += part

    @pl.when(step == 0)
    def _():
        count, position = place_rows(
            lengths_ref, keep_ref, dest_ref, offsets_ref, place_ref, mask_ref, empty_ref
        )
        at = lax.broadcasted_iota(jnp.int32, (rows, HD), 1) == position
        at = jnp.where(at, 1.0, 0.0)
        exact = lax.Precision.HIGHEST
        cos_ref[...] = jnp.dot(
            at, cos_table_ref[...], preferred_element_type=F32, precision=exact
        )
        sin_ref[...] = jnp.dot(
            at, sin_table_ref[...], preferred_element_type=F32, precision=exact
        )
        adv = jnp.dot(place_ref[...], adv_ref[...], preferred_element_type=F32)
        same = lax.broadcasted_iota(jnp.int32, (LANES, LANES), 0) == lax.broadcasted_iota(
            jnp.int32, (LANES, LANES), 1
        )
        ratio = jnp.concatenate(
            [
                jnp.sum(jnp.where(same, ratio_ref[i : i + 1, :], 0.0), axis=1, keepdims=True)
                for i in range(rows // LANES)
            ],
            axis=0,
        )
        clipped = (adv > 0) & (ratio > clip_high) | (adv < 0) & (ratio < clip_low)
        coef_ref[...] = jnp.where(clipped, 0.0, -loss_scale * adv * ratio) / count

    @pl.when(step == RING - 1)
    def _():
        for slot in range(rows // SLOT):
            here = pl.ds(slot * SLOT, SLOT)
            cosine = cos_table_ref[pl.ds(0, SLOT), :]
            sine = sin_table_ref[pl.ds(0, SLOT), :]
            for head in range(kv_width // HD):
                columns = pl.ds(head * HD, HD)
                key = acc_ref[here, columns]
                turned = key * cosine + pltpu.roll(key, HD // 2, 1) * sine
                kv_ref[here, columns] = turned.astype(BF)
            values = pl.ds(kv_width, kv_width)
            kv_ref[here, values] = acc_ref[here, values].astype(BF)
        kv_pad[pl.ds(0, SLOT), :] = jnp.zeros((SLOT, 2 * kv_width), BF)
        kv_pad[pl.ds(SLOT, rows), :] = jnp.dot(
            place_ref[...], kv_ref[...], preferred_element_type=F32
        ).astype(BF)

    @pl.when(step >= RING)
    def _():
        attend_head(
            step - RING,
            query_ref,
            upstream_ref,
            out_ref,
            kv_grad_ref,
            kv_pad,
            key_grad,
            value_grad,
            coef_ref,
            place_ref,
            mask_ref,
            empty_ref,
            cos_ref,
            sin_ref,
        )


def attend_head(
    head,
    query_ref,
    upstream_ref,
    out_ref,
    kv_grad_ref,
    kv_pad,
    key_grad,
    value_grad,
    coef_ref,
    place_ref,
    mask_ref,
    empty_ref,
    cos_ref,
    sin_ref,
):
    rows = query_ref.shape[0]
    group = query_ref.shape[1] // HD
    kv_width = kv_pad.shape[1] // 2
    scale = 1.0 / math.sqrt(HD)
    body = pl.ds(SLOT, rows)
    key_columns = pl.ds(pl.multiple_of(head * HD, HD), HD)
    value_columns = pl.ds(pl.multiple_of(kv_width + head * HD, HD), HD)
    across = (((1,), (1,)), ((), ()))
    along = (((0,), (0,)), ((), ()))
    key_grad[...] = jnp.zeros_like(key_grad)
    value_grad[...] = jnp.zeros_like(value_grad)
    for first, size, window in row_blocks(rows):
        here = pl.ds(first, size)
        span = pl.ds(window, HD)
        coef = coef_ref[here, :]
        allowed = mask_ref[here, :] > 0.0
        empty = empty_ref[here, :]
        allowed = jnp.broadcast_to(allowed[None], (group, size, HD)).reshape(group * size, HD)
        empty = jnp.broadcast_to(empty[None], (group, size, 1)).reshape(group * size, 1)
        query = jnp.concatenate(
            [query_ref[here, pl.ds(g * HD, HD)] for g in range(group)], axis=0
        )
        grad = jnp.concatenate(
            [
                (coef * upstream_ref[here, pl.ds(g * HD, HD)].astype(F32)).astype(BF)
                for g in range(group)
            ],
            axis=0,
        )
        key = kv_pad[span, key_columns]
        value = kv_pad[span, value_columns]
        scores = lax.dot_general(query, key, across, preferred_element_type=F32) * scale
        raw = jnp.where(allowed, jnp.exp(scores), 0.0)
        normed = raw * (1.0 / (jnp.sum(raw, axis=-1, keepdims=True) + empty))
        normed_low = normed.astype(BF)
        output = jnp.dot(normed_low, value, preferred_element_type=F32).astype(BF)
        for g in range(group):
            out_ref[here, pl.ds(g * HD, HD)] = output[g * size : (g + 1) * size]
        grad_normed = lax.dot_general(grad, value, across, preferred_element_type=F32)
        delta = jnp.sum(normed * grad_normed, axis=-1, keepdims=True)
        grad_scores = (normed * (grad_normed - delta) * scale).astype(BF)
        key_grad[span, :] += lax.dot_general(
            grad_scores, query, along, preferred_element_type=F32
        )
        value_grad[span, :] += lax.dot_general(
            normed_low, grad, along, preferred_element_type=F32
        )
    turned = key_grad[body, :]
    key_back = turned * cos_ref[...] - pltpu.roll(turned, HD // 2, 1) * sin_ref[...]
    both = jnp.concatenate([key_back.astype(BF), value_grad[body, :].astype(BF)], axis=1)
    kv_grad_ref[...] = lax.dot_general(
        both, place_ref[...], along, preferred_element_type=F32
    ).astype(BF)


def attend(plan, got, weights, queries, upstream, ratios):
    rows = got.shape[0]
    width, kv_columns = weights.shape
    heads = kv_columns // (2 * HD)
    query_width = queries.shape[1] // heads
    adv_block = got.shape[1] // LANES - 1
    depth = width // RING
    tables = [jnp.asarray(table) for table in slot_tables(HD)]
    whole = lambda array: pl.BlockSpec(array.shape, lambda k: (0,) * array.ndim)
    early = lambda k: jnp.minimum(k, RING - 1)
    late = lambda k: jnp.maximum(k - RING, 0)
    return pl.pallas_call(
        attend_kernel,
        grid=(RING + heads,),
        in_specs=[whole(array) for array in plan]
        + [
            pl.BlockSpec((rows, depth), lambda k: (0, early(k))),
            pl.BlockSpec((depth, kv_columns), lambda k: (early(k), 0)),
            pl.BlockSpec((rows, query_width), lambda k: (0, late(k))),
            pl.BlockSpec((rows, query_width), lambda k: (0, late(k))),
            pl.BlockSpec((rows, LANES), lambda k: (0, adv_block)),
            whole(ratios),
            whole(tables[0]),
            whole(tables[1]),
        ],
        out_specs=[
            pl.BlockSpec((rows, query_width), lambda k: (0, late(k))),
            pl.BlockSpec((2 * HD, rows), lambda k: (late(k), 0)),
        ],
        out_shape=[
            jax.ShapeDtypeStruct(queries.shape, BF),
            jax.ShapeDtypeStruct((kv_columns, rows), BF),
        ],
        scratch_shapes=[
            pltpu.VMEM((rows, kv_columns), F32),
            pltpu.VMEM((rows, kv_columns), BF),
            pltpu.VMEM((rows + SLOT, kv_columns), BF),
            pltpu.VMEM((rows + SLOT, HD), F32),
            pltpu.VMEM((rows + SLOT, HD), F32),
            pltpu.VMEM((rows, LANES), F32),
            pltpu.VMEM((rows, rows), BF),
            pltpu.VMEM((rows, HD), F32),
            pltpu.VMEM((rows, 1), F32),
            pltpu.VMEM((rows, HD), F32),
            pltpu.VMEM((rows, HD), F32),
        ],
        compiler_params=params(),
        cost_estimate=cost(
            2 * rows * width * kv_columns + 10 * rows * queries.shape[1] * HD,
            rows * width + width * kv_columns + 3 * rows * queries.shape[1],
        ),
    )(*plan, got, weights, queries, upstream, got, ratios, *tables)


def pair_product(own_ref, other_ref, mine_ref, sibling_ref):
    return jnp.dot(own_ref[...], mine_ref[...], preferred_element_type=F32) + jnp.dot(
        other_ref[...], sibling_ref[...], preferred_element_type=F32
    )


def grad_first_kernel(ids_ref, own_ref, other_ref, mine_ref, sibling_ref, *out_refs):
    product = pair_product(own_ref, other_ref, mine_ref, sibling_ref).astype(BF)
    for k in range(RING):

        @pl.when(pl.program_id(0) == k)
        def _(k=k):
            out_refs[k][...] = product


def grad_rest_kernel(ids_ref, own_ref, other_ref, mine_ref, sibling_ref, out_ref):
    product = pair_product(own_ref, other_ref, mine_ref, sibling_ref).astype(BF)
    size = out_ref.shape[2]
    for place in range(out_ref.shape[0]):
        out_ref[place, 0] = product[place * size : (place + 1) * size]


def grad_part(ids, own, other, got, sibling, width, places=0):
    columns, rows = own.shape
    piece = width // (2 * RING)
    if places:
        block = lambda k, ids: (0, 2 * k + ids[CORE])
        kernel = grad_rest_kernel
        count = columns - SPLIT
        size = count // places
        out_specs = pl.BlockSpec((places, 1, size, piece), lambda k, ids: (0, k, 0, 0))
        out_shape = jax.ShapeDtypeStruct((places, RING, size, piece), BF)
        kv_block = lambda k, ids: (1, 0)
    else:
        block = lambda k, ids: (0, 2 * lax.rem(ids[X] + k, RING) + ids[CORE])
        kernel = grad_first_kernel
        count = SPLIT
        out_specs = [pl.BlockSpec((count, piece), lambda k, ids: (0, 0))] * RING
        out_shape = [jax.ShapeDtypeStruct((count, piece), BF)] * RING
        kv_block = lambda k, ids: (0, 0)
    return pl.pallas_call(
        kernel,
        grid_spec=pltpu.PrefetchScalarGridSpec(
            num_scalar_prefetch=1,
            grid=(RING,),
            in_specs=[
                pl.BlockSpec((count, rows), kv_block),
                pl.BlockSpec((count, rows), kv_block),
                pl.BlockSpec((rows, piece), block),
                pl.BlockSpec((rows, piece), block),
            ],
            out_specs=out_specs,
        ),
        out_shape=out_shape,
        compiler_params=params(),
        cost_estimate=cost(
            4 * rows * count * RING * piece, RING * (2 * rows * piece + count * piece)
        ),
    )(ids, own, other, got, sibling)


def sum_places_kernel(ids_ref, parts_ref, *out_refs):
    for k in range(RING):
        block = lax.rem(ids_ref[X] + k, RING)
        terms = [parts_ref[place, block].astype(F32) for place in range(parts_ref.shape[0])]
        while len(terms) > 1:
            terms = [terms[i] + terms[i + 1] for i in range(0, len(terms), 2)]
        out_refs[k][...] = terms[0].astype(BF)


def sum_places(ids, parts):
    shape = jax.ShapeDtypeStruct(parts.shape[2:], BF)
    return pl.pallas_call(
        sum_places_kernel,
        in_specs=[
            pl.BlockSpec(memory_space=pltpu.SMEM),
            pl.BlockSpec(memory_space=pltpu.VMEM),
        ],
        out_specs=[pl.BlockSpec(memory_space=pltpu.VMEM)] * RING,
        out_shape=[shape] * RING,
        compiler_params=params(),
        cost_estimate=cost(0, parts.size),
    )(ids, parts)


def finish_kernel(spread_ref, key_ref, value_ref):
    places, both, _ = spread_ref.shape
    size = both // 2
    per_head = HD // size
    for part in range(2):
        for i in range(places // per_head):
            rows = [
                spread_ref[i * per_head + j, pl.ds(part * size, size), :].astype(F32)
                for j in range(per_head)
            ]
            block = jnp.concatenate(rows, axis=0).T
            head = (part * places // per_head + i) // 2
            out_ref = value_ref if i % 2 else key_ref
            out_ref[:, pl.ds(head * HD, HD)] = block


def finish(spread, kv_width):
    columns = spread.shape[2]
    return pl.pallas_call(
        finish_kernel,
        out_shape=[jax.ShapeDtypeStruct((columns, kv_width), F32)] * 2,
        compiler_params=params(),
        cost_estimate=cost(0, 3 * spread.size),
    )(spread)


def total(parts):
    own, after, opposite, before = [part.astype(F32) for part in parts]
    return (own + opposite) + (after + before)


def shifted(value, k):
    return lax.ppermute(value, "x", [(i, (i + k) % RING) for i in range(RING)])


def exchange(parts):
    far = shifted(parts[2], 2)
    return [parts[0], shifted(parts[1], 1), far, shifted(parts[3], 3)]


def swap_cores(value):
    return lax.ppermute(value, "core", [(0, 1), (1, 0)])


def over_dp(value):
    return lax.all_to_all(value, DP, split_axis=0, concat_axis=0, tiled=True)


def on_device(
    hidden,
    advantages,
    queries,
    upstream,
    ratios,
    key_weight,
    value_weight,
    lengths,
    keep_flags,
    destinations,
    offsets,
):
    dp_count = lengths.shape[0]
    rows_here, model_width = hidden.shape
    kv_width = key_weight.shape[1]
    ids = jnp.stack([lax.axis_index("core"), lax.axis_index("x")]).astype(jnp.int32)
    adv = jnp.broadcast_to(advantages[:, None], (rows_here, LANES))
    sent, weights = order(destinations, hidden, adv, key_weight, value_weight)
    weights = lax.all_gather(weights, FSDP, axis=0, tiled=True)
    got = over_dp(sent.reshape(dp_count, SLOT, sent.shape[1])).reshape(sent.shape)
    sibling = swap_cores(got)
    plan = (lengths, keep_flags, destinations, offsets)
    ratios = ratios.reshape(rows_here // LANES, LANES)
    attention, own = attend(plan, got, weights, queries, upstream, ratios)
    other = swap_cores(own)

    rest = over_dp(grad_part(ids, own, other, got, sibling, model_width, dp_count))
    first = exchange(grad_part(ids, own, other, got, sibling, model_width))
    rest = exchange(sum_places(ids, rest))
    first = total(first).astype(BF)
    first = over_dp(first.reshape(dp_count, SPLIT // dp_count, first.shape[1]))
    summed = jnp.concatenate([jnp.sum(first.astype(F32), axis=0), total(rest)], axis=0)
    spread = over_dp(jnp.broadcast_to(summed.astype(BF)[None], (dp_count,) + summed.shape))
    grad_key, grad_value = finish(spread, kv_width)
    return (attention, grad_key, grad_value)


def solution(mesh):
    chips = {"y": RING, "z": RING, "x": RING, "core": 2}
    fine = Mesh(mesh.devices.reshape(tuple(chips.values())), tuple(chips))
    in_specs = (
        P(ALL, None),
        P(ALL),
        P(ALL, None),
        P(ALL, None),
        P(ALL),
        P(FSDP, None),
        P(FSDP, None),
        P(),
        P(),
        P(),
        P(),
    )
    out_specs = (P(ALL, None), P(FSDP, None), P(FSDP, None))
    return jax.shard_map(
        on_device, mesh=fine, in_specs=in_specs, out_specs=out_specs, check_vma=False
    )
```

```python
import math

import jax
import jax.numpy as jnp
import numpy as np
from jax import lax
from jax.experimental import pallas as pl
from jax.experimental.pallas import tpu as pltpu
from jax.sharding import Mesh
from jax.sharding import PartitionSpec as P

HD = 128
SLOT = 32
RING = 4
SPLIT = 512
VMEM_LIMIT = 56 * 1024 * 1024

rope_base = 1000000.0
loss_scale = 256.0
clip_low = 0.8
clip_high = 1.28

DP = ("y", "z")
FSDP = ("x", "core")
ALL = DP + FSDP
BF = jnp.bfloat16
F32 = jnp.float32
LANES = 128


def row_blocks(rows):
    step = HD - SLOT
    blocks = []
    for first in range(0, rows, step):
        size = min(step, rows - first)
        blocks.append((first, size, min(first, rows + SLOT - HD)))
    return blocks


def slot_tables(rows=SLOT):
    frequency = rope_base ** (-(np.arange(HD // 2) * (2.0 / HD)))
    angle = np.arange(SLOT)[:, None] * frequency[None, :]
    cosine, sine = np.cos(angle), np.sin(angle)
    after = ((0, rows - SLOT), (0, 0))
    return (
        np.pad(np.concatenate([cosine, cosine], axis=1), after).astype(np.float32),
        np.pad(np.concatenate([-sine, sine], axis=1), after).astype(np.float32),
    )


def params():
    return pltpu.CompilerParams(vmem_limit_bytes=VMEM_LIMIT)


def cost(flops, count):
    return pl.CostEstimate(flops=int(flops), bytes_accessed=int(2 * count), transcendentals=0)


def dp_fsdp():
    dp_index = lax.axis_index("y") * RING + lax.axis_index("z")
    return dp_index, lax.axis_index("x") * 2 + lax.axis_index("core")


def column_of(row_ref):
    same = lax.broadcasted_iota(jnp.int32, (LANES, LANES), 0) == lax.broadcasted_iota(
        jnp.int32, (LANES, LANES), 1
    )
    parts = []
    for i in range(row_ref.shape[0]):
        row = row_ref[i : i + 1, :].astype(F32)
        parts.append(jnp.sum(jnp.where(same, row, 0.0), axis=1, keepdims=True))
    return jnp.concatenate(parts, axis=0)


def order_kernel(
    dest_ref,
    hidden_ref,
    adv_ref,
    key_ref,
    value_ref,
    sent_ref,
    weight_ref,
    rows_buf,
    adv_buf,
    weight_buf,
    in_sems,
    out_sems,
    adv_sems,
    weight_sems,
):
    dp_index, group = dp_fsdp()
    width = hidden_ref.shape[1]
    kv_width = key_ref.shape[1]
    slots = hidden_ref.shape[0] // SLOT
    both = [
        pltpu.make_async_copy(
            ref, weight_buf.at[:, pl.ds(i * kv_width, kv_width)], weight_sems.at[i]
        )
        for i, ref in enumerate((key_ref, value_ref))
    ]
    arrive, leave, adv_leave = [], [], []
    for slot in range(slots):
        here = pl.ds(slot * SLOT, SLOT)
        there = pl.ds(pl.multiple_of(dest_ref[dp_index, group, slot] * SLOT, SLOT), SLOT)
        arrive.append(
            pltpu.make_async_copy(hidden_ref.at[here, :], rows_buf.at[slot], in_sems.at[slot])
        )
        leave.append(
            pltpu.make_async_copy(
                rows_buf.at[slot], sent_ref.at[there, pl.ds(0, width)], out_sems.at[slot]
            )
        )
        adv_leave.append(
            pltpu.make_async_copy(
                adv_buf.at[here, :], sent_ref.at[there, pl.ds(width, LANES)], adv_sems.at[slot]
            )
        )
    for copy in both + arrive:
        copy.start()
    adv_buf[...] = jnp.broadcast_to(column_of(adv_ref), adv_buf.shape).astype(BF)
    for copy in adv_leave:
        copy.start()
    for copy in both:
        copy.wait()
    out = pltpu.make_async_copy(weight_buf, weight_ref, weight_sems.at[2])
    out.start()
    for slot in range(slots):
        arrive[slot].wait()
        leave[slot].start()
    out.wait()
    for copy in adv_leave + leave:
        copy.wait()


def order(destinations, hidden, adv, key_weight, value_weight):
    rows, width = hidden.shape
    depth, kv_width = key_weight.shape
    slots = rows // SLOT
    anywhere = pl.BlockSpec(memory_space=pl.ANY)
    return pl.pallas_call(
        order_kernel,
        in_specs=[
            pl.BlockSpec(memory_space=pltpu.SMEM),
            anywhere,
            pl.BlockSpec(memory_space=pltpu.VMEM),
            anywhere,
            anywhere,
        ],
        out_specs=[anywhere] * 2,
        out_shape=[
            jax.ShapeDtypeStruct((rows, width + LANES), BF),
            jax.ShapeDtypeStruct((depth, 2 * kv_width), BF),
        ],
        scratch_shapes=[
            pltpu.VMEM((slots, SLOT, width), BF),
            pltpu.VMEM((rows, LANES), BF),
            pltpu.VMEM((depth, 2 * kv_width), BF),
            pltpu.SemaphoreType.DMA((slots,)),
            pltpu.SemaphoreType.DMA((slots,)),
            pltpu.SemaphoreType.DMA((slots,)),
            pltpu.SemaphoreType.DMA((3,)),
        ],
        compiler_params=params(),
        cost_estimate=cost(0, 2 * rows * width),
    )(destinations, hidden, adv, key_weight, value_weight)


def place_rows(lengths_ref, keep_ref, dest_ref, offsets_ref, place, mask, empty):
    rows = place.shape[0]
    dp_count, fsdp_count, slots = lengths_ref.shape
    dp_index, group = dp_fsdp()

    def of_group(ref):
        picked = lax.broadcasted_iota(jnp.int32, (dp_count, fsdp_count, slots), 1) == group
        return jnp.sum(jnp.where(picked, ref[...], 0), axis=1)

    keep = keep_ref[...]
    same = lax.broadcasted_iota(jnp.int32, (dp_count, dp_count), 0) == lax.broadcasted_iota(
        jnp.int32, (dp_count, dp_count), 1
    )
    picked = lax.broadcasted_iota(jnp.int32, keep.shape, 0) == group
    keep_row = jnp.sum(jnp.where(picked, keep, 0), axis=0, keepdims=True)
    keep_column = jnp.sum(jnp.where(same, keep_row, 0), axis=1, keepdims=True)
    count = jnp.float32(0.0)
    for source in range(dp_count):
        kept = lengths_ref[source] * keep[:, source : source + 1]
        count += jnp.sum(kept.astype(F32))
    kept = of_group(lengths_ref) * keep_column
    incoming = (of_group(dest_ref) == dp_index) & (kept > 0)
    offset = jnp.sum(jnp.where(incoming, of_group(offsets_ref), 0), axis=1, keepdims=True)
    length = jnp.sum(jnp.where(incoming, kept, 0), axis=1, keepdims=True)

    offset_row = jnp.sum(jnp.where(same, offset, 0), axis=0, keepdims=True)
    length_row = jnp.sum(jnp.where(same, length, 0), axis=0, keepdims=True)
    source = lax.broadcasted_iota(jnp.int32, (rows, dp_count), 1)
    relative = lax.broadcasted_iota(jnp.int32, (rows, dp_count), 0) - offset_row
    inside = (relative >= 0) & (relative < length_row)
    filled = jnp.sum(jnp.where(inside, 1, 0), axis=1, keepdims=True) > 0
    position = jnp.sum(jnp.where(inside, relative, 0), axis=1, keepdims=True)
    origin = jnp.sum(jnp.where(inside, source * SLOT + relative, 0), axis=1, keepdims=True)
    origin = jnp.where(filled, origin, -1)
    wide = lax.broadcasted_iota(jnp.int32, (rows, rows), 1)
    place[...] = jnp.where(wide == origin, 1.0, 0.0).astype(BF)
    empty[...] = jnp.where(filled, 0.0, 1.0)

    row = lax.broadcasted_iota(jnp.int32, (rows, HD), 0)
    lane = lax.broadcasted_iota(jnp.int32, (rows, HD), 1)
    first = row - position
    window = jnp.zeros((rows, HD), jnp.int32)
    for start, size, at in row_blocks(rows):
        window = jnp.where(row >= start, at - SLOT, window)
    seen = window + lane
    mask[...] = jnp.where(filled & (seen >= first) & (seen <= row), 1.0, 0.0)
    return count, position


def attend_kernel(
    lengths_ref,
    keep_ref,
    dest_ref,
    offsets_ref,
    got_ref,
    weight_ref,
    query_ref,
    upstream_ref,
    ratio_ref,
    cos_table_ref,
    sin_table_ref,
    out_ref,
    kv_grad_ref,
    rows_buf,
    weight_buf,
    adv_buf,
    sems,
    acc_ref,
    kv_ref,
    kv_pad,
    key_grad,
    value_grad,
    coef_ref,
    place_ref,
    mask_ref,
    empty_ref,
    cos_ref,
    sin_ref,
):
    step = pl.program_id(0)
    rows = query_ref.shape[0]
    kv_width = acc_ref.shape[1] // 2
    depth = rows_buf.shape[2]

    def arrival(k):
        here = pl.ds(pl.multiple_of(k * depth, depth), depth)
        return (
            pltpu.make_async_copy(got_ref.at[:, here], rows_buf.at[k], sems.at[0, k]),
            pltpu.make_async_copy(weight_ref.at[here, :], weight_buf.at[k], sems.at[1, k]),
        )

    def adv_arrival():
        here = pl.ds(RING * depth, LANES)
        return pltpu.make_async_copy(got_ref.at[:, here], adv_buf, sems.at[0, RING])

    @pl.when(step == 0)
    def _():
        for k in range(RING):
            for copy in arrival(k):
                copy.start()
        adv_arrival().start()

    @pl.when(step == 0)
    def _():
        count, position = place_rows(
            lengths_ref, keep_ref, dest_ref, offsets_ref, place_ref, mask_ref, empty_ref
        )
        at = lax.broadcasted_iota(jnp.int32, (rows, HD), 1) == position
        at = jnp.where(at, 1.0, 0.0)
        exact = lax.Precision.HIGHEST
        cos_ref[...] = jnp.dot(
            at, cos_table_ref[...], preferred_element_type=F32, precision=exact
        )
        sin_ref[...] = jnp.dot(
            at, sin_table_ref[...], preferred_element_type=F32, precision=exact
        )
        adv_arrival().wait()
        adv = jnp.dot(place_ref[...], adv_buf[...], preferred_element_type=F32)
        ratio = column_of(ratio_ref)
        clipped = (adv > 0) & (ratio > clip_high) | (adv < 0) & (ratio < clip_low)
        coef_ref[...] = jnp.where(clipped, 0.0, -loss_scale * adv * ratio) / count

    @pl.when(step < RING)
    def _():
        for copy in arrival(step):
            copy.wait()
        part = jnp.dot(rows_buf[step], weight_buf[step], preferred_element_type=F32)

        @pl.when(step == 0)
        def _():
            acc_ref[...] = part

        @pl.when(step > 0)
        def _():
            acc_ref[...] += part

    @pl.when(step == RING - 1)
    def _():
        for slot in range(rows // SLOT):
            here = pl.ds(slot * SLOT, SLOT)
            cosine = cos_table_ref[pl.ds(0, SLOT), :]
            sine = sin_table_ref[pl.ds(0, SLOT), :]
            for head in range(kv_width // HD):
                columns = pl.ds(head * HD, HD)
                key = acc_ref[here, columns]
                turned = key * cosine + pltpu.roll(key, HD // 2, 1) * sine
                kv_ref[here, columns] = turned.astype(BF)
            values = pl.ds(kv_width, kv_width)
            kv_ref[here, values] = acc_ref[here, values].astype(BF)
        kv_pad[pl.ds(0, SLOT), :] = jnp.zeros((SLOT, 2 * kv_width), BF)
        kv_pad[pl.ds(SLOT, rows), :] = jnp.dot(
            place_ref[...], kv_ref[...], preferred_element_type=F32
        ).astype(BF)

    @pl.when(step >= RING)
    def _():
        attend_head(
            step - RING,
            query_ref,
            upstream_ref,
            out_ref,
            kv_grad_ref,
            kv_pad,
            key_grad,
            value_grad,
            coef_ref,
            place_ref,
            mask_ref,
            empty_ref,
            cos_ref,
            sin_ref,
        )


def attend_head(
    head,
    query_ref,
    upstream_ref,
    out_ref,
    kv_grad_ref,
    kv_pad,
    key_grad,
    value_grad,
    coef_ref,
    place_ref,
    mask_ref,
    empty_ref,
    cos_ref,
    sin_ref,
):
    rows = query_ref.shape[0]
    group = query_ref.shape[1] // HD
    kv_width = kv_pad.shape[1] // 2
    scale = 1.0 / math.sqrt(HD)
    body = pl.ds(SLOT, rows)
    key_columns = pl.ds(pl.multiple_of(head * HD, HD), HD)
    value_columns = pl.ds(pl.multiple_of(kv_width + head * HD, HD), HD)
    across = (((1,), (1,)), ((), ()))
    along = (((0,), (0,)), ((), ()))
    key_grad[...] = jnp.zeros_like(key_grad)
    value_grad[...] = jnp.zeros_like(value_grad)
    for first, size, window in row_blocks(rows):
        here = pl.ds(first, size)
        span = pl.ds(window, HD)
        coef = coef_ref[here, :]
        allowed = mask_ref[here, :] > 0.0
        empty = empty_ref[here, :]
        allowed = jnp.broadcast_to(allowed[None], (group, size, HD)).reshape(group * size, HD)
        empty = jnp.broadcast_to(empty[None], (group, size, 1)).reshape(group * size, 1)
        query = jnp.concatenate(
            [query_ref[here, pl.ds(g * HD, HD)] for g in range(group)], axis=0
        )
        grad = jnp.concatenate(
            [
                (coef * upstream_ref[here, pl.ds(g * HD, HD)].astype(F32)).astype(BF)
                for g in range(group)
            ],
            axis=0,
        )
        key = kv_pad[span, key_columns]
        value = kv_pad[span, value_columns]
        scores = lax.dot_general(query, key, across, preferred_element_type=F32) * scale
        raw = jnp.where(allowed, jnp.exp(scores), 0.0)
        normed = raw * (1.0 / (jnp.sum(raw, axis=-1, keepdims=True) + empty))
        normed_low = normed.astype(BF)
        output = jnp.dot(normed_low, value, preferred_element_type=F32).astype(BF)
        for g in range(group):
            out_ref[here, pl.ds(g * HD, HD)] = output[g * size : (g + 1) * size]
        grad_normed = lax.dot_general(grad, value, across, preferred_element_type=F32)
        delta = jnp.sum(normed * grad_normed, axis=-1, keepdims=True)
        grad_scores = (normed * (grad_normed - delta) * scale).astype(BF)
        key_grad[span, :] += lax.dot_general(
            grad_scores, query, along, preferred_element_type=F32
        )
        value_grad[span, :] += lax.dot_general(
            normed_low, grad, along, preferred_element_type=F32
        )
    turned = key_grad[body, :]
    key_back = turned * cos_ref[...] - pltpu.roll(turned, HD // 2, 1) * sin_ref[...]
    both = jnp.concatenate([key_back.astype(BF), value_grad[body, :].astype(BF)], axis=1)
    kv_grad_ref[...] = lax.dot_general(
        both, place_ref[...], along, preferred_element_type=F32
    ).astype(BF)


def attend(plan, got, weights, queries, upstream, ratios):
    rows = got.shape[0]
    width, kv_columns = weights.shape
    heads = kv_columns // (2 * HD)
    query_width = queries.shape[1] // heads
    depth = width // RING
    anywhere = pl.BlockSpec(memory_space=pl.ANY)
    tables = [jnp.asarray(table) for table in slot_tables(HD)]
    whole = lambda array: pl.BlockSpec(array.shape, lambda k: (0,) * array.ndim)
    late = lambda k: jnp.maximum(k - RING, 0)
    return pl.pallas_call(
        attend_kernel,
        grid=(RING + heads,),
        in_specs=[whole(array) for array in plan]
        + [
            anywhere,
            anywhere,
            pl.BlockSpec((rows, query_width), lambda k: (0, late(k))),
            pl.BlockSpec((rows, query_width), lambda k: (0, late(k))),
            whole(ratios),
            whole(tables[0]),
            whole(tables[1]),
        ],
        out_specs=[
            pl.BlockSpec((rows, query_width), lambda k: (0, late(k))),
            pl.BlockSpec((2 * HD, rows), lambda k: (late(k), 0)),
        ],
        out_shape=[
            jax.ShapeDtypeStruct(queries.shape, BF),
            jax.ShapeDtypeStruct((kv_columns, rows), BF),
        ],
        scratch_shapes=[
            pltpu.VMEM((RING, rows, depth), BF),
            pltpu.VMEM((RING, depth, kv_columns), BF),
            pltpu.VMEM((rows, LANES), BF),
            pltpu.SemaphoreType.DMA((2, RING + 1)),
            pltpu.VMEM((rows, kv_columns), F32),
            pltpu.VMEM((rows, kv_columns), BF),
            pltpu.VMEM((rows + SLOT, kv_columns), BF),
            pltpu.VMEM((rows + SLOT, HD), F32),
            pltpu.VMEM((rows + SLOT, HD), F32),
            pltpu.VMEM((rows, LANES), F32),
            pltpu.VMEM((rows, rows), BF),
            pltpu.VMEM((rows, HD), F32),
            pltpu.VMEM((rows, 1), F32),
            pltpu.VMEM((rows, HD), F32),
            pltpu.VMEM((rows, HD), F32),
        ],
        compiler_params=params(),
        cost_estimate=cost(
            2 * rows * width * kv_columns + 10 * rows * queries.shape[1] * HD,
            rows * width + width * kv_columns + 3 * rows * queries.shape[1],
        ),
    )(*plan, got, weights, queries, upstream, ratios, *tables)


def grad_kernel(
    own_ref,
    other_ref,
    got_ref,
    sibling_ref,
    *refs,
):
    first_refs, rest_ref = refs[:RING], refs[RING]
    own_buf, other_buf, mine_buf, sibling_buf, first_buf, rest_buf, sems, in_sems, out_sems = refs[
        RING + 1 :
    ]
    piece = mine_buf.shape[2]
    whole = [
        pltpu.make_async_copy(own_ref, own_buf, sems.at[0]),
        pltpu.make_async_copy(other_ref, other_buf, sems.at[1]),
    ]
    blocks = [lax.rem(lax.axis_index("x") + k, RING) for k in range(RING)]
    arrive = []
    for k in range(RING):
        start = (2 * blocks[k] + lax.axis_index("core")) * piece
        here = pl.ds(pl.multiple_of(start, LANES), piece)
        arrive.append(
            (
                pltpu.make_async_copy(got_ref.at[:, here], mine_buf.at[k], in_sems.at[0, k]),
                pltpu.make_async_copy(
                    sibling_ref.at[:, here], sibling_buf.at[k], in_sems.at[1, k]
                ),
            )
        )
    for copy in (whole[0], arrive[0][0], whole[1], arrive[0][1]):
        copy.start()
    for pair in arrive[1:]:
        for copy in pair:
            copy.start()
    for copy in whole:
        copy.wait()
    leave = []
    for k in range(RING):
        for copy in arrive[k]:
            copy.wait()
        product = jnp.dot(own_buf[...], mine_buf[k], preferred_element_type=F32) + jnp.dot(
            other_buf[...], sibling_buf[k], preferred_element_type=F32
        )
        product = product.astype(BF)
        first_buf[k] = product[:SPLIT]
        rest_buf[k] = product[SPLIT:].reshape(rest_buf.shape[1:])
        pair = (
            pltpu.make_async_copy(first_buf.at[k], first_refs[k], out_sems.at[0, k]),
            pltpu.make_async_copy(
                rest_buf.at[k], rest_ref.at[:, blocks[k]], out_sems.at[1, k]
            ),
        )
        for copy in pair:
            copy.start()
            leave.append(copy)
    for copy in leave:
        copy.wait()


def grad_parts(own, other, got, sibling, width, places):
    columns, rows = own.shape
    piece = width // (2 * RING)
    size = (columns - SPLIT) // places
    anywhere = pl.BlockSpec(memory_space=pl.ANY)
    *first, rest = pl.pallas_call(
        grad_kernel,
        in_specs=[anywhere] * 4,
        out_specs=[anywhere] * (RING + 1),
        out_shape=[jax.ShapeDtypeStruct((SPLIT, piece), BF)] * RING
        + [jax.ShapeDtypeStruct((places, RING, size, piece), BF)],
        scratch_shapes=[
            pltpu.VMEM((columns, rows), BF),
            pltpu.VMEM((columns, rows), BF),
            pltpu.VMEM((RING, rows, piece), BF),
            pltpu.VMEM((RING, rows, piece), BF),
            pltpu.VMEM((RING, SPLIT, piece), BF),
            pltpu.VMEM((RING, places, size, piece), BF),
            pltpu.SemaphoreType.DMA((2,)),
            pltpu.SemaphoreType.DMA((2, RING)),
            pltpu.SemaphoreType.DMA((2, RING)),
        ],
        compiler_params=params(),
        cost_estimate=cost(
            4 * rows * columns * RING * piece, RING * piece * (2 * rows + columns)
        ),
    )(own, other, got, sibling)
    return first, rest


def sum_places_kernel(parts_ref, *out_refs):
    for k in range(RING):
        block = lax.rem(lax.axis_index("x") + k, RING)
        terms = [parts_ref[place, block].astype(F32) for place in range(parts_ref.shape[0])]
        while len(terms) > 1:
            terms = [terms[i] + terms[i + 1] for i in range(0, len(terms), 2)]
        out_refs[k][...] = terms[0].astype(BF)


def sum_places(parts):
    shape = jax.ShapeDtypeStruct(parts.shape[2:], BF)
    return pl.pallas_call(
        sum_places_kernel,
        out_shape=[shape] * RING,
        compiler_params=params(),
        cost_estimate=cost(0, parts.size),
    )(parts)


def finish_kernel(spread_ref, key_ref, value_ref):
    places, both, _ = spread_ref.shape
    size = both // 2
    per_head = HD // size
    for part in range(2):
        for i in range(places // per_head):
            rows = [
                spread_ref[i * per_head + j, pl.ds(part * size, size), :].astype(F32)
                for j in range(per_head)
            ]
            block = jnp.concatenate(rows, axis=0).T
            head = (part * places // per_head + i) // 2
            out_ref = value_ref if i % 2 else key_ref
            out_ref[:, pl.ds(head * HD, HD)] = block


def finish(spread, kv_width):
    columns = spread.shape[2]
    return pl.pallas_call(
        finish_kernel,
        out_shape=[jax.ShapeDtypeStruct((columns, kv_width), F32)] * 2,
        compiler_params=params(),
        cost_estimate=cost(0, 3 * spread.size),
    )(spread)


def total(parts):
    own, after, opposite, before = [part.astype(F32) for part in parts]
    return (own + opposite) + (after + before)


def shifted(value, k):
    return lax.ppermute(value, "x", [(i, (i + k) % RING) for i in range(RING)])


def exchange(parts):
    far = shifted(parts[2], 2)
    return [parts[0], shifted(parts[1], 1), far, shifted(parts[3], 3)]


def swap_cores(value):
    return lax.ppermute(value, "core", [(0, 1), (1, 0)])


def over_dp(value):
    return lax.all_to_all(value, DP, split_axis=0, concat_axis=0, tiled=True)


def on_device(
    hidden,
    advantages,
    queries,
    upstream,
    ratios,
    key_weight,
    value_weight,
    lengths,
    keep_flags,
    destinations,
    offsets,
):
    dp_count = lengths.shape[0]
    rows_here, model_width = hidden.shape
    kv_width = key_weight.shape[1]
    adv = advantages.reshape(rows_here // LANES, LANES)
    sent, weights = order(destinations, hidden, adv, key_weight, value_weight)
    weights = lax.all_gather(weights, FSDP, axis=0, tiled=True)
    got = over_dp(sent.reshape(dp_count, SLOT, sent.shape[1])).reshape(sent.shape)
    sibling = swap_cores(got)
    plan = (lengths, keep_flags, destinations, offsets)
    ratios = ratios.reshape(rows_here // LANES, LANES)
    attention, own = attend(plan, got, weights, queries, upstream, ratios)
    other = swap_cores(own)

    first, rest = grad_parts(own, other, got, sibling, model_width, dp_count)
    rest = over_dp(rest)
    first = exchange(first)
    rest = exchange(sum_places(rest))
    first = total(first).astype(BF)
    first = over_dp(first.reshape(dp_count, SPLIT // dp_count, first.shape[1]))
    summed = jnp.concatenate([jnp.sum(first.astype(F32), axis=0), total(rest)], axis=0)
    spread = over_dp(jnp.broadcast_to(summed.astype(BF)[None], (dp_count,) + summed.shape))
    grad_key, grad_value = finish(spread, kv_width)
    return (attention, grad_key, grad_value)


def solution(mesh):
    chips = {"y": RING, "z": RING, "x": RING, "core": 2}
    fine = Mesh(mesh.devices.reshape(tuple(chips.values())), tuple(chips))
    in_specs = (
        P(ALL, None),
        P(ALL),
        P(ALL, None),
        P(ALL, None),
        P(ALL),
        P(FSDP, None),
        P(FSDP, None),
        P(),
        P(),
        P(),
        P(),
    )
    out_specs = (P(ALL, None), P(FSDP, None), P(FSDP, None))
    return jax.shard_map(
        on_device, mesh=fine, in_specs=in_specs, out_specs=out_specs, check_vma=False
    )
```

```python
import math

import jax
import jax.numpy as jnp
import numpy as np
from jax import lax
from jax.experimental import pallas as pl
from jax.experimental.pallas import tpu as pltpu
from jax.sharding import Mesh
from jax.sharding import PartitionSpec as P

HD = 128
SLOT = 32
RING = 4
SPLIT = 512
VMEM_LIMIT = 56 * 1024 * 1024

rope_base = 1000000.0
loss_scale = 256.0
clip_low = 0.8
clip_high = 1.28

DP = ("y", "z")
FSDP = ("x", "core")
ALL = DP + FSDP
BF = jnp.bfloat16
F32 = jnp.float32
LANES = 128
AHEAD = 2


def row_blocks(rows):
    step = HD - SLOT
    blocks = []
    for first in range(0, rows, step):
        size = min(step, rows - first)
        blocks.append((first, size, min(first, rows + SLOT - HD)))
    return blocks


def slot_tables(rows=SLOT):
    frequency = rope_base ** (-(np.arange(HD // 2) * (2.0 / HD)))
    angle = np.arange(SLOT)[:, None] * frequency[None, :]
    cosine, sine = np.cos(angle), np.sin(angle)
    after = ((0, rows - SLOT), (0, 0))
    return (
        np.pad(np.concatenate([cosine, cosine], axis=1), after).astype(np.float32),
        np.pad(np.concatenate([-sine, sine], axis=1), after).astype(np.float32),
    )


def params():
    return pltpu.CompilerParams(vmem_limit_bytes=VMEM_LIMIT)


def cost(flops, count):
    return pl.CostEstimate(flops=int(flops), bytes_accessed=int(2 * count), transcendentals=0)


def dp_fsdp():
    dp_index = lax.axis_index("y") * RING + lax.axis_index("z")
    return dp_index, lax.axis_index("x") * 2 + lax.axis_index("core")


def column_of(row_ref):
    same = lax.broadcasted_iota(jnp.int32, (LANES, LANES), 0) == lax.broadcasted_iota(
        jnp.int32, (LANES, LANES), 1
    )
    parts = []
    for i in range(row_ref.shape[0]):
        row = row_ref[i : i + 1, :].astype(F32)
        parts.append(jnp.sum(jnp.where(same, row, 0.0), axis=1, keepdims=True))
    return jnp.concatenate(parts, axis=0)


def order_kernel(
    dest_ref,
    hidden_ref,
    adv_ref,
    key_ref,
    value_ref,
    sent_ref,
    weight_ref,
    rows_buf,
    adv_buf,
    weight_buf,
    in_sems,
    out_sems,
    adv_sems,
    weight_sems,
):
    dp_index, group = dp_fsdp()
    width = hidden_ref.shape[1]
    kv_width = key_ref.shape[1]
    slots = hidden_ref.shape[0] // SLOT
    both = [
        pltpu.make_async_copy(
            ref, weight_buf.at[:, pl.ds(i * kv_width, kv_width)], weight_sems.at[i]
        )
        for i, ref in enumerate((key_ref, value_ref))
    ]
    arrive, leave, adv_leave = [], [], []
    for slot in range(slots):
        here = pl.ds(slot * SLOT, SLOT)
        there = pl.ds(pl.multiple_of(dest_ref[dp_index, group, slot] * SLOT, SLOT), SLOT)
        arrive.append(
            pltpu.make_async_copy(hidden_ref.at[here, :], rows_buf.at[slot], in_sems.at[slot])
        )
        leave.append(
            pltpu.make_async_copy(
                rows_buf.at[slot], sent_ref.at[there, pl.ds(0, width)], out_sems.at[slot]
            )
        )
        adv_leave.append(
            pltpu.make_async_copy(
                adv_buf.at[here, :], sent_ref.at[there, pl.ds(width, LANES)], adv_sems.at[slot]
            )
        )
    for copy in both + arrive:
        copy.start()
    adv_buf[...] = jnp.broadcast_to(column_of(adv_ref), adv_buf.shape).astype(BF)
    for copy in adv_leave:
        copy.start()
    for copy in both:
        copy.wait()
    out = pltpu.make_async_copy(weight_buf, weight_ref, weight_sems.at[2])
    out.start()
    for slot in range(slots):
        arrive[slot].wait()
        leave[slot].start()
    out.wait()
    for copy in adv_leave + leave:
        copy.wait()


def order(destinations, hidden, adv, key_weight, value_weight):
    rows, width = hidden.shape
    depth, kv_width = key_weight.shape
    slots = rows // SLOT
    anywhere = pl.BlockSpec(memory_space=pl.ANY)
    return pl.pallas_call(
        order_kernel,
        in_specs=[
            pl.BlockSpec(memory_space=pltpu.SMEM),
            anywhere,
            pl.BlockSpec(memory_space=pltpu.VMEM),
            anywhere,
            anywhere,
        ],
        out_specs=[anywhere] * 2,
        out_shape=[
            jax.ShapeDtypeStruct((rows, width + LANES), BF),
            jax.ShapeDtypeStruct((depth, 2 * kv_width), BF),
        ],
        scratch_shapes=[
            pltpu.VMEM((slots, SLOT, width), BF),
            pltpu.VMEM((rows, LANES), BF),
            pltpu.VMEM((depth, 2 * kv_width), BF),
            pltpu.SemaphoreType.DMA((slots,)),
            pltpu.SemaphoreType.DMA((slots,)),
            pltpu.SemaphoreType.DMA((slots,)),
            pltpu.SemaphoreType.DMA((3,)),
        ],
        compiler_params=params(),
        cost_estimate=cost(0, 2 * rows * width),
    )(destinations, hidden, adv, key_weight, value_weight)


def place_rows(lengths_ref, keep_ref, dest_ref, offsets_ref, place, mask, empty):
    rows = place.shape[0]
    dp_count, fsdp_count, slots = lengths_ref.shape
    dp_index, group = dp_fsdp()

    def of_group(ref):
        picked = lax.broadcasted_iota(jnp.int32, (dp_count, fsdp_count, slots), 1) == group
        return jnp.sum(jnp.where(picked, ref[...], 0), axis=1)

    keep = keep_ref[...]
    same = lax.broadcasted_iota(jnp.int32, (dp_count, dp_count), 0) == lax.broadcasted_iota(
        jnp.int32, (dp_count, dp_count), 1
    )
    picked = lax.broadcasted_iota(jnp.int32, keep.shape, 0) == group
    keep_row = jnp.sum(jnp.where(picked, keep, 0), axis=0, keepdims=True)
    keep_column = jnp.sum(jnp.where(same, keep_row, 0), axis=1, keepdims=True)
    count = jnp.float32(0.0)
    for source in range(dp_count):
        kept = lengths_ref[source] * keep[:, source : source + 1]
        count += jnp.sum(kept.astype(F32))
    kept = of_group(lengths_ref) * keep_column
    incoming = (of_group(dest_ref) == dp_index) & (kept > 0)
    offset = jnp.sum(jnp.where(incoming, of_group(offsets_ref), 0), axis=1, keepdims=True)
    length = jnp.sum(jnp.where(incoming, kept, 0), axis=1, keepdims=True)

    offset_row = jnp.sum(jnp.where(same, offset, 0), axis=0, keepdims=True)
    length_row = jnp.sum(jnp.where(same, length, 0), axis=0, keepdims=True)
    source = lax.broadcasted_iota(jnp.int32, (rows, dp_count), 1)
    relative = lax.broadcasted_iota(jnp.int32, (rows, dp_count), 0) - offset_row
    inside = (relative >= 0) & (relative < length_row)
    origin = jnp.sum(
        jnp.where(inside, source * SLOT + relative + 1, 0), axis=1, keepdims=True
    )
    origin = origin - 1
    filled = origin >= 0
    position = jnp.where(filled, lax.rem(origin, SLOT), 0)
    wide = lax.broadcasted_iota(jnp.int32, (rows, rows), 1)
    place[...] = jnp.where(wide == origin, 1.0, 0.0).astype(BF)
    empty[...] = jnp.where(filled, 0.0, 1.0)

    row = lax.broadcasted_iota(jnp.int32, (rows, HD), 0)
    lane = lax.broadcasted_iota(jnp.int32, (rows, HD), 1)
    first = row - position
    window = jnp.zeros((rows, HD), jnp.int32)
    for start, size, at in row_blocks(rows):
        window = jnp.where(row >= start, at - SLOT, window)
    seen = window + lane
    mask[...] = jnp.where(filled & (seen >= first) & (seen <= row), 1.0, 0.0)
    return count, position


def attend_kernel(
    lengths_ref,
    keep_ref,
    dest_ref,
    offsets_ref,
    got_ref,
    weight_ref,
    query_ref,
    upstream_ref,
    ratio_ref,
    cos_table_ref,
    sin_table_ref,
    out_ref,
    kv_grad_ref,
    rows_buf,
    weight_buf,
    adv_buf,
    sems,
    acc_ref,
    kv_ref,
    kv_pad,
    key_grad,
    value_grad,
    coef_ref,
    place_ref,
    mask_ref,
    empty_ref,
    cos_ref,
    sin_ref,
):
    step = pl.program_id(0)
    rows = query_ref.shape[0]
    kv_width = acc_ref.shape[1] // 2
    depth = rows_buf.shape[2]

    def arrival(k):
        here = pl.ds(pl.multiple_of(k * depth, depth), depth)
        return (
            pltpu.make_async_copy(got_ref.at[:, here], rows_buf.at[k], sems.at[0, k]),
            pltpu.make_async_copy(weight_ref.at[here, :], weight_buf.at[k], sems.at[1, k]),
        )

    def adv_arrival():
        here = pl.ds(RING * depth, LANES)
        return pltpu.make_async_copy(got_ref.at[:, here], adv_buf, sems.at[0, RING])

    @pl.when(step == 0)
    def _():
        adv_arrival().start()
        for k in range(AHEAD):
            for copy in arrival(k):
                copy.start()

    @pl.when(step == 0)
    def _():
        count, position = place_rows(
            lengths_ref, keep_ref, dest_ref, offsets_ref, place_ref, mask_ref, empty_ref
        )
        at = lax.broadcasted_iota(jnp.int32, (rows, HD), 1) == position
        at = jnp.where(at, 1.0, 0.0)
        exact = lax.Precision.HIGHEST
        cos_ref[...] = jnp.dot(
            at, cos_table_ref[...], preferred_element_type=F32, precision=exact
        )
        sin_ref[...] = jnp.dot(
            at, sin_table_ref[...], preferred_element_type=F32, precision=exact
        )
        adv_arrival().wait()
        adv = jnp.dot(place_ref[...], adv_buf[...], preferred_element_type=F32)
        ratio = column_of(ratio_ref)
        clipped = (adv > 0) & (ratio > clip_high) | (adv < 0) & (ratio < clip_low)
        coef_ref[...] = jnp.where(clipped, 0.0, -loss_scale * adv * ratio) / count

    @pl.when(step < RING)
    def _():
        for copy in arrival(step):
            copy.wait()

        @pl.when(step + AHEAD < RING)
        def _():
            for copy in arrival(step + AHEAD):
                copy.start()

        part = jnp.dot(rows_buf[step], weight_buf[step], preferred_element_type=F32)

        @pl.when(step == 0)
        def _():
            acc_ref[...] = part

        @pl.when(step > 0)
        def _():
            acc_ref[...] += part

    @pl.when(step == RING - 1)
    def _():
        for slot in range(rows // SLOT):
            here = pl.ds(slot * SLOT, SLOT)
            cosine = cos_table_ref[pl.ds(0, SLOT), :]
            sine = sin_table_ref[pl.ds(0, SLOT), :]
            for head in range(kv_width // HD):
                columns = pl.ds(head * HD, HD)
                key = acc_ref[here, columns]
                turned = key * cosine + pltpu.roll(key, HD // 2, 1) * sine
                kv_ref[here, columns] = turned.astype(BF)
            values = pl.ds(kv_width, kv_width)
            kv_ref[here, values] = acc_ref[here, values].astype(BF)
        kv_pad[pl.ds(0, SLOT), :] = jnp.zeros((SLOT, 2 * kv_width), BF)
        kv_pad[pl.ds(SLOT, rows), :] = jnp.dot(
            place_ref[...], kv_ref[...], preferred_element_type=F32
        ).astype(BF)

    @pl.when(step >= RING)
    def _():
        attend_head(
            step - RING,
            query_ref,
            upstream_ref,
            out_ref,
            kv_grad_ref,
            kv_pad,
            key_grad,
            value_grad,
            coef_ref,
            place_ref,
            mask_ref,
            empty_ref,
            cos_ref,
            sin_ref,
        )


def attend_head(
    head,
    query_ref,
    upstream_ref,
    out_ref,
    kv_grad_ref,
    kv_pad,
    key_grad,
    value_grad,
    coef_ref,
    place_ref,
    mask_ref,
    empty_ref,
    cos_ref,
    sin_ref,
):
    rows = query_ref.shape[0]
    group = query_ref.shape[1] // HD
    kv_width = kv_pad.shape[1] // 2
    scale = 1.0 / math.sqrt(HD)
    body = pl.ds(SLOT, rows)
    key_columns = pl.ds(pl.multiple_of(head * HD, HD), HD)
    value_columns = pl.ds(pl.multiple_of(kv_width + head * HD, HD), HD)
    across = (((1,), (1,)), ((), ()))
    along = (((0,), (0,)), ((), ()))
    key_grad[...] = jnp.zeros_like(key_grad)
    value_grad[...] = jnp.zeros_like(value_grad)
    for first, size, window in row_blocks(rows):
        here = pl.ds(first, size)
        span = pl.ds(window, HD)
        coef = coef_ref[here, :]
        allowed = mask_ref[here, :] > 0.0
        empty = empty_ref[here, :]
        allowed = jnp.broadcast_to(allowed[None], (group, size, HD)).reshape(group * size, HD)
        empty = jnp.broadcast_to(empty[None], (group, size, 1)).reshape(group * size, 1)
        query = jnp.concatenate(
            [query_ref[here, pl.ds(g * HD, HD)] for g in range(group)], axis=0
        )
        grad = jnp.concatenate(
            [
                (coef * upstream_ref[here, pl.ds(g * HD, HD)].astype(F32)).astype(BF)
                for g in range(group)
            ],
            axis=0,
        )
        key = kv_pad[span, key_columns]
        value = kv_pad[span, value_columns]
        scores = lax.dot_general(query, key, across, preferred_element_type=F32) * scale
        raw = jnp.where(allowed, jnp.exp(scores), 0.0)
        normed = raw * (1.0 / (jnp.sum(raw, axis=-1, keepdims=True) + empty))
        normed_low = normed.astype(BF)
        output = jnp.dot(normed_low, value, preferred_element_type=F32).astype(BF)
        for g in range(group):
            out_ref[here, pl.ds(g * HD, HD)] = output[g * size : (g + 1) * size]
        grad_normed = lax.dot_general(grad, value, across, preferred_element_type=F32)
        delta = jnp.sum(normed * grad_normed, axis=-1, keepdims=True)
        grad_scores = (normed * (grad_normed - delta) * scale).astype(BF)
        key_grad[span, :] += lax.dot_general(
            grad_scores, query, along, preferred_element_type=F32
        )
        value_grad[span, :] += lax.dot_general(
            normed_low, grad, along, preferred_element_type=F32
        )
    turned = key_grad[body, :]
    key_back = turned * cos_ref[...] - pltpu.roll(turned, HD // 2, 1) * sin_ref[...]
    both = jnp.concatenate([key_back.astype(BF), value_grad[body, :].astype(BF)], axis=1)
    kv_grad_ref[...] = lax.dot_general(
        both, place_ref[...], along, preferred_element_type=F32
    ).astype(BF)


def attend(plan, got, weights, queries, upstream, ratios):
    rows = got.shape[0]
    width, kv_columns = weights.shape
    heads = kv_columns // (2 * HD)
    query_width = queries.shape[1] // heads
    depth = width // RING
    anywhere = pl.BlockSpec(memory_space=pl.ANY)
    tables = [jnp.asarray(table) for table in slot_tables(HD)]
    whole = lambda array: pl.BlockSpec(array.shape, lambda k: (0,) * array.ndim)
    late = lambda k: jnp.maximum(k - RING, 0)
    return pl.pallas_call(
        attend_kernel,
        grid=(RING + heads,),
        in_specs=[whole(array) for array in plan]
        + [
            anywhere,
            anywhere,
            pl.BlockSpec((rows, query_width), lambda k: (0, late(k))),
            pl.BlockSpec((rows, query_width), lambda k: (0, late(k))),
            whole(ratios),
            whole(tables[0]),
            whole(tables[1]),
        ],
        out_specs=[
            pl.BlockSpec((rows, query_width), lambda k: (0, late(k))),
            pl.BlockSpec((2 * HD, rows), lambda k: (late(k), 0)),
        ],
        out_shape=[
            jax.ShapeDtypeStruct(queries.shape, BF),
            jax.ShapeDtypeStruct((kv_columns, rows), BF),
        ],
        scratch_shapes=[
            pltpu.VMEM((RING, rows, depth), BF),
            pltpu.VMEM((RING, depth, kv_columns), BF),
            pltpu.VMEM((rows, LANES), BF),
            pltpu.SemaphoreType.DMA((2, RING + 1)),
            pltpu.VMEM((rows, kv_columns), F32),
            pltpu.VMEM((rows, kv_columns), BF),
            pltpu.VMEM((rows + SLOT, kv_columns), BF),
            pltpu.VMEM((rows + SLOT, HD), F32),
            pltpu.VMEM((rows + SLOT, HD), F32),
            pltpu.VMEM((rows, LANES), F32),
            pltpu.VMEM((rows, rows), BF),
            pltpu.VMEM((rows, HD), F32),
            pltpu.VMEM((rows, 1), F32),
            pltpu.VMEM((rows, HD), F32),
            pltpu.VMEM((rows, HD), F32),
        ],
        compiler_params=params(),
        cost_estimate=cost(
            2 * rows * width * kv_columns + 10 * rows * queries.shape[1] * HD,
            rows * width + width * kv_columns + 3 * rows * queries.shape[1],
        ),
    )(*plan, got, weights, queries, upstream, ratios, *tables)


def grad_kernel(
    own_ref,
    other_ref,
    got_ref,
    sibling_ref,
    first_ref,
    rest_ref,
    own_buf,
    other_buf,
    mine_buf,
    sibling_buf,
    first_buf,
    rest_buf,
    sems,
    in_sems,
    out_sems,
):
    piece = mine_buf.shape[2] // 2
    blocks = [lax.rem(lax.axis_index("x") + k, RING) for k in range(RING)]
    own = pltpu.make_async_copy(own_ref, own_buf, sems.at[0])
    other = pltpu.make_async_copy(other_ref, other_buf, sems.at[1])

    def arrival(source, target, k, row):
        start = (2 * blocks[k] + lax.axis_index("core")) * piece
        here = pl.ds(pl.multiple_of(start, LANES), piece)
        there = pl.ds((k % 2) * piece, piece)
        return pltpu.make_async_copy(
            source.at[:, here], target.at[k // 2, :, there], in_sems.at[row, k]
        )

    mine = [arrival(got_ref, mine_buf, k, 0) for k in range(RING)]
    sibling = [arrival(sibling_ref, sibling_buf, k, 1) for k in range(RING)]
    early = [own, mine[0], mine[1]]
    late = [[other, sibling[0], sibling[1]], [mine[2], mine[3], sibling[2], sibling[3]]]
    for copy in early + late[0]:
        copy.start()
    for copy in early:
        copy.wait()
    for copy in late[1]:
        copy.start()
    leave = []
    for half in range(2):
        product = jnp.dot(own_buf[...], mine_buf[half], preferred_element_type=F32)
        if half == 0:
            for copy in late[0]:
                copy.wait()
        product += jnp.dot(other_buf[...], sibling_buf[half], preferred_element_type=F32)
        product = product.astype(BF)
        for k in (2 * half, 2 * half + 1):
            columns = slice((k % 2) * piece, (k % 2 + 1) * piece)
            first_buf[k] = product[:SPLIT, columns]
            rest_buf[k] = product[SPLIT:, columns].reshape(rest_buf.shape[1:])
            pair = (
                pltpu.make_async_copy(first_buf.at[k], first_ref.at[blocks[k]], out_sems.at[0, k]),
                pltpu.make_async_copy(
                    rest_buf.at[k], rest_ref.at[:, blocks[k]], out_sems.at[1, k]
                ),
            )
            for copy in pair:
                copy.start()
                leave.append(copy)
        if half == 0:
            for copy in late[1]:
                copy.wait()
    for copy in leave:
        copy.wait()


def grad_parts(own, other, got, sibling, width, places):
    columns, rows = own.shape
    piece = width // (2 * RING)
    size = (columns - SPLIT) // places
    anywhere = pl.BlockSpec(memory_space=pl.ANY)
    return pl.pallas_call(
        grad_kernel,
        in_specs=[anywhere] * 4,
        out_specs=[anywhere] * 2,
        out_shape=[
            jax.ShapeDtypeStruct((RING, SPLIT, piece), BF),
            jax.ShapeDtypeStruct((places, RING, size, piece), BF),
        ],
        scratch_shapes=[
            pltpu.VMEM((columns, rows), BF),
            pltpu.VMEM((columns, rows), BF),
            pltpu.VMEM((2, rows, 2 * piece), BF),
            pltpu.VMEM((2, rows, 2 * piece), BF),
            pltpu.VMEM((RING, SPLIT, piece), BF),
            pltpu.VMEM((RING, places, size, piece), BF),
            pltpu.SemaphoreType.DMA((2,)),
            pltpu.SemaphoreType.DMA((2, RING)),
            pltpu.SemaphoreType.DMA((2, RING)),
        ],
        compiler_params=params(),
        cost_estimate=cost(
            4 * rows * columns * RING * piece, RING * piece * (2 * rows + columns)
        ),
    )(own, other, got, sibling)


def sum_places_kernel(parts_ref, *out_refs):
    for k in range(RING):
        block = lax.rem(lax.axis_index("x") + k, RING)
        terms = [parts_ref[place, block].astype(F32) for place in range(parts_ref.shape[0])]
        while len(terms) > 1:
            terms = [terms[i] + terms[i + 1] for i in range(0, len(terms), 2)]
        out_refs[k][...] = terms[0].astype(BF)


def sum_places(parts):
    shape = jax.ShapeDtypeStruct(parts.shape[2:], BF)
    return pl.pallas_call(
        sum_places_kernel,
        out_shape=[shape] * RING,
        compiler_params=params(),
        cost_estimate=cost(0, parts.size),
    )(parts)


def finish_kernel(spread_ref, key_ref, value_ref):
    places, both, _ = spread_ref.shape
    size = both // 2
    per_head = HD // size
    for part in range(2):
        for i in range(places // per_head):
            rows = [
                spread_ref[i * per_head + j, pl.ds(part * size, size), :].astype(F32)
                for j in range(per_head)
            ]
            block = jnp.concatenate(rows, axis=0).T
            head = (part * places // per_head + i) // 2
            out_ref = value_ref if i % 2 else key_ref
            out_ref[:, pl.ds(head * HD, HD)] = block


def finish(spread, kv_width):
    columns = spread.shape[2]
    return pl.pallas_call(
        finish_kernel,
        out_shape=[jax.ShapeDtypeStruct((columns, kv_width), F32)] * 2,
        compiler_params=params(),
        cost_estimate=cost(0, 3 * spread.size),
    )(spread)


def total(parts):
    own, after, opposite, before = [part.astype(F32) for part in parts]
    return (own + opposite) + (after + before)


def shifted(value, k):
    return lax.ppermute(value, "x", [(i, (i + k) % RING) for i in range(RING)])


def exchange(parts):
    far = shifted(parts[2], 2)
    return [parts[0], shifted(parts[1], 1), far, shifted(parts[3], 3)]


def swap_cores(value):
    return lax.ppermute(value, "core", [(0, 1), (1, 0)])


def over_dp(value):
    return lax.all_to_all(value, DP, split_axis=0, concat_axis=0, tiled=True)


def on_device(
    hidden,
    advantages,
    queries,
    upstream,
    ratios,
    key_weight,
    value_weight,
    lengths,
    keep_flags,
    destinations,
    offsets,
):
    dp_count = lengths.shape[0]
    rows_here, model_width = hidden.shape
    kv_width = key_weight.shape[1]
    adv = advantages.reshape(rows_here // LANES, LANES)
    sent, weights = order(destinations, hidden, adv, key_weight, value_weight)
    weights = lax.all_gather(weights, FSDP, axis=0, tiled=True)
    got = over_dp(sent.reshape(dp_count, SLOT, sent.shape[1])).reshape(sent.shape)
    sibling = swap_cores(got)
    plan = (lengths, keep_flags, destinations, offsets)
    ratios = ratios.reshape(rows_here // LANES, LANES)
    attention, own = attend(plan, got, weights, queries, upstream, ratios)
    other = swap_cores(own)

    first, rest = grad_parts(own, other, got, sibling, model_width, dp_count)
    first = lax.psum_scatter(
        first.reshape(-1, first.shape[2]), "x", scatter_dimension=0, tiled=True
    )
    rest = exchange(sum_places(over_dp(rest)))
    first = over_dp(first.reshape(dp_count, SPLIT // dp_count, first.shape[1]))
    summed = jnp.concatenate([jnp.sum(first.astype(F32), axis=0), total(rest)], axis=0)
    spread = over_dp(jnp.broadcast_to(summed.astype(BF)[None], (dp_count,) + summed.shape))
    grad_key, grad_value = finish(spread, kv_width)
    return (attention, grad_key, grad_value)


def solution(mesh):
    chips = {"y": RING, "z": RING, "x": RING, "core": 2}
    fine = Mesh(mesh.devices.reshape(tuple(chips.values())), tuple(chips))
    in_specs = (
        P(ALL, None),
        P(ALL),
        P(ALL, None),
        P(ALL, None),
        P(ALL),
        P(FSDP, None),
        P(FSDP, None),
        P(),
        P(),
        P(),
        P(),
    )
    out_specs = (P(ALL, None), P(FSDP, None), P(FSDP, None))
    return jax.shard_map(
        on_device, mesh=fine, in_specs=in_specs, out_specs=out_specs, check_vma=False
    )
```

```python
import math

import jax
import jax.numpy as jnp
import numpy as np
from jax import lax
from jax.experimental import pallas as pl
from jax.experimental.pallas import tpu as pltpu
from jax.sharding import Mesh
from jax.sharding import PartitionSpec as P

HD = 128
SLOT = 32
RING = 4
SPLIT = 3
VMEM_LIMIT = 56 * 1024 * 1024

rope_base = 1000000.0
loss_scale = 256.0
clip_low = 0.8
clip_high = 1.28

DP = ("y", "z")
FSDP = ("x", "core")
ALL = DP + FSDP
BF = jnp.bfloat16
F32 = jnp.float32
LANES = 128
AHEAD = 2


def row_blocks(rows):
    step = HD - SLOT
    blocks = []
    for first in range(0, rows, step):
        size = min(step, rows - first)
        blocks.append((first, size, min(first, rows + SLOT - HD)))
    return blocks


def slot_tables(rows=SLOT):
    frequency = rope_base ** (-(np.arange(HD // 2) * (2.0 / HD)))
    angle = np.arange(SLOT)[:, None] * frequency[None, :]
    cosine, sine = np.cos(angle), np.sin(angle)
    after = ((0, rows - SLOT), (0, 0))
    return (
        np.pad(np.concatenate([cosine, cosine], axis=1), after).astype(np.float32),
        np.pad(np.concatenate([-sine, sine], axis=1), after).astype(np.float32),
    )


def params(limit=VMEM_LIMIT):
    return pltpu.CompilerParams(vmem_limit_bytes=limit)


def cost(flops, count):
    return pl.CostEstimate(flops=int(flops), bytes_accessed=int(2 * count), transcendentals=0)


def dp_fsdp():
    dp_index = lax.axis_index("y") * RING + lax.axis_index("z")
    return dp_index, lax.axis_index("x") * 2 + lax.axis_index("core")


def column_of(row_ref):
    same = lax.broadcasted_iota(jnp.int32, (LANES, LANES), 0) == lax.broadcasted_iota(
        jnp.int32, (LANES, LANES), 1
    )
    parts = []
    for i in range(row_ref.shape[0]):
        row = row_ref[i : i + 1, :].astype(F32)
        parts.append(jnp.sum(jnp.where(same, row, 0.0), axis=1, keepdims=True))
    return jnp.concatenate(parts, axis=0)


def order_kernel(
    dest_ref,
    hidden_ref,
    adv_ref,
    key_ref,
    value_ref,
    sent_ref,
    weight_ref,
    rows_buf,
    adv_buf,
    weight_buf,
    in_sems,
    out_sems,
    adv_sems,
    weight_sems,
):
    dp_index, group = dp_fsdp()
    width = hidden_ref.shape[1]
    kv_width = key_ref.shape[1]
    slots = hidden_ref.shape[0] // SLOT
    both = [
        pltpu.make_async_copy(
            ref, weight_buf.at[:, pl.ds(i * kv_width, kv_width)], weight_sems.at[i]
        )
        for i, ref in enumerate((key_ref, value_ref))
    ]
    arrive, leave, adv_leave = [], [], []
    for slot in range(slots):
        here = pl.ds(slot * SLOT, SLOT)
        there = pl.ds(pl.multiple_of(dest_ref[dp_index, group, slot] * SLOT, SLOT), SLOT)
        arrive.append(
            pltpu.make_async_copy(hidden_ref.at[here, :], rows_buf.at[slot], in_sems.at[slot])
        )
        leave.append(
            pltpu.make_async_copy(
                rows_buf.at[slot], sent_ref.at[there, pl.ds(0, width)], out_sems.at[slot]
            )
        )
        adv_leave.append(
            pltpu.make_async_copy(
                adv_buf.at[here, :], sent_ref.at[there, pl.ds(width, LANES)], adv_sems.at[slot]
            )
        )
    for copy in both + arrive:
        copy.start()
    adv_buf[...] = jnp.broadcast_to(column_of(adv_ref), adv_buf.shape).astype(BF)
    for copy in adv_leave:
        copy.start()
    for copy in both:
        copy.wait()
    out = pltpu.make_async_copy(weight_buf, weight_ref, weight_sems.at[2])
    out.start()
    for slot in range(slots):
        arrive[slot].wait()
        leave[slot].start()
    out.wait()
    for copy in adv_leave + leave:
        copy.wait()


def order(destinations, hidden, adv, key_weight, value_weight):
    rows, width = hidden.shape
    depth, kv_width = key_weight.shape
    slots = rows // SLOT
    anywhere = pl.BlockSpec(memory_space=pl.ANY)
    return pl.pallas_call(
        order_kernel,
        in_specs=[
            pl.BlockSpec(memory_space=pltpu.SMEM),
            anywhere,
            pl.BlockSpec(memory_space=pltpu.VMEM),
            anywhere,
            anywhere,
        ],
        out_specs=[anywhere] * 2,
        out_shape=[
            jax.ShapeDtypeStruct((rows, width + LANES), BF),
            jax.ShapeDtypeStruct((depth, 2 * kv_width), BF),
        ],
        scratch_shapes=[
            pltpu.VMEM((slots, SLOT, width), BF),
            pltpu.VMEM((rows, LANES), BF),
            pltpu.VMEM((depth, 2 * kv_width), BF),
            pltpu.SemaphoreType.DMA((slots,)),
            pltpu.SemaphoreType.DMA((slots,)),
            pltpu.SemaphoreType.DMA((slots,)),
            pltpu.SemaphoreType.DMA((3,)),
        ],
        compiler_params=params(),
        cost_estimate=cost(0, 2 * rows * width),
    )(destinations, hidden, adv, key_weight, value_weight)


def place_rows(lengths_ref, keep_ref, dest_ref, offsets_ref, place, mask, empty):
    rows = place.shape[0]
    dp_count, fsdp_count, slots = lengths_ref.shape
    dp_index, group = dp_fsdp()

    def of_group(ref):
        picked = lax.broadcasted_iota(jnp.int32, (dp_count, fsdp_count, slots), 1) == group
        return jnp.sum(jnp.where(picked, ref[...], 0), axis=1)

    keep = keep_ref[...]
    same = lax.broadcasted_iota(jnp.int32, (dp_count, dp_count), 0) == lax.broadcasted_iota(
        jnp.int32, (dp_count, dp_count), 1
    )
    picked = lax.broadcasted_iota(jnp.int32, keep.shape, 0) == group
    keep_row = jnp.sum(jnp.where(picked, keep, 0), axis=0, keepdims=True)
    keep_column = jnp.sum(jnp.where(same, keep_row, 0), axis=1, keepdims=True)
    count = jnp.float32(0.0)
    for source in range(dp_count):
        kept = lengths_ref[source] * keep[:, source : source + 1]
        count += jnp.sum(kept.astype(F32))
    kept = of_group(lengths_ref) * keep_column
    incoming = (of_group(dest_ref) == dp_index) & (kept > 0)
    offset = jnp.sum(jnp.where(incoming, of_group(offsets_ref), 0), axis=1, keepdims=True)
    length = jnp.sum(jnp.where(incoming, kept, 0), axis=1, keepdims=True)

    offset_row = jnp.sum(jnp.where(same, offset, 0), axis=0, keepdims=True)
    length_row = jnp.sum(jnp.where(same, length, 0), axis=0, keepdims=True)
    source = lax.broadcasted_iota(jnp.int32, (rows, dp_count), 1)
    relative = lax.broadcasted_iota(jnp.int32, (rows, dp_count), 0) - offset_row
    inside = (relative >= 0) & (relative < length_row)
    origin = jnp.sum(
        jnp.where(inside, source * SLOT + relative + 1, 0), axis=1, keepdims=True
    )
    origin = origin - 1
    filled = origin >= 0
    position = jnp.where(filled, lax.rem(origin, SLOT), 0)
    wide = lax.broadcasted_iota(jnp.int32, (rows, rows), 1)
    place[...] = jnp.where(wide == origin, 1.0, 0.0).astype(BF)

    for block, (first, size, window) in enumerate(row_blocks(rows)):
        width = mask.shape[2]
        across = first + lax.rem(lax.broadcasted_iota(jnp.int32, (dp_count, width), 1), size)
        relative = across - offset
        inside = (relative >= 0) & (relative < length)
        reach = jnp.sum(jnp.where(inside, relative + 1, 0), axis=0, keepdims=True)
        row = across[0:1]
        seen = window - SLOT + lax.broadcasted_iota(jnp.int32, (HD, width), 0)
        visible = (seen > row - reach) & (seen <= row)
        mask[block] = jnp.where(visible, 1.0, 0.0)
        empty[block] = jnp.where(reach > 0, 0.0, 1.0)
    return count, position


def attend_kernel(
    lengths_ref,
    keep_ref,
    dest_ref,
    offsets_ref,
    got_ref,
    weight_ref,
    query_ref,
    upstream_ref,
    ratio_ref,
    cos_table_ref,
    sin_table_ref,
    out_ref,
    kv_grad_ref,
    rows_buf,
    weight_buf,
    adv_buf,
    sems,
    acc_ref,
    kv_ref,
    kv_pad,
    key_grad,
    value_grad,
    coef_ref,
    place_ref,
    mask_ref,
    empty_ref,
    cos_ref,
    sin_ref,
):
    step = pl.program_id(0)
    rows = query_ref.shape[0]
    kv_width = acc_ref.shape[1] // 2
    depth = rows_buf.shape[2]

    def arrival(k):
        here = pl.ds(pl.multiple_of(k * depth, depth), depth)
        return (
            pltpu.make_async_copy(got_ref.at[:, here], rows_buf.at[k], sems.at[0, k]),
            pltpu.make_async_copy(weight_ref.at[here, :], weight_buf.at[k], sems.at[1, k]),
        )

    def adv_arrival():
        here = pl.ds(RING * depth, LANES)
        return pltpu.make_async_copy(got_ref.at[:, here], adv_buf, sems.at[0, RING])

    @pl.when(step == 0)
    def _():
        adv_arrival().start()
        for k in range(AHEAD):
            for copy in arrival(k):
                copy.start()

    @pl.when(step == 0)
    def _():
        count, position = place_rows(
            lengths_ref, keep_ref, dest_ref, offsets_ref, place_ref, mask_ref, empty_ref
        )
        at = lax.broadcasted_iota(jnp.int32, (rows, HD), 1) == position
        at = jnp.where(at, 1.0, 0.0)
        exact = lax.Precision.HIGHEST
        cos_ref[...] = jnp.dot(
            at, cos_table_ref[...], preferred_element_type=F32, precision=exact
        )
        sin_ref[...] = jnp.dot(
            at, sin_table_ref[...], preferred_element_type=F32, precision=exact
        )
        adv_arrival().wait()
        adv = jnp.dot(place_ref[...], adv_buf[...], preferred_element_type=F32)
        ratio = column_of(ratio_ref)
        clipped = (adv > 0) & (ratio > clip_high) | (adv < 0) & (ratio < clip_low)
        coef_ref[...] = jnp.where(clipped, 0.0, -loss_scale * adv * ratio) / count

    @pl.when(step < RING)
    def _():
        for copy in arrival(step):
            copy.wait()

        @pl.when(step + AHEAD < RING)
        def _():
            for copy in arrival(step + AHEAD):
                copy.start()

        part = jnp.dot(rows_buf[step], weight_buf[step], preferred_element_type=F32)

        @pl.when(step == 0)
        def _():
            acc_ref[...] = part

        @pl.when(step > 0)
        def _():
            acc_ref[...] += part

    @pl.when(step == RING - 1)
    def _():
        for slot in range(rows // SLOT):
            here = pl.ds(slot * SLOT, SLOT)
            cosine = cos_table_ref[pl.ds(0, SLOT), :]
            sine = sin_table_ref[pl.ds(0, SLOT), :]
            for head in range(kv_width // HD):
                columns = pl.ds(head * HD, HD)
                key = acc_ref[here, columns]
                turned = key * cosine + pltpu.roll(key, HD // 2, 1) * sine
                kv_ref[here, columns] = turned.astype(BF)
            values = pl.ds(kv_width, kv_width)
            kv_ref[here, values] = acc_ref[here, values].astype(BF)
        kv_pad[pl.ds(0, SLOT), :] = jnp.zeros((SLOT, 2 * kv_width), BF)
        kv_pad[pl.ds(SLOT, rows), :] = jnp.dot(
            place_ref[...], kv_ref[...], preferred_element_type=F32
        ).astype(BF)

    @pl.when(step >= RING)
    def _():
        attend_head(
            step - RING,
            query_ref,
            upstream_ref,
            out_ref,
            kv_grad_ref,
            kv_pad,
            key_grad,
            value_grad,
            coef_ref,
            place_ref,
            mask_ref,
            empty_ref,
            cos_ref,
            sin_ref,
        )


def attend_head(
    head,
    query_ref,
    upstream_ref,
    out_ref,
    kv_grad_ref,
    kv_pad,
    key_grad,
    value_grad,
    coef_ref,
    place_ref,
    mask_ref,
    empty_ref,
    cos_ref,
    sin_ref,
):
    rows = query_ref.shape[0]
    group = query_ref.shape[1] // HD
    kv_width = kv_pad.shape[1] // 2
    scale = 1.0 / math.sqrt(HD)
    body = pl.ds(SLOT, rows)
    key_columns = pl.ds(pl.multiple_of(head * HD, HD), HD)
    value_columns = pl.ds(pl.multiple_of(kv_width + head * HD, HD), HD)
    across = (((1,), (1,)), ((), ()))
    along = (((0,), (0,)), ((), ()))
    key_grad[...] = jnp.zeros_like(key_grad)
    value_grad[...] = jnp.zeros_like(value_grad)
    for block, (first, size, window) in enumerate(row_blocks(rows)):
        here = pl.ds(first, size)
        span = pl.ds(window, HD)
        coef = coef_ref[here, :]
        many = pl.ds(0, group * size)
        allowed = mask_ref[block, :, many] > 0.0
        empty = empty_ref[block, :, many]
        query = jnp.concatenate(
            [query_ref[here, pl.ds(g * HD, HD)] for g in range(group)], axis=0
        )
        grad = jnp.concatenate(
            [
                (coef * upstream_ref[here, pl.ds(g * HD, HD)].astype(F32)).astype(BF)
                for g in range(group)
            ],
            axis=0,
        )
        key = kv_pad[span, key_columns]
        value = kv_pad[span, value_columns]
        scores = lax.dot_general(key, query, across, preferred_element_type=F32) * scale
        raw = jnp.where(allowed, jnp.exp(scores), 0.0)
        normed = raw * (1.0 / (jnp.sum(raw, axis=0, keepdims=True) + empty))
        normed_low = normed.astype(BF)
        output = lax.dot_general(normed_low, value, along, preferred_element_type=F32).astype(BF)
        for g in range(group):
            out_ref[here, pl.ds(g * HD, HD)] = output[g * size : (g + 1) * size]
        grad_normed = lax.dot_general(value, grad, across, preferred_element_type=F32)
        delta = jnp.sum(normed * grad_normed, axis=0, keepdims=True)
        grad_scores = (normed * (grad_normed - delta) * scale).astype(BF)
        key_grad[span, :] += jnp.dot(grad_scores, query, preferred_element_type=F32)
        value_grad[span, :] += jnp.dot(normed_low, grad, preferred_element_type=F32)
    turned = key_grad[body, :]
    key_back = turned * cos_ref[...] - pltpu.roll(turned, HD // 2, 1) * sin_ref[...]
    both = jnp.concatenate([key_back.astype(BF), value_grad[body, :].astype(BF)], axis=1)
    kv_grad_ref[...] = lax.dot_general(
        both, place_ref[...], along, preferred_element_type=F32
    ).astype(BF)


def attend(plan, got, weights, queries, upstream, ratios):
    rows = got.shape[0]
    width, kv_columns = weights.shape
    heads = kv_columns // (2 * HD)
    query_width = queries.shape[1] // heads
    depth = width // RING
    blocks, most = len(row_blocks(rows)), HD - SLOT
    anywhere = pl.BlockSpec(memory_space=pl.ANY)
    tables = [jnp.asarray(table) for table in slot_tables(HD)]
    whole = lambda array: pl.BlockSpec(array.shape, lambda k: (0,) * array.ndim)
    late = lambda k: jnp.maximum(k - RING, 0)
    return pl.pallas_call(
        attend_kernel,
        grid=(RING + heads,),
        in_specs=[whole(array) for array in plan]
        + [
            anywhere,
            anywhere,
            pl.BlockSpec((rows, query_width), lambda k: (0, late(k))),
            pl.BlockSpec((rows, query_width), lambda k: (0, late(k))),
            whole(ratios),
            whole(tables[0]),
            whole(tables[1]),
        ],
        out_specs=[
            pl.BlockSpec((rows, query_width), lambda k: (0, late(k))),
            pl.BlockSpec((2 * HD, rows), lambda k: (late(k), 0)),
        ],
        out_shape=[
            jax.ShapeDtypeStruct(queries.shape, BF),
            jax.ShapeDtypeStruct((kv_columns, rows), BF),
        ],
        scratch_shapes=[
            pltpu.VMEM((RING, rows, depth), BF),
            pltpu.VMEM((RING, depth, kv_columns), BF),
            pltpu.VMEM((rows, LANES), BF),
            pltpu.SemaphoreType.DMA((2, RING + 1)),
            pltpu.VMEM((rows, kv_columns), F32),
            pltpu.VMEM((rows, kv_columns), BF),
            pltpu.VMEM((rows + SLOT, kv_columns), BF),
            pltpu.VMEM((rows + SLOT, HD), F32),
            pltpu.VMEM((rows + SLOT, HD), F32),
            pltpu.VMEM((rows, LANES), F32),
            pltpu.VMEM((rows, rows), BF),
            pltpu.VMEM((blocks, HD, query_width // HD * most), F32),
            pltpu.VMEM((blocks, 1, query_width // HD * most), F32),
            pltpu.VMEM((rows, HD), F32),
            pltpu.VMEM((rows, HD), F32),
        ],
        compiler_params=params(),
        cost_estimate=cost(
            2 * rows * width * kv_columns + 10 * rows * queries.shape[1] * HD,
            rows * width + width * kv_columns + 3 * rows * queries.shape[1],
        ),
    )(*plan, got, weights, queries, upstream, ratios, *tables)


def grad_kernel(
    own_ref,
    other_ref,
    got_ref,
    sibling_ref,
    first_ref,
    rest_ref,
    own_buf,
    other_buf,
    mine_buf,
    sibling_buf,
    first_buf,
    rest_buf,
    sems,
    in_sems,
    out_sems,
):
    piece = mine_buf.shape[2] // 2
    split = first_buf.shape[2]
    blocks = [lax.rem(lax.axis_index("x") + k, RING) for k in range(RING)]
    own = pltpu.make_async_copy(own_ref, own_buf, sems.at[0])
    other = pltpu.make_async_copy(other_ref, other_buf, sems.at[1])

    def arrival(source, target, k, row):
        start = (2 * blocks[k] + lax.axis_index("core")) * piece
        here = pl.ds(pl.multiple_of(start, LANES), piece)
        there = pl.ds((k % 2) * piece, piece)
        return pltpu.make_async_copy(
            source.at[:, here], target.at[k // 2, :, there], in_sems.at[row, k]
        )

    mine = [arrival(got_ref, mine_buf, k, 0) for k in range(RING)]
    sibling = [arrival(sibling_ref, sibling_buf, k, 1) for k in range(RING)]
    early = [own, mine[0], mine[1]]
    late = [[other, sibling[0], sibling[1]], [mine[2], mine[3], sibling[2], sibling[3]]]
    for copy in early + late[0]:
        copy.start()
    for copy in early:
        copy.wait()
    for copy in late[1]:
        copy.start()
    leave = []
    for half in range(2):
        product = jnp.dot(own_buf[...], mine_buf[half], preferred_element_type=F32)
        if half == 0:
            for copy in late[0]:
                copy.wait()
        product += jnp.dot(other_buf[...], sibling_buf[half], preferred_element_type=F32)
        product = product.astype(BF)
        for k in (2 * half, 2 * half + 1):
            columns = slice((k % 2) * piece, (k % 2 + 1) * piece)
            first_buf[k] = product[:, columns][:, :split]
            rest_buf[k] = product[:, columns][:, split:].reshape(rest_buf.shape[1:])
            pair = (
                pltpu.make_async_copy(first_buf.at[k], first_ref.at[blocks[k]], out_sems.at[0, k]),
                pltpu.make_async_copy(
                    rest_buf.at[k], rest_ref.at[:, blocks[k]], out_sems.at[1, k]
                ),
            )
            for copy in pair:
                copy.start()
                leave.append(copy)
        if half == 0:
            for copy in late[1]:
                copy.wait()
    for copy in leave:
        copy.wait()


def grad_parts(own, other, got, sibling, width, places):
    columns, rows = own.shape
    piece = width // (2 * RING)
    split = piece // 5 * SPLIT
    size = columns // places
    anywhere = pl.BlockSpec(memory_space=pl.ANY)
    return pl.pallas_call(
        grad_kernel,
        in_specs=[anywhere] * 4,
        out_specs=[anywhere] * 2,
        out_shape=[
            jax.ShapeDtypeStruct((RING, columns, split), BF),
            jax.ShapeDtypeStruct((places, RING, size, piece - split), BF),
        ],
        scratch_shapes=[
            pltpu.VMEM((columns, rows), BF),
            pltpu.VMEM((columns, rows), BF),
            pltpu.VMEM((2, rows, 2 * piece), BF),
            pltpu.VMEM((2, rows, 2 * piece), BF),
            pltpu.VMEM((RING, columns, split), BF),
            pltpu.VMEM((RING, places, size, piece - split), BF),
            pltpu.SemaphoreType.DMA((2,)),
            pltpu.SemaphoreType.DMA((2, RING)),
            pltpu.SemaphoreType.DMA((2, RING)),
        ],
        compiler_params=params(20 * 1024 * 1024),
        cost_estimate=cost(
            4 * rows * columns * RING * piece, RING * piece * (2 * rows + columns)
        ),
    )(own, other, got, sibling)


def sum_places_kernel(parts_ref, *out_refs):
    for k in range(RING):
        block = lax.rem(lax.axis_index("x") + k, RING)
        terms = [parts_ref[place, block].astype(F32) for place in range(parts_ref.shape[0])]
        while len(terms) > 1:
            terms = [terms[i] + terms[i + 1] for i in range(0, len(terms), 2)]
        out_refs[k][...] = terms[0].astype(BF)


def sum_places(parts):
    shape = jax.ShapeDtypeStruct(parts.shape[2:], BF)
    return pl.pallas_call(
        sum_places_kernel,
        out_shape=[shape] * RING,
        compiler_params=params(),
        cost_estimate=cost(0, parts.size),
    )(parts)


def finish_kernel(spread_ref, key_ref, value_ref):
    places, size, _ = spread_ref.shape
    per_head = HD // size
    for i in range(places // per_head):
        rows = [spread_ref[i * per_head + j].astype(F32) for j in range(per_head)]
        out_ref = value_ref if i % 2 else key_ref
        out_ref[:, pl.ds(i // 2 * HD, HD)] = jnp.concatenate(rows, axis=0).T


def finish(spread, kv_width):
    columns = spread.shape[2]
    return pl.pallas_call(
        finish_kernel,
        out_shape=[jax.ShapeDtypeStruct((columns, kv_width), F32)] * 2,
        compiler_params=params(),
        cost_estimate=cost(0, 3 * spread.size),
    )(spread)


def total(parts):
    own, after, opposite, before = [part.astype(F32) for part in parts]
    return (own + opposite) + (after + before)


def shifted(value, k):
    return lax.ppermute(value, "x", [(i, (i + k) % RING) for i in range(RING)])


def exchange(parts):
    far = shifted(parts[2], 2)
    return [parts[0], shifted(parts[1], 1), far, shifted(parts[3], 3)]


def swap_cores(value):
    return lax.ppermute(value, "core", [(0, 1), (1, 0)])


def over_dp(value):
    return lax.all_to_all(value, DP, split_axis=0, concat_axis=0, tiled=True)


def on_device(
    hidden,
    advantages,
    queries,
    upstream,
    ratios,
    key_weight,
    value_weight,
    lengths,
    keep_flags,
    destinations,
    offsets,
):
    dp_count = lengths.shape[0]
    rows_here, model_width = hidden.shape
    kv_width = key_weight.shape[1]
    adv = advantages.reshape(rows_here // LANES, LANES)
    sent, weights = order(destinations, hidden, adv, key_weight, value_weight)
    weights = lax.all_gather(weights, FSDP, axis=0, tiled=True)
    got = over_dp(sent.reshape(dp_count, SLOT, sent.shape[1])).reshape(sent.shape)
    sibling = swap_cores(got)
    plan = (lengths, keep_flags, destinations, offsets)
    ratios = ratios.reshape(rows_here // LANES, LANES)
    attention, own = attend(plan, got, weights, queries, upstream, ratios)
    other = swap_cores(own)

    first, rest = grad_parts(own, other, got, sibling, model_width, dp_count)
    first = lax.psum_scatter(
        first.reshape(-1, first.shape[2]), "x", scatter_dimension=0, tiled=True
    )
    rest = exchange(sum_places(over_dp(rest)))
    first, rest = lax.optimization_barrier((first, rest))
    first = over_dp(first.reshape(dp_count, -1, first.shape[1]))
    summed = jnp.concatenate([jnp.sum(first.astype(F32), axis=0), total(rest)], axis=1)
    spread = over_dp(jnp.broadcast_to(summed.astype(BF)[None], (dp_count,) + summed.shape))
    grad_key, grad_value = finish(spread, kv_width)
    return (attention, grad_key, grad_value)


def solution(mesh):
    chips = {"y": RING, "z": RING, "x": RING, "core": 2}
    fine = Mesh(mesh.devices.reshape(tuple(chips.values())), tuple(chips))
    in_specs = (
        P(ALL, None),
        P(ALL),
        P(ALL, None),
        P(ALL, None),
        P(ALL),
        P(FSDP, None),
        P(FSDP, None),
        P(),
        P(),
        P(),
        P(),
    )
    out_specs = (P(ALL, None), P(FSDP, None), P(FSDP, None))
    return jax.shard_map(
        on_device, mesh=fine, in_specs=in_specs, out_specs=out_specs, check_vma=False
    )
```

```python
import math

import jax
import jax.numpy as jnp
import ml_dtypes
import numpy as np
from jax import lax
from jax.experimental import pallas as pl
from jax.experimental.pallas import tpu as pltpu
from jax.sharding import Mesh
from jax.sharding import PartitionSpec as P

HD = 128
SLOT = 32
RING = 4
SPLIT = 3
VMEM_LIMIT = 56 * 1024 * 1024

rope_base = 1000000.0
loss_scale = 256.0
clip_low = 0.8
clip_high = 1.28

DP = ("y", "z")
FSDP = ("x", "core")
ALL = DP + FSDP
BF = jnp.bfloat16
F32 = jnp.float32
LANES = 128
DEPTH_BLOCKS = 5
AHEAD = 3


def row_blocks(rows):
    step = HD - SLOT
    blocks = []
    for first in range(0, rows, step):
        size = min(step, rows - first)
        blocks.append((first, size, min(first, rows + SLOT - HD)))
    return blocks


def slot_tables():
    frequency = rope_base ** (-(np.arange(HD // 2) * (2.0 / HD)))
    angle = np.arange(SLOT)[:, None] * frequency[None, :]
    cosine, sine = np.cos(angle), np.sin(angle)
    return (
        np.concatenate([cosine, cosine], axis=1).astype(np.float32),
        np.concatenate([-sine, sine], axis=1).astype(np.float32),
    )


def lookup_tables():
    terms = []
    for table in slot_tables():
        left = table
        for _ in range(3):
            term = left.astype(ml_dtypes.bfloat16)
            left = left - term.astype(np.float32)
            terms.append(term)
    return np.pad(np.concatenate(terms, axis=1), ((0, HD - SLOT), (0, 0)))


def params(limit=VMEM_LIMIT):
    return pltpu.CompilerParams(vmem_limit_bytes=limit)


def cost(flops, count):
    return pl.CostEstimate(flops=int(flops), bytes_accessed=int(2 * count), transcendentals=0)


def dp_fsdp():
    dp_index = lax.axis_index("y") * RING + lax.axis_index("z")
    return dp_index, lax.axis_index("x") * 2 + lax.axis_index("core")


def column_of(row_ref):
    same = lax.broadcasted_iota(jnp.int32, (LANES, LANES), 0) == lax.broadcasted_iota(
        jnp.int32, (LANES, LANES), 1
    )
    parts = []
    for i in range(row_ref.shape[0]):
        row = row_ref[i : i + 1, :].astype(F32)
        parts.append(jnp.sum(jnp.where(same, row, 0.0), axis=1, keepdims=True))
    return jnp.concatenate(parts, axis=0)


def order_kernel(
    dest_ref,
    hidden_ref,
    adv_ref,
    key_ref,
    value_ref,
    sent_ref,
    weight_ref,
    rows_buf,
    adv_buf,
    weight_buf,
    in_sems,
    out_sems,
    adv_sems,
    weight_sems,
):
    dp_index, group = dp_fsdp()
    width = hidden_ref.shape[1]
    kv_width = key_ref.shape[1]
    slots = hidden_ref.shape[0] // SLOT
    both = [
        pltpu.make_async_copy(
            ref, weight_buf.at[:, pl.ds(i * kv_width, kv_width)], weight_sems.at[i]
        )
        for i, ref in enumerate((key_ref, value_ref))
    ]
    arrive, leave, adv_leave = [], [], []
    for slot in range(slots):
        here = pl.ds(slot * SLOT, SLOT)
        there = pl.ds(pl.multiple_of(dest_ref[dp_index, group, slot] * SLOT, SLOT), SLOT)
        arrive.append(
            pltpu.make_async_copy(hidden_ref.at[here, :], rows_buf.at[slot], in_sems.at[slot])
        )
        leave.append(
            pltpu.make_async_copy(
                rows_buf.at[slot], sent_ref.at[there, pl.ds(0, width)], out_sems.at[slot]
            )
        )
        adv_leave.append(
            pltpu.make_async_copy(
                adv_buf.at[here, :], sent_ref.at[there, pl.ds(width, LANES)], adv_sems.at[slot]
            )
        )
    for copy in both + arrive:
        copy.start()
    adv_buf[...] = jnp.broadcast_to(column_of(adv_ref), adv_buf.shape).astype(BF)
    for copy in adv_leave:
        copy.start()
    for copy in both:
        copy.wait()
    out = pltpu.make_async_copy(weight_buf, weight_ref, weight_sems.at[2])
    out.start()
    for slot in range(slots):
        arrive[slot].wait()
        leave[slot].start()
    out.wait()
    for copy in adv_leave + leave:
        copy.wait()


def order(destinations, hidden, adv, key_weight, value_weight):
    rows, width = hidden.shape
    depth, kv_width = key_weight.shape
    slots = rows // SLOT
    anywhere = pl.BlockSpec(memory_space=pl.ANY)
    return pl.pallas_call(
        order_kernel,
        in_specs=[
            pl.BlockSpec(memory_space=pltpu.SMEM),
            anywhere,
            pl.BlockSpec(memory_space=pltpu.VMEM),
            anywhere,
            anywhere,
        ],
        out_specs=[anywhere] * 2,
        out_shape=[
            jax.ShapeDtypeStruct((rows, width + LANES), BF),
            jax.ShapeDtypeStruct((depth, 2 * kv_width), BF),
        ],
        scratch_shapes=[
            pltpu.VMEM((slots, SLOT, width), BF),
            pltpu.VMEM((rows, LANES), BF),
            pltpu.VMEM((depth, 2 * kv_width), BF),
            pltpu.SemaphoreType.DMA((slots,)),
            pltpu.SemaphoreType.DMA((slots,)),
            pltpu.SemaphoreType.DMA((slots,)),
            pltpu.SemaphoreType.DMA((3,)),
        ],
        compiler_params=params(),
        cost_estimate=cost(0, 2 * rows * width),
    )(destinations, hidden, adv, key_weight, value_weight)


def place_rows(lengths_ref, keep_ref, dest_ref, offsets_ref, place, mask, empty):
    rows = place.shape[0]
    dp_count, fsdp_count, slots = lengths_ref.shape
    dp_index, group = dp_fsdp()

    def of_group(ref):
        picked = lax.broadcasted_iota(jnp.int32, (dp_count, fsdp_count, slots), 1) == group
        return jnp.sum(jnp.where(picked, ref[...], 0), axis=1)

    keep = keep_ref[...]
    same = lax.broadcasted_iota(jnp.int32, (dp_count, dp_count), 0) == lax.broadcasted_iota(
        jnp.int32, (dp_count, dp_count), 1
    )
    picked = lax.broadcasted_iota(jnp.int32, keep.shape, 0) == group
    keep_row = jnp.sum(jnp.where(picked, keep, 0), axis=0, keepdims=True)
    keep_column = jnp.sum(jnp.where(same, keep_row, 0), axis=1, keepdims=True)
    kept = lengths_ref[0] * keep[:, 0:1]
    for source in range(1, dp_count):
        kept += lengths_ref[source] * keep[:, source : source + 1]
    count = jnp.sum(kept.astype(F32))
    kept = of_group(lengths_ref) * keep_column
    incoming = (of_group(dest_ref) == dp_index) & (kept > 0)
    offset = jnp.sum(jnp.where(incoming, of_group(offsets_ref), 0), axis=1, keepdims=True)
    length = jnp.sum(jnp.where(incoming, kept, 0), axis=1, keepdims=True)

    offset_row = jnp.sum(jnp.where(same, offset, 0), axis=0, keepdims=True)
    length_row = jnp.sum(jnp.where(same, length, 0), axis=0, keepdims=True)
    source = lax.broadcasted_iota(jnp.int32, (rows, dp_count), 1)
    relative = lax.broadcasted_iota(jnp.int32, (rows, dp_count), 0) - offset_row
    inside = (relative >= 0) & (relative < length_row)
    origin = jnp.sum(
        jnp.where(inside, source * SLOT + relative + 1, 0), axis=1, keepdims=True
    )
    origin = origin - 1
    filled = origin >= 0
    position = jnp.where(filled, lax.rem(origin, SLOT), 0)
    wide = lax.broadcasted_iota(jnp.int32, (rows, rows), 1)
    place[...] = jnp.where(wide == origin, 1.0, 0.0).astype(BF)

    for block, (first, size, window) in enumerate(row_blocks(rows)):
        width = mask.shape[2]
        across = first + lax.rem(lax.broadcasted_iota(jnp.int32, (dp_count, width), 1), size)
        relative = across - offset
        inside = (relative >= 0) & (relative < length)
        reach = jnp.sum(jnp.where(inside, relative + 1, 0), axis=0, keepdims=True)
        row = across[0:1]
        seen = window - SLOT + lax.broadcasted_iota(jnp.int32, (HD, width), 0)
        visible = (seen > row - reach) & (seen <= row)
        mask[block] = jnp.where(visible, 1.0, 0.0)
        empty[block] = jnp.where(reach > 0, 0.0, 1.0)
    return count, position


def attend_kernel(
    lengths_ref,
    keep_ref,
    dest_ref,
    offsets_ref,
    got_ref,
    weight_ref,
    query_ref,
    upstream_ref,
    ratio_ref,
    cos_table_ref,
    sin_table_ref,
    tables_ref,
    out_ref,
    kv_grad_ref,
    rows_buf,
    weight_buf,
    adv_buf,
    sems,
    acc_ref,
    kv_ref,
    kv_pad,
    key_grad,
    value_grad,
    coef_ref,
    place_ref,
    mask_ref,
    empty_ref,
    cos_ref,
    sin_ref,
):
    head = pl.program_id(0)
    rows = query_ref.shape[0]
    kv_width = acc_ref.shape[1] // 2
    blocks, _, depth = rows_buf.shape

    def arrival(k):
        here = pl.ds(pl.multiple_of(k * depth, depth), depth)
        return (
            pltpu.make_async_copy(got_ref.at[:, here], rows_buf.at[k], sems.at[0, k]),
            pltpu.make_async_copy(weight_ref.at[here, :], weight_buf.at[k], sems.at[1, k]),
        )

    def adv_arrival():
        here = pl.ds(blocks * depth, LANES)
        return pltpu.make_async_copy(got_ref.at[:, here], adv_buf, sems.at[0, blocks])

    @pl.when(head == 0)
    def _():
        adv_arrival().start()
        for k in range(AHEAD):
            for copy in arrival(k):
                copy.start()

    @pl.when(head == 0)
    def _():
        count, position = place_rows(
            lengths_ref, keep_ref, dest_ref, offsets_ref, place_ref, mask_ref, empty_ref
        )
        at = lax.broadcasted_iota(jnp.int32, (rows, HD), 1) == position
        at = jnp.where(at, 1.0, 0.0).astype(BF)
        looked_up = jnp.dot(at, tables_ref[...], preferred_element_type=F32)
        for ref, first in ((cos_ref, 0), (sin_ref, 3 * HD)):
            parts = [looked_up[:, first + i * HD : first + (i + 1) * HD] for i in range(3)]
            ref[...] = parts[0] + (parts[1] + parts[2])
        adv_arrival().wait()
        adv = jnp.dot(place_ref[...], adv_buf[...], preferred_element_type=F32)
        ratio = column_of(ratio_ref)
        clipped = (adv > 0) & (ratio > clip_high) | (adv < 0) & (ratio < clip_low)
        coef_ref[...] = jnp.where(clipped, 0.0, adv * ratio) * (-loss_scale / count)

    @pl.when(head == 0)
    def _():
        acc_ref[...] = jnp.zeros_like(acc_ref)

        @pl.loop(0, blocks)
        def _(k):
            for copy in arrival(k):
                copy.wait()

            @pl.when(k + AHEAD < blocks)
            def _():
                for copy in arrival(k + AHEAD):
                    copy.start()

            acc_ref[...] += jnp.dot(rows_buf[k], weight_buf[k], preferred_element_type=F32)

        for slot in range(rows // SLOT):
            here = pl.ds(slot * SLOT, SLOT)
            cosine, sine = cos_table_ref[...], sin_table_ref[...]
            for head in range(kv_width // HD):
                columns = pl.ds(head * HD, HD)
                key = acc_ref[here, columns]
                turned = key * cosine + pltpu.roll(key, HD // 2, 1) * sine
                kv_ref[here, columns] = turned.astype(BF)
            values = pl.ds(kv_width, kv_width)
            kv_ref[here, values] = acc_ref[here, values].astype(BF)
        kv_pad[pl.ds(0, SLOT), :] = jnp.zeros((SLOT, 2 * kv_width), BF)
        kv_pad[pl.ds(SLOT, rows), :] = jnp.dot(
            place_ref[...], kv_ref[...], preferred_element_type=F32
        ).astype(BF)

    attend_head(
        head,
        query_ref,
        upstream_ref,
        out_ref,
        kv_grad_ref,
        kv_pad,
        key_grad,
        value_grad,
        coef_ref,
        place_ref,
        mask_ref,
        empty_ref,
        cos_ref,
        sin_ref,
    )


def attend_head(
    head,
    query_ref,
    upstream_ref,
    out_ref,
    kv_grad_ref,
    kv_pad,
    key_grad,
    value_grad,
    coef_ref,
    place_ref,
    mask_ref,
    empty_ref,
    cos_ref,
    sin_ref,
):
    rows = query_ref.shape[0]
    group = query_ref.shape[1] // HD
    kv_width = kv_pad.shape[1] // 2
    scale = 1.0 / math.sqrt(HD)
    body = pl.ds(SLOT, rows)
    key_columns = pl.ds(pl.multiple_of(head * HD, HD), HD)
    value_columns = pl.ds(pl.multiple_of(kv_width + head * HD, HD), HD)
    across = (((1,), (1,)), ((), ()))
    along = (((0,), (0,)), ((), ()))
    key_grad[...] = jnp.zeros_like(key_grad)
    value_grad[...] = jnp.zeros_like(value_grad)
    for block, (first, size, window) in enumerate(row_blocks(rows)):
        here = pl.ds(first, size)
        span = pl.ds(window, HD)
        coef = coef_ref[here, :]
        many = pl.ds(0, group * size)
        allowed = mask_ref[block, :, many] > 0.0
        empty = empty_ref[block, :, many]
        query = jnp.concatenate(
            [query_ref[here, pl.ds(g * HD, HD)] for g in range(group)], axis=0
        )
        grad = jnp.concatenate(
            [
                (coef * upstream_ref[here, pl.ds(g * HD, HD)].astype(F32)).astype(BF)
                for g in range(group)
            ],
            axis=0,
        )
        key = kv_pad[span, key_columns]
        value = kv_pad[span, value_columns]
        scores = lax.dot_general(key, query, across, preferred_element_type=F32) * scale
        raw = jnp.where(allowed, jnp.exp(scores), 0.0)
        normed = raw * (1.0 / (jnp.sum(raw, axis=0, keepdims=True) + empty))
        normed_low = normed.astype(BF)
        output = lax.dot_general(normed_low, value, along, preferred_element_type=F32).astype(BF)
        for g in range(group):
            out_ref[here, pl.ds(g * HD, HD)] = output[g * size : (g + 1) * size]
        grad_normed = lax.dot_general(value, grad, across, preferred_element_type=F32)
        delta = jnp.sum(normed * grad_normed, axis=0, keepdims=True)
        grad_scores = (normed * (grad_normed - delta) * scale).astype(BF)
        key_grad[span, :] += jnp.dot(grad_scores, query, preferred_element_type=F32)
        value_grad[span, :] += jnp.dot(normed_low, grad, preferred_element_type=F32)
    turned = key_grad[body, :]
    key_back = turned * cos_ref[...] - pltpu.roll(turned, HD // 2, 1) * sin_ref[...]
    both = jnp.concatenate([key_back.astype(BF), value_grad[body, :].astype(BF)], axis=1)
    kv_grad_ref[...] = lax.dot_general(
        both, place_ref[...], along, preferred_element_type=F32
    ).astype(BF)


def attend(plan, got, weights, queries, upstream, ratios):
    rows = got.shape[0]
    width, kv_columns = weights.shape
    heads = kv_columns // (2 * HD)
    query_width = queries.shape[1] // heads
    depth = width // DEPTH_BLOCKS
    blocks, most = len(row_blocks(rows)), HD - SLOT
    anywhere = pl.BlockSpec(memory_space=pl.ANY)
    tables = [jnp.asarray(table) for table in slot_tables() + (lookup_tables(),)]
    whole = lambda array: pl.BlockSpec(array.shape, lambda k: (0,) * array.ndim)
    return pl.pallas_call(
        attend_kernel,
        grid=(heads,),
        in_specs=[whole(array) for array in plan]
        + [
            anywhere,
            anywhere,
            pl.BlockSpec((rows, query_width), lambda h: (0, h)),
            pl.BlockSpec((rows, query_width), lambda h: (0, h)),
            whole(ratios),
            whole(tables[0]),
            whole(tables[1]),
            whole(tables[2]),
        ],
        out_specs=[
            pl.BlockSpec((rows, query_width), lambda h: (0, h)),
            pl.BlockSpec((2 * HD, rows), lambda h: (h, 0)),
        ],
        out_shape=[
            jax.ShapeDtypeStruct(queries.shape, BF),
            jax.ShapeDtypeStruct((kv_columns, rows), BF),
        ],
        scratch_shapes=[
            pltpu.VMEM((DEPTH_BLOCKS, rows, depth), BF),
            pltpu.VMEM((DEPTH_BLOCKS, depth, kv_columns), BF),
            pltpu.VMEM((rows, LANES), BF),
            pltpu.SemaphoreType.DMA((2, DEPTH_BLOCKS + 1)),
            pltpu.VMEM((rows, kv_columns), F32),
            pltpu.VMEM((rows, kv_columns), BF),
            pltpu.VMEM((rows + SLOT, kv_columns), BF),
            pltpu.VMEM((rows + SLOT, HD), F32),
            pltpu.VMEM((rows + SLOT, HD), F32),
            pltpu.VMEM((rows, LANES), F32),
            pltpu.VMEM((rows, rows), BF),
            pltpu.VMEM((blocks, HD, query_width // HD * most), F32),
            pltpu.VMEM((blocks, 1, query_width // HD * most), F32),
            pltpu.VMEM((rows, HD), F32),
            pltpu.VMEM((rows, HD), F32),
        ],
        compiler_params=params(),
        cost_estimate=cost(
            2 * rows * width * kv_columns + 10 * rows * queries.shape[1] * HD,
            rows * width + width * kv_columns + 3 * rows * queries.shape[1],
        ),
    )(*plan, got, weights, queries, upstream, ratios, *tables)


def grad_kernel(
    own_ref,
    other_ref,
    got_ref,
    sibling_ref,
    first_ref,
    rest_ref,
    own_buf,
    other_buf,
    mine_buf,
    sibling_buf,
    first_buf,
    rest_buf,
    sems,
    in_sems,
    out_sems,
):
    piece = mine_buf.shape[2] // 2
    split = first_buf.shape[2]
    blocks = [lax.rem(lax.axis_index("x") + k, RING) for k in range(RING)]
    own = pltpu.make_async_copy(own_ref, own_buf, sems.at[0])
    other = pltpu.make_async_copy(other_ref, other_buf, sems.at[1])

    def arrival(source, target, k, row):
        start = (2 * blocks[k] + lax.axis_index("core")) * piece
        here = pl.ds(pl.multiple_of(start, LANES), piece)
        there = pl.ds((k % 2) * piece, piece)
        return pltpu.make_async_copy(
            source.at[:, here], target.at[k // 2, :, there], in_sems.at[row, k]
        )

    mine = [arrival(got_ref, mine_buf, k, 0) for k in range(RING)]
    sibling = [arrival(sibling_ref, sibling_buf, k, 1) for k in range(RING)]
    early = [own, mine[0], mine[1]]
    late = [[other, sibling[0], sibling[1]], [mine[2], mine[3], sibling[2], sibling[3]]]
    for copy in early + late[0]:
        copy.start()
    for copy in early:
        copy.wait()
    for copy in late[1]:
        copy.start()
    leave = []
    for half in range(2):
        product = jnp.dot(own_buf[...], mine_buf[half], preferred_element_type=F32)
        if half == 0:
            for copy in late[0]:
                copy.wait()
        product += jnp.dot(other_buf[...], sibling_buf[half], preferred_element_type=F32)
        product = product.astype(BF)
        for k in (2 * half, 2 * half + 1):
            columns = slice((k % 2) * piece, (k % 2 + 1) * piece)
            first_buf[k] = product[:, columns][:, :split]
            rest_buf[k] = product[:, columns][:, split:].reshape(rest_buf.shape[1:])
            pair = (
                pltpu.make_async_copy(first_buf.at[k], first_ref.at[blocks[k]], out_sems.at[0, k]),
                pltpu.make_async_copy(
                    rest_buf.at[k], rest_ref.at[:, blocks[k]], out_sems.at[1, k]
                ),
            )
            for copy in pair:
                copy.start()
                leave.append(copy)
        if half == 0:
            for copy in late[1]:
                copy.wait()
    for copy in leave:
        copy.wait()


def grad_parts(own, other, got, sibling, width, places):
    columns, rows = own.shape
    piece = width // (2 * RING)
    split = piece // 5 * SPLIT
    size = columns // places
    anywhere = pl.BlockSpec(memory_space=pl.ANY)
    return pl.pallas_call(
        grad_kernel,
        in_specs=[anywhere] * 4,
        out_specs=[anywhere] * 2,
        out_shape=[
            jax.ShapeDtypeStruct((RING, columns, split), BF),
            jax.ShapeDtypeStruct((places, RING, size, piece - split), BF),
        ],
        scratch_shapes=[
            pltpu.VMEM((columns, rows), BF),
            pltpu.VMEM((columns, rows), BF),
            pltpu.VMEM((2, rows, 2 * piece), BF),
            pltpu.VMEM((2, rows, 2 * piece), BF),
            pltpu.VMEM((RING, columns, split), BF),
            pltpu.VMEM((RING, places, size, piece - split), BF),
            pltpu.SemaphoreType.DMA((2,)),
            pltpu.SemaphoreType.DMA((2, RING)),
            pltpu.SemaphoreType.DMA((2, RING)),
        ],
        compiler_params=params(20 * 1024 * 1024),
        cost_estimate=cost(
            4 * rows * columns * RING * piece, RING * piece * (2 * rows + columns)
        ),
    )(own, other, got, sibling)


def sum_places_kernel(parts_ref, *out_refs):
    for k in range(RING):
        block = lax.rem(lax.axis_index("x") + k, RING)
        terms = [parts_ref[place, block].astype(F32) for place in range(parts_ref.shape[0])]
        while len(terms) > 1:
            terms = [terms[i] + terms[i + 1] for i in range(0, len(terms), 2)]
        out_refs[k][...] = terms[0].astype(BF)


def sum_places(parts):
    shape = jax.ShapeDtypeStruct(parts.shape[2:], BF)
    return pl.pallas_call(
        sum_places_kernel,
        out_shape=[shape] * RING,
        compiler_params=params(),
        cost_estimate=cost(0, parts.size),
    )(parts)


def finish_kernel(spread_ref, key_ref, value_ref):
    places, size, _ = spread_ref.shape
    per_head = HD // size
    for i in range(places // per_head):
        rows = [spread_ref[i * per_head + j].astype(F32) for j in range(per_head)]
        out_ref = value_ref if i % 2 else key_ref
        out_ref[:, pl.ds(i // 2 * HD, HD)] = jnp.concatenate(rows, axis=0).T


def finish(spread, kv_width):
    columns = spread.shape[2]
    return pl.pallas_call(
        finish_kernel,
        out_shape=[jax.ShapeDtypeStruct((columns, kv_width), F32)] * 2,
        compiler_params=params(),
        cost_estimate=cost(0, 3 * spread.size),
    )(spread)


def total(parts):
    own, after, opposite, before = [part.astype(F32) for part in parts]
    return (own + opposite) + (after + before)


def shifted(value, k):
    return lax.ppermute(value, "x", [(i, (i + k) % RING) for i in range(RING)])


def exchange(parts):
    far = shifted(parts[2], 2)
    return [parts[0], shifted(parts[1], 1), far, shifted(parts[3], 3)]


def swap_cores(value):
    return lax.ppermute(value, "core", [(0, 1), (1, 0)])


def over_dp(value):
    return lax.all_to_all(value, DP, split_axis=0, concat_axis=0, tiled=True)


def on_device(
    hidden,
    advantages,
    queries,
    upstream,
    ratios,
    key_weight,
    value_weight,
    lengths,
    keep_flags,
    destinations,
    offsets,
):
    dp_count = lengths.shape[0]
    rows_here, model_width = hidden.shape
    kv_width = key_weight.shape[1]
    adv = advantages.reshape(rows_here // LANES, LANES)
    sent, weights = order(destinations, hidden, adv, key_weight, value_weight)
    weights = lax.all_gather(weights, FSDP, axis=0, tiled=True)
    got = over_dp(sent.reshape(dp_count, SLOT, sent.shape[1])).reshape(sent.shape)
    sibling = swap_cores(got)
    plan = (lengths, keep_flags, destinations, offsets)
    ratios = ratios.reshape(rows_here // LANES, LANES)
    attention, own = attend(plan, got, weights, queries, upstream, ratios)
    other = swap_cores(own)

    first, rest = grad_parts(own, other, got, sibling, model_width, dp_count)
    first = lax.psum_scatter(
        first.reshape(-1, first.shape[2]), "x", scatter_dimension=0, tiled=True
    )
    rest = sum_places(over_dp(rest))
    first, rest = lax.optimization_barrier((first, rest))
    rest = exchange(rest)
    first = over_dp(first.reshape(dp_count, -1, first.shape[1]))
    summed = jnp.concatenate([jnp.sum(first.astype(F32), axis=0), total(rest)], axis=1)
    spread = over_dp(jnp.broadcast_to(summed.astype(BF)[None], (dp_count,) + summed.shape))
    grad_key, grad_value = finish(spread, kv_width)
    return (attention, grad_key, grad_value)


def solution(mesh):
    chips = {"y": RING, "z": RING, "x": RING, "core": 2}
    fine = Mesh(mesh.devices.reshape(tuple(chips.values())), tuple(chips))
    in_specs = (
        P(ALL, None),
        P(ALL),
        P(ALL, None),
        P(ALL, None),
        P(ALL),
        P(FSDP, None),
        P(FSDP, None),
        P(),
        P(),
        P(),
        P(),
    )
    out_specs = (P(ALL, None), P(FSDP, None), P(FSDP, None))
    return jax.shard_map(
        on_device, mesh=fine, in_specs=in_specs, out_specs=out_specs, check_vma=False
    )
```

```python
import math

import jax
import jax.numpy as jnp
import ml_dtypes
import numpy as np
from jax import lax
from jax.experimental import pallas as pl
from jax.experimental.pallas import tpu as pltpu
from jax.sharding import Mesh
from jax.sharding import PartitionSpec as P

HD = 128
SLOT = 32
RING = 4
ROW_PARTS = 2
WINDOW = 160
SPLIT = 3
VMEM_LIMIT = 56 * 1024 * 1024

rope_base = 1000000.0
loss_scale = 256.0
clip_low = 0.8
clip_high = 1.28

DP = ("y", "z")
FSDP = ("x", "core")
ALL = DP + FSDP
BF = jnp.bfloat16
F32 = jnp.float32
LANES = 128
DEPTH_BLOCKS = 5
AHEAD = 3


def row_blocks(rows):
    step = WINDOW - SLOT
    blocks = []
    for first in range(0, rows, step):
        size = min(step, rows - first)
        blocks.append((first, size, min(first, rows + SLOT - WINDOW)))
    return blocks


def slot_tables():
    frequency = rope_base ** (-(np.arange(HD // 2) * (2.0 / HD)))
    angle = np.arange(SLOT)[:, None] * frequency[None, :]
    cosine, sine = np.cos(angle), np.sin(angle)
    return (
        np.concatenate([cosine, cosine], axis=1).astype(np.float32),
        np.concatenate([-sine, sine], axis=1).astype(np.float32),
    )


def lookup_tables():
    terms = []
    for table in slot_tables():
        left = table
        for _ in range(3):
            term = left.astype(ml_dtypes.bfloat16)
            left = left - term.astype(np.float32)
            terms.append(term)
    return np.pad(np.concatenate(terms, axis=1), ((0, HD - SLOT), (0, 0)))


def params(limit=VMEM_LIMIT):
    return pltpu.CompilerParams(vmem_limit_bytes=limit)


def cost(flops, count):
    return pl.CostEstimate(flops=int(flops), bytes_accessed=int(2 * count), transcendentals=0)


def dp_fsdp():
    dp_index = lax.axis_index("y") * RING + lax.axis_index("z")
    return dp_index, lax.axis_index("x") * 2 + lax.axis_index("core")


def column_of(row_ref):
    same = lax.broadcasted_iota(jnp.int32, (LANES, LANES), 0) == lax.broadcasted_iota(
        jnp.int32, (LANES, LANES), 1
    )
    parts = []
    for i in range(row_ref.shape[0]):
        row = row_ref[i : i + 1, :].astype(F32)
        parts.append(jnp.sum(jnp.where(same, row, 0.0), axis=1, keepdims=True))
    return jnp.concatenate(parts, axis=0)


def order_kernel(
    dest_ref,
    hidden_ref,
    adv_ref,
    key_ref,
    value_ref,
    sent_ref,
    weight_ref,
    rows_buf,
    adv_buf,
    weight_buf,
    in_sems,
    out_sems,
    adv_sems,
    weight_sems,
):
    dp_index, group = dp_fsdp()
    width = hidden_ref.shape[1]
    kv_width = key_ref.shape[1]
    slots = hidden_ref.shape[0] // SLOT
    both = [
        pltpu.make_async_copy(
            ref, weight_buf.at[:, pl.ds(i * kv_width, kv_width)], weight_sems.at[i]
        )
        for i, ref in enumerate((key_ref, value_ref))
    ]
    arrive, leave, adv_leave = [], [], []
    for slot in range(slots):
        here = pl.ds(slot * SLOT, SLOT)
        there = pl.ds(pl.multiple_of(dest_ref[dp_index, group, slot] * SLOT, SLOT), SLOT)
        arrive.append(
            pltpu.make_async_copy(hidden_ref.at[here, :], rows_buf.at[slot], in_sems.at[slot])
        )
        leave.append(
            pltpu.make_async_copy(
                rows_buf.at[slot], sent_ref.at[there, pl.ds(0, width)], out_sems.at[slot]
            )
        )
        adv_leave.append(
            pltpu.make_async_copy(
                adv_buf.at[here, :], sent_ref.at[there, pl.ds(width, LANES)], adv_sems.at[slot]
            )
        )
    for copy in both + arrive:
        copy.start()
    adv_buf[...] = jnp.broadcast_to(column_of(adv_ref), adv_buf.shape).astype(BF)
    for copy in adv_leave:
        copy.start()
    for copy in both:
        copy.wait()
    out = pltpu.make_async_copy(weight_buf, weight_ref, weight_sems.at[2])
    out.start()
    for slot in range(slots):
        arrive[slot].wait()
        leave[slot].start()
    out.wait()
    for copy in adv_leave + leave:
        copy.wait()


def order(destinations, hidden, adv, key_weight, value_weight):
    rows, width = hidden.shape
    depth, kv_width = key_weight.shape
    slots = rows // SLOT
    anywhere = pl.BlockSpec(memory_space=pl.ANY)
    return pl.pallas_call(
        order_kernel,
        in_specs=[
            pl.BlockSpec(memory_space=pltpu.SMEM),
            anywhere,
            pl.BlockSpec(memory_space=pltpu.VMEM),
            anywhere,
            anywhere,
        ],
        out_specs=[anywhere] * 2,
        out_shape=[
            jax.ShapeDtypeStruct((rows, width + LANES), BF),
            jax.ShapeDtypeStruct((depth, 2 * kv_width), BF),
        ],
        scratch_shapes=[
            pltpu.VMEM((slots, SLOT, width), BF),
            pltpu.VMEM((rows, LANES), BF),
            pltpu.VMEM((depth, 2 * kv_width), BF),
            pltpu.SemaphoreType.DMA((slots,)),
            pltpu.SemaphoreType.DMA((slots,)),
            pltpu.SemaphoreType.DMA((slots,)),
            pltpu.SemaphoreType.DMA((3,)),
        ],
        compiler_params=params(),
        cost_estimate=cost(0, 2 * rows * width),
    )(destinations, hidden, adv, key_weight, value_weight)


def place_rows(lengths_ref, keep_ref, dest_ref, offsets_ref, place, mask, empty):
    rows = place.shape[0]
    dp_count, fsdp_count, slots = lengths_ref.shape
    dp_index, group = dp_fsdp()

    def of_group(ref):
        picked = lax.broadcasted_iota(jnp.int32, (dp_count, fsdp_count, slots), 1) == group
        return jnp.sum(jnp.where(picked, ref[...], 0), axis=1)

    keep = keep_ref[...]
    same = lax.broadcasted_iota(jnp.int32, (dp_count, dp_count), 0) == lax.broadcasted_iota(
        jnp.int32, (dp_count, dp_count), 1
    )
    picked = lax.broadcasted_iota(jnp.int32, keep.shape, 0) == group
    keep_row = jnp.sum(jnp.where(picked, keep, 0), axis=0, keepdims=True)
    keep_column = jnp.sum(jnp.where(same, keep_row, 0), axis=1, keepdims=True)
    kept = lengths_ref[0] * keep[:, 0:1]
    for source in range(1, dp_count):
        kept += lengths_ref[source] * keep[:, source : source + 1]
    count = jnp.sum(kept.astype(F32))
    kept = of_group(lengths_ref) * keep_column
    incoming = (of_group(dest_ref) == dp_index) & (kept > 0)
    offset = jnp.sum(jnp.where(incoming, of_group(offsets_ref), 0), axis=1, keepdims=True)
    length = jnp.sum(jnp.where(incoming, kept, 0), axis=1, keepdims=True)

    offset_row = jnp.sum(jnp.where(same, offset, 0), axis=0, keepdims=True)
    length_row = jnp.sum(jnp.where(same, length, 0), axis=0, keepdims=True)
    source = lax.broadcasted_iota(jnp.int32, (rows, dp_count), 1)
    relative = lax.broadcasted_iota(jnp.int32, (rows, dp_count), 0) - offset_row
    inside = (relative >= 0) & (relative < length_row)
    origin = jnp.sum(
        jnp.where(inside, source * SLOT + relative + 1, 0), axis=1, keepdims=True
    )
    origin = origin - 1
    filled = origin >= 0
    position = jnp.where(filled, lax.rem(origin, SLOT), 0)
    wide = lax.broadcasted_iota(jnp.int32, (rows, rows), 1)
    place[...] = jnp.where(wide == origin, 1.0, 0.0).astype(BF)

    for block, (first, size, window) in enumerate(row_blocks(rows)):
        width = mask.shape[2]
        across = first + lax.rem(lax.broadcasted_iota(jnp.int32, (dp_count, width), 1), size)
        relative = across - offset
        inside = (relative >= 0) & (relative < length)
        reach = jnp.sum(jnp.where(inside, relative + 1, 0), axis=0, keepdims=True)
        row = across[0:1]
        seen = window - SLOT + lax.broadcasted_iota(jnp.int32, (WINDOW, width), 0)
        visible = (seen > row - reach) & (seen <= row)
        mask[block] = jnp.where(visible, 1.0, 0.0)
        empty[block] = jnp.where(reach > 0, 0.0, 1.0)
    return count, position


def attend_kernel(
    lengths_ref,
    keep_ref,
    dest_ref,
    offsets_ref,
    got_ref,
    weight_ref,
    query_ref,
    upstream_ref,
    ratio_ref,
    cos_table_ref,
    sin_table_ref,
    tables_ref,
    out_ref,
    kv_grad_ref,
    rows_buf,
    weight_buf,
    adv_buf,
    sems,
    acc_ref,
    kv_ref,
    kv_pad,
    key_grad,
    value_grad,
    coef_ref,
    place_ref,
    mask_ref,
    empty_ref,
    cos_ref,
    sin_ref,
):
    head = pl.program_id(0)
    rows = query_ref.shape[0]
    kv_width = acc_ref.shape[1] // 2
    blocks, _, depth = rows_buf.shape

    def arrival(k):
        here = pl.ds(pl.multiple_of(k * depth, depth), depth)
        return (
            pltpu.make_async_copy(got_ref.at[:, here], rows_buf.at[k], sems.at[0, k]),
            pltpu.make_async_copy(weight_ref.at[here, :], weight_buf.at[k], sems.at[1, k]),
        )

    def adv_arrival():
        here = pl.ds(blocks * depth, LANES)
        return pltpu.make_async_copy(got_ref.at[:, here], adv_buf, sems.at[0, blocks])

    @pl.when(head == 0)
    def _():
        adv_arrival().start()
        for k in range(AHEAD):
            for copy in arrival(k):
                copy.start()

    @pl.when(head == 0)
    def _():
        count, position = place_rows(
            lengths_ref, keep_ref, dest_ref, offsets_ref, place_ref, mask_ref, empty_ref
        )
        at = lax.broadcasted_iota(jnp.int32, (rows, HD), 1) == position
        at = jnp.where(at, 1.0, 0.0).astype(BF)
        looked_up = jnp.dot(at, tables_ref[...], preferred_element_type=F32)
        for ref, first in ((cos_ref, 0), (sin_ref, 3 * HD)):
            parts = [looked_up[:, first + i * HD : first + (i + 1) * HD] for i in range(3)]
            ref[...] = parts[0] + (parts[1] + parts[2])
        adv_arrival().wait()
        adv = jnp.dot(place_ref[...], adv_buf[...], preferred_element_type=F32)
        ratio = column_of(ratio_ref)
        clipped = (adv > 0) & (ratio > clip_high) | (adv < 0) & (ratio < clip_low)
        coef_ref[...] = jnp.where(clipped, 0.0, adv * ratio) * (-loss_scale / count)

    @pl.when(head == 0)
    def _():
        acc_ref[...] = jnp.zeros_like(acc_ref)

        @pl.loop(0, blocks)
        def _(k):
            for copy in arrival(k):
                copy.wait()

            @pl.when(k + AHEAD < blocks)
            def _():
                for copy in arrival(k + AHEAD):
                    copy.start()

            acc_ref[...] += jnp.dot(rows_buf[k], weight_buf[k], preferred_element_type=F32)

        for slot in range(rows // SLOT):
            here = pl.ds(slot * SLOT, SLOT)
            cosine, sine = cos_table_ref[...], sin_table_ref[...]
            for head in range(kv_width // HD):
                columns = pl.ds(head * HD, HD)
                key = acc_ref[here, columns]
                turned = key * cosine + pltpu.roll(key, HD // 2, 1) * sine
                kv_ref[here, columns] = turned.astype(BF)
            values = pl.ds(kv_width, kv_width)
            kv_ref[here, values] = acc_ref[here, values].astype(BF)
        kv_pad[pl.ds(0, SLOT), :] = jnp.zeros((SLOT, 2 * kv_width), BF)
        kv_pad[pl.ds(SLOT, rows), :] = jnp.dot(
            place_ref[...], kv_ref[...], preferred_element_type=F32
        ).astype(BF)

    attend_head(
        head,
        query_ref,
        upstream_ref,
        out_ref,
        kv_grad_ref,
        kv_pad,
        key_grad,
        value_grad,
        coef_ref,
        place_ref,
        mask_ref,
        empty_ref,
        cos_ref,
        sin_ref,
    )


def attend_head(
    head,
    query_ref,
    upstream_ref,
    out_ref,
    kv_grad_ref,
    kv_pad,
    key_grad,
    value_grad,
    coef_ref,
    place_ref,
    mask_ref,
    empty_ref,
    cos_ref,
    sin_ref,
):
    rows = query_ref.shape[0]
    group = query_ref.shape[1] // HD
    kv_width = kv_pad.shape[1] // 2
    scale = 1.0 / math.sqrt(HD)
    body = pl.ds(SLOT, rows)
    key_columns = pl.ds(pl.multiple_of(head * HD, HD), HD)
    value_columns = pl.ds(pl.multiple_of(kv_width + head * HD, HD), HD)
    across = (((1,), (1,)), ((), ()))
    along = (((0,), (0,)), ((), ()))
    key_grad[...] = jnp.zeros_like(key_grad)
    value_grad[...] = jnp.zeros_like(value_grad)
    for block, (first, size, window) in enumerate(row_blocks(rows)):
        here = pl.ds(first, size)
        span = pl.ds(window, WINDOW)
        coef = coef_ref[here, :]
        many = pl.ds(0, group * size)
        allowed = mask_ref[block, :, many] > 0.0
        empty = empty_ref[block, :, many]
        query = jnp.concatenate(
            [query_ref[here, pl.ds(g * HD, HD)] for g in range(group)], axis=0
        )
        grad = jnp.concatenate(
            [
                (coef * upstream_ref[here, pl.ds(g * HD, HD)].astype(F32)).astype(BF)
                for g in range(group)
            ],
            axis=0,
        )
        key = kv_pad[span, key_columns]
        value = kv_pad[span, value_columns]
        scores = lax.dot_general(key, query, across, preferred_element_type=F32) * scale
        raw = jnp.where(allowed, jnp.exp(scores), 0.0)
        normed = raw * (1.0 / (jnp.sum(raw, axis=0, keepdims=True) + empty))
        normed_low = normed.astype(BF)
        output = lax.dot_general(normed_low, value, along, preferred_element_type=F32).astype(BF)
        for g in range(group):
            out_ref[here, pl.ds(g * HD, HD)] = output[g * size : (g + 1) * size]
        grad_normed = lax.dot_general(value, grad, across, preferred_element_type=F32)
        delta = jnp.sum(normed * grad_normed, axis=0, keepdims=True)
        grad_scores = (normed * (grad_normed - delta) * scale).astype(BF)
        key_grad[span, :] += jnp.dot(grad_scores, query, preferred_element_type=F32)
        value_grad[span, :] += jnp.dot(normed_low, grad, preferred_element_type=F32)
    turned = key_grad[body, :]
    key_back = turned * cos_ref[...] - pltpu.roll(turned, HD // 2, 1) * sin_ref[...]
    both = jnp.concatenate([key_back.astype(BF), value_grad[body, :].astype(BF)], axis=1)
    kv_grad_ref[...] = lax.dot_general(
        both, place_ref[...], along, preferred_element_type=F32
    ).astype(BF)


def attend(plan, got, weights, queries, upstream, ratios):
    rows = got.shape[0]
    width, kv_columns = weights.shape
    heads = kv_columns // (2 * HD)
    query_width = queries.shape[1] // heads
    depth = width // DEPTH_BLOCKS
    blocks, most = len(row_blocks(rows)), WINDOW - SLOT
    anywhere = pl.BlockSpec(memory_space=pl.ANY)
    tables = [jnp.asarray(table) for table in slot_tables() + (lookup_tables(),)]
    whole = lambda array: pl.BlockSpec(array.shape, lambda k: (0,) * array.ndim)
    return pl.pallas_call(
        attend_kernel,
        grid=(heads,),
        in_specs=[whole(array) for array in plan]
        + [
            anywhere,
            anywhere,
            pl.BlockSpec((rows, query_width), lambda h: (0, h)),
            pl.BlockSpec((rows, query_width), lambda h: (0, h)),
            whole(ratios),
            whole(tables[0]),
            whole(tables[1]),
            whole(tables[2]),
        ],
        out_specs=[
            pl.BlockSpec((rows, query_width), lambda h: (0, h)),
            pl.BlockSpec((2 * HD, rows), lambda h: (h, 0)),
        ],
        out_shape=[
            jax.ShapeDtypeStruct(queries.shape, BF),
            jax.ShapeDtypeStruct((kv_columns, rows), BF),
        ],
        scratch_shapes=[
            pltpu.VMEM((DEPTH_BLOCKS, rows, depth), BF),
            pltpu.VMEM((DEPTH_BLOCKS, depth, kv_columns), BF),
            pltpu.VMEM((rows, LANES), BF),
            pltpu.SemaphoreType.DMA((2, DEPTH_BLOCKS + 1)),
            pltpu.VMEM((rows, kv_columns), F32),
            pltpu.VMEM((rows, kv_columns), BF),
            pltpu.VMEM((rows + SLOT, kv_columns), BF),
            pltpu.VMEM((rows + SLOT, HD), F32),
            pltpu.VMEM((rows + SLOT, HD), F32),
            pltpu.VMEM((rows, LANES), F32),
            pltpu.VMEM((rows, rows), BF),
            pltpu.VMEM((blocks, WINDOW, query_width // HD * most), F32),
            pltpu.VMEM((blocks, 1, query_width // HD * most), F32),
            pltpu.VMEM((rows, HD), F32),
            pltpu.VMEM((rows, HD), F32),
        ],
        compiler_params=params(),
        cost_estimate=cost(
            2 * rows * width * kv_columns + 10 * rows * queries.shape[1] * HD,
            rows * width + width * kv_columns + 3 * rows * queries.shape[1],
        ),
    )(*plan, got, weights, queries, upstream, ratios, *tables)


def grad_kernel(
    own_ref,
    other_ref,
    got_ref,
    sibling_ref,
    first_ref,
    rest_ref,
    own_buf,
    other_buf,
    mine_buf,
    sibling_buf,
    first_buf,
    rest_buf,
    sems,
    in_sems,
    out_sems,
):
    piece = mine_buf.shape[2] // 2
    split = first_buf.shape[2]
    blocks = [lax.rem(lax.axis_index("x") + k, RING) for k in range(RING)]
    own = pltpu.make_async_copy(own_ref, own_buf, sems.at[0])
    other = pltpu.make_async_copy(other_ref, other_buf, sems.at[1])

    def arrival(source, target, k, row):
        start = (2 * blocks[k] + lax.axis_index("core")) * piece
        here = pl.ds(pl.multiple_of(start, LANES), piece)
        there = pl.ds((k % 2) * piece, piece)
        return pltpu.make_async_copy(
            source.at[:, here], target.at[k // 2, :, there], in_sems.at[row, k]
        )

    mine = [arrival(got_ref, mine_buf, k, 0) for k in range(RING)]
    sibling = [arrival(sibling_ref, sibling_buf, k, 1) for k in range(RING)]
    early = [own, mine[0], mine[1]]
    late = [[other, sibling[0], sibling[1]], [mine[2], mine[3], sibling[2], sibling[3]]]
    for copy in early + late[0]:
        copy.start()
    for copy in early:
        copy.wait()
    for copy in late[1]:
        copy.start()
    leave = []
    for half in range(2):
        for part in range(ROW_PARTS):
            count = own_buf.shape[0] // ROW_PARTS
            rows = pl.ds(part * count, count)
            product = jnp.dot(own_buf[rows, :], mine_buf[half], preferred_element_type=F32)
            if half == 0 and part == 0:
                for copy in late[0]:
                    copy.wait()
            product += jnp.dot(other_buf[rows, :], sibling_buf[half], preferred_element_type=F32)
            product = product.astype(BF)
            places = rest_buf.shape[1] // ROW_PARTS
            there = pl.ds(part * places, places)
            for k in (2 * half, 2 * half + 1):
                columns = slice((k % 2) * piece, (k % 2 + 1) * piece)
                first_buf[k, rows, :] = product[:, columns][:, :split]
                rest_buf[k, there] = product[:, columns][:, split:].reshape(
                    (places,) + rest_buf.shape[2:]
                )
                pair = (
                    pltpu.make_async_copy(
                        first_buf.at[k, rows], first_ref.at[blocks[k], rows], out_sems.at[0, k, part]
                    ),
                    pltpu.make_async_copy(
                        rest_buf.at[k, there],
                        rest_ref.at[there, blocks[k]],
                        out_sems.at[1, k, part],
                    ),
                )
                for copy in pair:
                    copy.start()
                    leave.append(copy)
        if half == 0:
            for copy in late[1]:
                copy.wait()
    for copy in leave:
        copy.wait()


def grad_parts(own, other, got, sibling, width, places):
    columns, rows = own.shape
    piece = width // (2 * RING)
    split = piece // 5 * SPLIT
    size = columns // places
    anywhere = pl.BlockSpec(memory_space=pl.ANY)
    return pl.pallas_call(
        grad_kernel,
        in_specs=[anywhere] * 4,
        out_specs=[anywhere] * 2,
        out_shape=[
            jax.ShapeDtypeStruct((RING, columns, split), BF),
            jax.ShapeDtypeStruct((places, RING, size, piece - split), BF),
        ],
        scratch_shapes=[
            pltpu.VMEM((columns, rows), BF),
            pltpu.VMEM((columns, rows), BF),
            pltpu.VMEM((2, rows, 2 * piece), BF),
            pltpu.VMEM((2, rows, 2 * piece), BF),
            pltpu.VMEM((RING, columns, split), BF),
            pltpu.VMEM((RING, places, size, piece - split), BF),
            pltpu.SemaphoreType.DMA((2,)),
            pltpu.SemaphoreType.DMA((2, RING)),
            pltpu.SemaphoreType.DMA((2, RING, ROW_PARTS)),
        ],
        compiler_params=params(20 * 1024 * 1024),
        cost_estimate=cost(
            4 * rows * columns * RING * piece, RING * piece * (2 * rows + columns)
        ),
    )(own, other, got, sibling)


def finish_kernel(spread_ref, key_ref, value_ref):
    places, size, _ = spread_ref.shape
    per_head = HD // size
    for i in range(places // per_head):
        rows = [spread_ref[i * per_head + j].astype(F32) for j in range(per_head)]
        out_ref = value_ref if i % 2 else key_ref
        out_ref[:, pl.ds(i // 2 * HD, HD)] = jnp.concatenate(rows, axis=0).T


def finish(spread, kv_width):
    columns = spread.shape[2]
    return pl.pallas_call(
        finish_kernel,
        out_shape=[jax.ShapeDtypeStruct((columns, kv_width), F32)] * 2,
        compiler_params=params(),
        cost_estimate=cost(0, 3 * spread.size),
    )(spread)


def summed(parts):
    return jnp.sum(parts.astype(F32), axis=0)


def swap_cores(value):
    return lax.ppermute(value, "core", [(0, 1), (1, 0)])


def exchange(value, axis):
    return lax.all_to_all(value, axis, split_axis=0, concat_axis=0, tiled=True)


def on_device(
    hidden,
    advantages,
    queries,
    upstream,
    ratios,
    key_weight,
    value_weight,
    lengths,
    keep_flags,
    destinations,
    offsets,
):
    dp_count = lengths.shape[0]
    rows_here, model_width = hidden.shape
    kv_width = key_weight.shape[1]
    adv = advantages.reshape(rows_here // LANES, LANES)
    sent, weights = order(destinations, hidden, adv, key_weight, value_weight)
    weights = lax.all_gather(weights, FSDP, axis=0, tiled=True)
    got = exchange(sent.reshape(dp_count, SLOT, sent.shape[1]), DP).reshape(sent.shape)
    sibling = swap_cores(got)
    plan = (lengths, keep_flags, destinations, offsets)
    ratios = ratios.reshape(rows_here // LANES, LANES)
    attention, own = attend(plan, got, weights, queries, upstream, ratios)
    other = swap_cores(own)

    first, rest = grad_parts(own, other, got, sibling, model_width, dp_count)
    first = lax.psum_scatter(
        first.reshape(-1, first.shape[2]), "x", scatter_dimension=0, tiled=True
    )
    rest = exchange(summed(exchange(rest, DP)).astype(BF), "x")
    first, rest = lax.optimization_barrier((first, rest))
    first = exchange(first.reshape(dp_count, -1, first.shape[1]), DP)
    share = jnp.concatenate([summed(first), summed(rest)], axis=1).astype(BF)
    spread = exchange(jnp.broadcast_to(share[None], (dp_count,) + share.shape), DP)
    grad_key, grad_value = finish(spread, kv_width)
    return (attention, grad_key, grad_value)


def solution(mesh):
    chips = {"y": RING, "z": RING, "x": RING, "core": 2}
    fine = Mesh(mesh.devices.reshape(tuple(chips.values())), tuple(chips))
    in_specs = (
        P(ALL, None),
        P(ALL),
        P(ALL, None),
        P(ALL, None),
        P(ALL),
        P(FSDP, None),
        P(FSDP, None),
        P(),
        P(),
        P(),
        P(),
    )
    out_specs = (P(ALL, None), P(FSDP, None), P(FSDP, None))
    return jax.shard_map(
        on_device, mesh=fine, in_specs=in_specs, out_specs=out_specs, check_vma=False
    )
```

```python
import math

import jax
import jax.numpy as jnp
import ml_dtypes
import numpy as np
from jax import lax
from jax.experimental import pallas as pl
from jax.experimental.pallas import tpu as pltpu
from jax.sharding import Mesh
from jax.sharding import PartitionSpec as P

HD = 128
SLOT = 32
RING = 4
ROW_PARTS = 2
WINDOW = 160
SPLIT = 3
VMEM_LIMIT = 56 * 1024 * 1024

rope_base = 1000000.0
loss_scale = 256.0
clip_low = 0.8
clip_high = 1.28

DP = ("y", "z")
FSDP = ("x", "core")
ALL = DP + FSDP
BF = jnp.bfloat16
F32 = jnp.float32
LANES = 128
DEPTH_BLOCKS = 5
AHEAD = 3


def row_blocks(rows):
    step = WINDOW - SLOT
    blocks = []
    for first in range(0, rows, step):
        size = min(step, rows - first)
        blocks.append((first, size, min(first, rows + SLOT - WINDOW)))
    return blocks


def slot_tables():
    frequency = rope_base ** (-(np.arange(HD // 2) * (2.0 / HD)))
    angle = np.arange(SLOT)[:, None] * frequency[None, :]
    cosine, sine = np.cos(angle), np.sin(angle)
    return (
        np.concatenate([cosine, cosine], axis=1).astype(np.float32),
        np.concatenate([-sine, sine], axis=1).astype(np.float32),
    )


def lookup_tables():
    terms = []
    for table in slot_tables():
        left = table
        for _ in range(3):
            term = left.astype(ml_dtypes.bfloat16)
            left = left - term.astype(np.float32)
            terms.append(term)
    return np.pad(np.concatenate(terms, axis=1), ((0, HD - SLOT), (0, 0)))


def params(limit=VMEM_LIMIT):
    return pltpu.CompilerParams(vmem_limit_bytes=limit)


def cost(flops, count):
    return pl.CostEstimate(flops=int(flops), bytes_accessed=int(2 * count), transcendentals=0)


def dp_fsdp():
    dp_index = lax.axis_index("y") * RING + lax.axis_index("z")
    return dp_index, lax.axis_index("x") * 2 + lax.axis_index("core")


def column_of(row_ref):
    same = lax.broadcasted_iota(jnp.int32, (LANES, LANES), 0) == lax.broadcasted_iota(
        jnp.int32, (LANES, LANES), 1
    )
    parts = []
    for i in range(row_ref.shape[0]):
        row = row_ref[i : i + 1, :].astype(F32)
        parts.append(jnp.sum(jnp.where(same, row, 0.0), axis=1, keepdims=True))
    return jnp.concatenate(parts, axis=0)


def order_kernel(
    dest_ref,
    hidden_ref,
    adv_ref,
    key_ref,
    value_ref,
    sent_ref,
    weight_ref,
    rows_buf,
    adv_buf,
    weight_buf,
    in_sems,
    out_sems,
    adv_sems,
    weight_sems,
):
    dp_index, group = dp_fsdp()
    width = hidden_ref.shape[1]
    kv_width = key_ref.shape[1]
    slots = hidden_ref.shape[0] // SLOT
    both = [
        pltpu.make_async_copy(
            ref, weight_buf.at[:, pl.ds(i * kv_width, kv_width)], weight_sems.at[i]
        )
        for i, ref in enumerate((key_ref, value_ref))
    ]
    arrive, leave, adv_leave = [], [], []
    for slot in range(slots):
        here = pl.ds(slot * SLOT, SLOT)
        there = pl.ds(pl.multiple_of(dest_ref[dp_index, group, slot] * SLOT, SLOT), SLOT)
        arrive.append(
            pltpu.make_async_copy(hidden_ref.at[here, :], rows_buf.at[slot], in_sems.at[slot])
        )
        leave.append(
            pltpu.make_async_copy(
                rows_buf.at[slot], sent_ref.at[there, pl.ds(0, width)], out_sems.at[slot]
            )
        )
        adv_leave.append(
            pltpu.make_async_copy(
                adv_buf.at[here, :], sent_ref.at[there, pl.ds(width, LANES)], adv_sems.at[slot]
            )
        )
    for copy in both + arrive:
        copy.start()
    adv_buf[...] = jnp.broadcast_to(column_of(adv_ref), adv_buf.shape).astype(BF)
    for copy in adv_leave:
        copy.start()
    for copy in both:
        copy.wait()
    out = pltpu.make_async_copy(weight_buf, weight_ref, weight_sems.at[2])
    out.start()
    for slot in range(slots):
        arrive[slot].wait()
        leave[slot].start()
    out.wait()
    for copy in adv_leave + leave:
        copy.wait()


def order(destinations, hidden, adv, key_weight, value_weight):
    rows, width = hidden.shape
    depth, kv_width = key_weight.shape
    slots = rows // SLOT
    anywhere = pl.BlockSpec(memory_space=pl.ANY)
    return pl.pallas_call(
        order_kernel,
        in_specs=[
            pl.BlockSpec(memory_space=pltpu.SMEM),
            anywhere,
            pl.BlockSpec(memory_space=pltpu.VMEM),
            anywhere,
            anywhere,
        ],
        out_specs=[anywhere] * 2,
        out_shape=[
            jax.ShapeDtypeStruct((rows, width + LANES), BF),
            jax.ShapeDtypeStruct((depth, 2 * kv_width), BF),
        ],
        scratch_shapes=[
            pltpu.VMEM((slots, SLOT, width), BF),
            pltpu.VMEM((rows, LANES), BF),
            pltpu.VMEM((depth, 2 * kv_width), BF),
            pltpu.SemaphoreType.DMA((slots,)),
            pltpu.SemaphoreType.DMA((slots,)),
            pltpu.SemaphoreType.DMA((slots,)),
            pltpu.SemaphoreType.DMA((3,)),
        ],
        compiler_params=params(),
        cost_estimate=cost(0, 2 * rows * width),
    )(destinations, hidden, adv, key_weight, value_weight)


def place_rows(lengths_ref, keep_ref, dest_ref, offsets_ref, place, mask, empty):
    rows = place.shape[0]
    dp_count, fsdp_count, slots = lengths_ref.shape
    dp_index, group = dp_fsdp()

    def of_group(ref):
        picked = lax.broadcasted_iota(jnp.int32, (dp_count, fsdp_count, slots), 1) == group
        return jnp.sum(jnp.where(picked, ref[...], 0), axis=1)

    keep = keep_ref[...]
    same = lax.broadcasted_iota(jnp.int32, (dp_count, dp_count), 0) == lax.broadcasted_iota(
        jnp.int32, (dp_count, dp_count), 1
    )
    picked = lax.broadcasted_iota(jnp.int32, keep.shape, 0) == group
    keep_row = jnp.sum(jnp.where(picked, keep, 0), axis=0, keepdims=True)
    keep_column = jnp.sum(jnp.where(same, keep_row, 0), axis=1, keepdims=True)
    kept = lengths_ref[0] * keep[:, 0:1]
    for source in range(1, dp_count):
        kept += lengths_ref[source] * keep[:, source : source + 1]
    count = jnp.sum(kept.astype(F32))
    kept = of_group(lengths_ref) * keep_column
    incoming = (of_group(dest_ref) == dp_index) & (kept > 0)
    offset = jnp.sum(jnp.where(incoming, of_group(offsets_ref), 0), axis=1, keepdims=True)
    length = jnp.sum(jnp.where(incoming, kept, 0), axis=1, keepdims=True)

    offset_row = jnp.sum(jnp.where(same, offset, 0), axis=0, keepdims=True)
    length_row = jnp.sum(jnp.where(same, length, 0), axis=0, keepdims=True)
    source = lax.broadcasted_iota(jnp.int32, (rows, dp_count), 1)
    relative = lax.broadcasted_iota(jnp.int32, (rows, dp_count), 0) - offset_row
    inside = (relative >= 0) & (relative < length_row)
    origin = jnp.sum(
        jnp.where(inside, source * SLOT + relative + 1, 0), axis=1, keepdims=True
    )
    origin = origin - 1
    filled = origin >= 0
    position = jnp.where(filled, lax.rem(origin, SLOT), 0)
    wide = lax.broadcasted_iota(jnp.int32, (rows, rows), 1)
    place[...] = jnp.where(wide == origin, 1.0, 0.0).astype(BF)

    for block, (first, size, window) in enumerate(row_blocks(rows)):
        width = mask.shape[2]
        across = first + lax.rem(lax.broadcasted_iota(jnp.int32, (dp_count, width), 1), size)
        relative = across - offset
        inside = (relative >= 0) & (relative < length)
        reach = jnp.sum(jnp.where(inside, relative + 1, 0), axis=0, keepdims=True)
        row = across[0:1]
        seen = window - SLOT + lax.broadcasted_iota(jnp.int32, (WINDOW, width), 0)
        visible = (seen > row - reach) & (seen <= row)
        mask[block] = jnp.where(visible, 1.0, 0.0)
        empty[block] = jnp.where(reach > 0, 0.0, 1.0)
    return count, position


def attend_kernel(
    lengths_ref,
    keep_ref,
    dest_ref,
    offsets_ref,
    got_ref,
    weight_ref,
    query_ref,
    upstream_ref,
    ratio_ref,
    cos_table_ref,
    sin_table_ref,
    tables_ref,
    out_ref,
    kv_grad_ref,
    rows_buf,
    weight_buf,
    adv_buf,
    sems,
    acc_ref,
    kv_ref,
    kv_pad,
    key_grad,
    value_grad,
    coef_ref,
    place_ref,
    mask_ref,
    empty_ref,
    cos_ref,
    sin_ref,
):
    head = pl.program_id(0)
    rows = query_ref.shape[0]
    kv_width = acc_ref.shape[1] // 2
    blocks, _, depth = rows_buf.shape

    def arrival(k):
        here = pl.ds(pl.multiple_of(k * depth, depth), depth)
        return (
            pltpu.make_async_copy(got_ref.at[:, here], rows_buf.at[k], sems.at[0, k]),
            pltpu.make_async_copy(weight_ref.at[here, :], weight_buf.at[k], sems.at[1, k]),
        )

    def adv_arrival():
        here = pl.ds(blocks * depth, LANES)
        return pltpu.make_async_copy(got_ref.at[:, here], adv_buf, sems.at[0, blocks])

    @pl.when(head == 0)
    def _():
        adv_arrival().start()
        for k in range(AHEAD):
            for copy in arrival(k):
                copy.start()

    @pl.when(head == 0)
    def _():
        count, position = place_rows(
            lengths_ref, keep_ref, dest_ref, offsets_ref, place_ref, mask_ref, empty_ref
        )
        at = lax.broadcasted_iota(jnp.int32, (rows, HD), 1) == position
        at = jnp.where(at, 1.0, 0.0).astype(BF)
        looked_up = jnp.dot(at, tables_ref[...], preferred_element_type=F32)
        for ref, first in ((cos_ref, 0), (sin_ref, 3 * HD)):
            parts = [looked_up[:, first + i * HD : first + (i + 1) * HD] for i in range(3)]
            ref[...] = parts[0] + (parts[1] + parts[2])
        adv_arrival().wait()
        adv = jnp.dot(place_ref[...], adv_buf[...], preferred_element_type=F32)
        ratio = column_of(ratio_ref)
        clipped = (adv > 0) & (ratio > clip_high) | (adv < 0) & (ratio < clip_low)
        coef_ref[...] = jnp.where(clipped, 0.0, adv * ratio) * (-loss_scale / count)

    @pl.when(head == 0)
    def _():
        acc_ref[...] = jnp.zeros_like(acc_ref)

        @pl.loop(0, blocks)
        def _(k):
            for copy in arrival(k):
                copy.wait()

            @pl.when(k + AHEAD < blocks)
            def _():
                for copy in arrival(k + AHEAD):
                    copy.start()

            acc_ref[...] += jnp.dot(rows_buf[k], weight_buf[k], preferred_element_type=F32)

        for slot in range(rows // SLOT):
            here = pl.ds(slot * SLOT, SLOT)
            cosine, sine = cos_table_ref[...], sin_table_ref[...]
            for head in range(kv_width // HD):
                columns = pl.ds(head * HD, HD)
                key = acc_ref[here, columns]
                turned = key * cosine + pltpu.roll(key, HD // 2, 1) * sine
                kv_ref[here, columns] = turned.astype(BF)
            values = pl.ds(kv_width, kv_width)
            kv_ref[here, values] = acc_ref[here, values].astype(BF)
        kv_pad[pl.ds(0, SLOT), :] = jnp.zeros((SLOT, 2 * kv_width), BF)
        kv_pad[pl.ds(SLOT, rows), :] = jnp.dot(
            place_ref[...], kv_ref[...], preferred_element_type=F32
        ).astype(BF)

    attend_head(
        head,
        query_ref,
        upstream_ref,
        out_ref,
        kv_grad_ref,
        kv_pad,
        key_grad,
        value_grad,
        coef_ref,
        place_ref,
        mask_ref,
        empty_ref,
        cos_ref,
        sin_ref,
    )


def attend_head(
    head,
    query_ref,
    upstream_ref,
    out_ref,
    kv_grad_ref,
    kv_pad,
    key_grad,
    value_grad,
    coef_ref,
    place_ref,
    mask_ref,
    empty_ref,
    cos_ref,
    sin_ref,
):
    rows = query_ref.shape[0]
    group = query_ref.shape[1] // HD
    kv_width = kv_pad.shape[1] // 2
    scale = 1.0 / math.sqrt(HD)
    body = pl.ds(SLOT, rows)
    key_columns = pl.ds(pl.multiple_of(head * HD, HD), HD)
    value_columns = pl.ds(pl.multiple_of(kv_width + head * HD, HD), HD)
    across = (((1,), (1,)), ((), ()))
    along = (((0,), (0,)), ((), ()))
    key_grad[...] = jnp.zeros_like(key_grad)
    value_grad[...] = jnp.zeros_like(value_grad)
    for block, (first, size, window) in enumerate(row_blocks(rows)):
        here = pl.ds(first, size)
        span = pl.ds(window, WINDOW)
        coef = coef_ref[here, :]
        many = pl.ds(0, group * size)
        allowed = mask_ref[block, :, many] > 0.0
        empty = empty_ref[block, :, many]
        query = jnp.concatenate(
            [query_ref[here, pl.ds(g * HD, HD)] for g in range(group)], axis=0
        )
        grad = jnp.concatenate(
            [
                (coef * upstream_ref[here, pl.ds(g * HD, HD)].astype(F32)).astype(BF)
                for g in range(group)
            ],
            axis=0,
        )
        key = kv_pad[span, key_columns]
        value = kv_pad[span, value_columns]
        scores = lax.dot_general(key, query, across, preferred_element_type=F32) * scale
        raw = jnp.where(allowed, jnp.exp(scores), 0.0)
        normed = raw * (1.0 / (jnp.sum(raw, axis=0, keepdims=True) + empty))
        normed_low = normed.astype(BF)
        output = lax.dot_general(normed_low, value, along, preferred_element_type=F32).astype(BF)
        for g in range(group):
            out_ref[here, pl.ds(g * HD, HD)] = output[g * size : (g + 1) * size]
        grad_normed = lax.dot_general(value, grad, across, preferred_element_type=F32)
        delta = jnp.sum(normed * grad_normed, axis=0, keepdims=True)
        grad_scores = (normed * (grad_normed - delta) * scale).astype(BF)
        key_grad[span, :] += jnp.dot(grad_scores, query, preferred_element_type=F32)
        value_grad[span, :] += jnp.dot(normed_low, grad, preferred_element_type=F32)
    turned = key_grad[body, :]
    key_back = turned * cos_ref[...] - pltpu.roll(turned, HD // 2, 1) * sin_ref[...]
    both = jnp.concatenate([key_back.astype(BF), value_grad[body, :].astype(BF)], axis=1)
    kv_grad_ref[...] = lax.dot_general(
        both, place_ref[...], along, preferred_element_type=F32
    ).astype(BF)


def attend(plan, got, weights, queries, upstream, ratios):
    rows = got.shape[0]
    width, kv_columns = weights.shape
    heads = kv_columns // (2 * HD)
    query_width = queries.shape[1] // heads
    depth = width // DEPTH_BLOCKS
    blocks, most = len(row_blocks(rows)), WINDOW - SLOT
    anywhere = pl.BlockSpec(memory_space=pl.ANY)
    tables = [jnp.asarray(table) for table in slot_tables() + (lookup_tables(),)]
    whole = lambda array: pl.BlockSpec(array.shape, lambda k: (0,) * array.ndim)
    return pl.pallas_call(
        attend_kernel,
        grid=(heads,),
        in_specs=[whole(array) for array in plan]
        + [
            anywhere,
            anywhere,
            pl.BlockSpec((rows, query_width), lambda h: (0, h)),
            pl.BlockSpec((rows, query_width), lambda h: (0, h)),
            whole(ratios),
            whole(tables[0]),
            whole(tables[1]),
            whole(tables[2]),
        ],
        out_specs=[
            pl.BlockSpec((rows, query_width), lambda h: (0, h)),
            pl.BlockSpec((2 * HD, rows), lambda h: (h, 0)),
        ],
        out_shape=[
            jax.ShapeDtypeStruct(queries.shape, BF),
            jax.ShapeDtypeStruct((kv_columns, rows), BF),
        ],
        scratch_shapes=[
            pltpu.VMEM((DEPTH_BLOCKS, rows, depth), BF),
            pltpu.VMEM((DEPTH_BLOCKS, depth, kv_columns), BF),
            pltpu.VMEM((rows, LANES), BF),
            pltpu.SemaphoreType.DMA((2, DEPTH_BLOCKS + 1)),
            pltpu.VMEM((rows, kv_columns), F32),
            pltpu.VMEM((rows, kv_columns), BF),
            pltpu.VMEM((rows + SLOT, kv_columns), BF),
            pltpu.VMEM((rows + SLOT, HD), F32),
            pltpu.VMEM((rows + SLOT, HD), F32),
            pltpu.VMEM((rows, LANES), F32),
            pltpu.VMEM((rows, rows), BF),
            pltpu.VMEM((blocks, WINDOW, query_width // HD * most), F32),
            pltpu.VMEM((blocks, 1, query_width // HD * most), F32),
            pltpu.VMEM((rows, HD), F32),
            pltpu.VMEM((rows, HD), F32),
        ],
        compiler_params=params(),
        cost_estimate=cost(
            2 * rows * width * kv_columns + 10 * rows * queries.shape[1] * HD,
            rows * width + width * kv_columns + 3 * rows * queries.shape[1],
        ),
    )(*plan, got, weights, queries, upstream, ratios, *tables)


def grad_kernel(
    own_ref,
    other_ref,
    got_ref,
    sibling_ref,
    first_ref,
    rest_ref,
    own_buf,
    other_buf,
    mine_buf,
    sibling_buf,
    first_buf,
    rest_buf,
    sems,
    in_sems,
    out_sems,
):
    piece = mine_buf.shape[2] // 2
    split = first_buf.shape[2]
    blocks = [lax.rem(lax.axis_index("x") + k, RING) for k in range(RING)]
    own = pltpu.make_async_copy(own_ref, own_buf, sems.at[0])
    other = pltpu.make_async_copy(other_ref, other_buf, sems.at[1])

    def arrival(source, target, k, row):
        start = (2 * blocks[k] + lax.axis_index("core")) * piece
        here = pl.ds(pl.multiple_of(start, LANES), piece)
        there = pl.ds((k % 2) * piece, piece)
        return pltpu.make_async_copy(
            source.at[:, here], target.at[k // 2, :, there], in_sems.at[row, k]
        )

    mine = [arrival(got_ref, mine_buf, k, 0) for k in range(RING)]
    sibling = [arrival(sibling_ref, sibling_buf, k, 1) for k in range(RING)]
    early = [own, mine[0], mine[1]]
    late = [[other, sibling[0], sibling[1]], [mine[2], mine[3], sibling[2], sibling[3]]]
    for copy in early + late[0]:
        copy.start()
    for copy in early:
        copy.wait()
    for copy in late[1]:
        copy.start()
    leave = []
    for half in range(2):
        for part in range(ROW_PARTS):
            count = own_buf.shape[0] // ROW_PARTS
            rows = pl.ds(part * count, count)
            product = jnp.dot(own_buf[rows, :], mine_buf[half], preferred_element_type=F32)
            if half == 0 and part == 0:
                for copy in late[0]:
                    copy.wait()
            product += jnp.dot(other_buf[rows, :], sibling_buf[half], preferred_element_type=F32)
            product = product.astype(BF)
            places = rest_buf.shape[1] // ROW_PARTS
            there = pl.ds(part * places, places)
            for k in (2 * half, 2 * half + 1):
                columns = slice((k % 2) * piece, (k % 2 + 1) * piece)
                first_buf[k, rows, :] = product[:, columns][:, :split]
                rest_buf[k, there] = product[:, columns][:, split:].reshape(
                    (places,) + rest_buf.shape[2:]
                )
                pair = (
                    pltpu.make_async_copy(
                        first_buf.at[k, rows], first_ref.at[blocks[k], rows], out_sems.at[0, k, part]
                    ),
                    pltpu.make_async_copy(
                        rest_buf.at[k, there],
                        rest_ref.at[there, blocks[k]],
                        out_sems.at[1, k, part],
                    ),
                )
                for copy in pair:
                    copy.start()
                    leave.append(copy)
        if half == 0:
            for copy in late[1]:
                copy.wait()
    for copy in leave:
        copy.wait()


def grad_parts(own, other, got, sibling, width, places):
    columns, rows = own.shape
    piece = width // (2 * RING)
    split = piece // 5 * SPLIT
    size = columns // places
    anywhere = pl.BlockSpec(memory_space=pl.ANY)
    return pl.pallas_call(
        grad_kernel,
        in_specs=[anywhere] * 4,
        out_specs=[anywhere] * 2,
        out_shape=[
            jax.ShapeDtypeStruct((RING, columns, split), BF),
            jax.ShapeDtypeStruct((places, RING, size, piece - split), BF),
        ],
        scratch_shapes=[
            pltpu.VMEM((columns, rows), BF),
            pltpu.VMEM((columns, rows), BF),
            pltpu.VMEM((2, rows, 2 * piece), BF),
            pltpu.VMEM((2, rows, 2 * piece), BF),
            pltpu.VMEM((RING, columns, split), BF),
            pltpu.VMEM((RING, places, size, piece - split), BF),
            pltpu.SemaphoreType.DMA((2,)),
            pltpu.SemaphoreType.DMA((2, RING)),
            pltpu.SemaphoreType.DMA((2, RING, ROW_PARTS)),
        ],
        compiler_params=params(20 * 1024 * 1024),
        cost_estimate=cost(
            4 * rows * columns * RING * piece, RING * piece * (2 * rows + columns)
        ),
    )(own, other, got, sibling)


def finish_kernel(spread_ref, key_ref, value_ref):
    places, size, _ = spread_ref.shape
    per_head = HD // size
    for i in range(places // per_head):
        rows = [spread_ref[i * per_head + j].astype(F32) for j in range(per_head)]
        out_ref = value_ref if i % 2 else key_ref
        out_ref[:, pl.ds(i // 2 * HD, HD)] = jnp.concatenate(rows, axis=0).T


def finish(spread, kv_width):
    columns = spread.shape[2]
    return pl.pallas_call(
        finish_kernel,
        out_shape=[jax.ShapeDtypeStruct((columns, kv_width), F32)] * 2,
        compiler_params=params(),
        cost_estimate=cost(0, 3 * spread.size),
    )(spread)


def summed(parts):
    return jnp.sum(parts.astype(F32), axis=0)


def swap_cores(value):
    return lax.ppermute(value, "core", [(0, 1), (1, 0)])


def exchange(value, axis):
    return lax.all_to_all(value, axis, split_axis=0, concat_axis=0, tiled=True)


def scatter_over_x(blocks):
    flat = blocks.reshape(-1, blocks.shape[2])
    return lax.psum_scatter(flat, "x", scatter_dimension=0, tiled=True)


def on_device(
    hidden,
    advantages,
    queries,
    upstream,
    ratios,
    key_weight,
    value_weight,
    lengths,
    keep_flags,
    destinations,
    offsets,
):
    dp_count = lengths.shape[0]
    rows_here, model_width = hidden.shape
    kv_width = key_weight.shape[1]
    adv = advantages.reshape(rows_here // LANES, LANES)
    sent, weights = order(destinations, hidden, adv, key_weight, value_weight)
    weights = lax.all_gather(weights, FSDP, axis=0, tiled=True)
    got = exchange(sent.reshape(dp_count, SLOT, sent.shape[1]), DP).reshape(sent.shape)
    sibling = swap_cores(got)
    plan = (lengths, keep_flags, destinations, offsets)
    ratios = ratios.reshape(rows_here // LANES, LANES)
    attention, own = attend(plan, got, weights, queries, upstream, ratios)
    other = swap_cores(own)

    first, rest = grad_parts(own, other, got, sibling, model_width, dp_count)
    first = scatter_over_x(first)
    rest = summed(exchange(rest, DP)).astype(BF)
    first, rest = lax.optimization_barrier((first, rest))
    rest = scatter_over_x(rest)
    first = exchange(first.reshape(dp_count, -1, first.shape[1]), DP)
    share = jnp.concatenate([summed(first), rest.astype(F32)], axis=1).astype(BF)
    spread = exchange(jnp.broadcast_to(share[None], (dp_count,) + share.shape), DP)
    grad_key, grad_value = finish(spread, kv_width)
    return (attention, grad_key, grad_value)


def solution(mesh):
    chips = {"y": RING, "z": RING, "x": RING, "core": 2}
    fine = Mesh(mesh.devices.reshape(tuple(chips.values())), tuple(chips))
    in_specs = (
        P(ALL, None),
        P(ALL),
        P(ALL, None),
        P(ALL, None),
        P(ALL),
        P(FSDP, None),
        P(FSDP, None),
        P(),
        P(),
        P(),
        P(),
    )
    out_specs = (P(ALL, None), P(FSDP, None), P(FSDP, None))
    return jax.shard_map(
        on_device, mesh=fine, in_specs=in_specs, out_specs=out_specs, check_vma=False
    )
```

```python
import math

import jax
import jax.numpy as jnp
import ml_dtypes
import numpy as np
from jax import lax
from jax.experimental import pallas as pl
from jax.experimental.pallas import tpu as pltpu
from jax.sharding import Mesh
from jax.sharding import PartitionSpec as P

HD = 128
SLOT = 32
RING = 4
ROW_PARTS = 1
WINDOW = 160
SPLIT = 3
VMEM_LIMIT = 56 * 1024 * 1024

rope_base = 1000000.0
loss_scale = 256.0
clip_low = 0.8
clip_high = 1.28

DP = ("y", "z")
FSDP = ("x", "core")
ALL = DP + FSDP
BF = jnp.bfloat16
F32 = jnp.float32
LANES = 128
DEPTH_BLOCKS = 5
AHEAD = 3


def row_blocks(rows):
    step = WINDOW - SLOT
    blocks = []
    for first in range(0, rows, step):
        size = min(step, rows - first)
        blocks.append((first, size, min(first, rows + SLOT - WINDOW)))
    return blocks


def slot_tables():
    frequency = rope_base ** (-(np.arange(HD // 2) * (2.0 / HD)))
    angle = np.arange(SLOT)[:, None] * frequency[None, :]
    cosine, sine = np.cos(angle), np.sin(angle)
    return (
        np.concatenate([cosine, cosine], axis=1).astype(np.float32),
        np.concatenate([-sine, sine], axis=1).astype(np.float32),
    )


def lookup_tables():
    terms = []
    for table in slot_tables():
        left = table
        for _ in range(3):
            term = left.astype(ml_dtypes.bfloat16)
            left = left - term.astype(np.float32)
            terms.append(term)
    return np.pad(np.concatenate(terms, axis=1), ((0, HD - SLOT), (0, 0)))


def params(limit=VMEM_LIMIT):
    return pltpu.CompilerParams(vmem_limit_bytes=limit)


def cost(flops, count):
    return pl.CostEstimate(flops=int(flops), bytes_accessed=int(2 * count), transcendentals=0)


def dp_fsdp():
    dp_index = lax.axis_index("y") * RING + lax.axis_index("z")
    return dp_index, lax.axis_index("x") * 2 + lax.axis_index("core")


def column_of(row_ref):
    same = lax.broadcasted_iota(jnp.int32, (LANES, LANES), 0) == lax.broadcasted_iota(
        jnp.int32, (LANES, LANES), 1
    )
    parts = []
    for i in range(row_ref.shape[0]):
        row = row_ref[i : i + 1, :].astype(F32)
        parts.append(jnp.sum(jnp.where(same, row, 0.0), axis=1, keepdims=True))
    return jnp.concatenate(parts, axis=0)


def order_kernel(
    dest_ref,
    hidden_ref,
    adv_ref,
    key_ref,
    value_ref,
    sent_ref,
    weight_ref,
    rows_buf,
    adv_buf,
    weight_buf,
    in_sems,
    out_sems,
    adv_sems,
    weight_sems,
):
    dp_index, group = dp_fsdp()
    width = hidden_ref.shape[1]
    kv_width = key_ref.shape[1]
    slots = hidden_ref.shape[0] // SLOT
    both = [
        pltpu.make_async_copy(
            ref, weight_buf.at[:, pl.ds(i * kv_width, kv_width)], weight_sems.at[i]
        )
        for i, ref in enumerate((key_ref, value_ref))
    ]
    arrive, leave, adv_leave = [], [], []
    for slot in range(slots):
        here = pl.ds(slot * SLOT, SLOT)
        there = pl.ds(pl.multiple_of(dest_ref[dp_index, group, slot] * SLOT, SLOT), SLOT)
        arrive.append(
            pltpu.make_async_copy(hidden_ref.at[here, :], rows_buf.at[slot], in_sems.at[slot])
        )
        leave.append(
            pltpu.make_async_copy(
                rows_buf.at[slot], sent_ref.at[there, pl.ds(0, width)], out_sems.at[slot]
            )
        )
        adv_leave.append(
            pltpu.make_async_copy(
                adv_buf.at[here, :], sent_ref.at[there, pl.ds(width, LANES)], adv_sems.at[slot]
            )
        )
    for copy in both + arrive:
        copy.start()
    adv_buf[...] = jnp.broadcast_to(column_of(adv_ref), adv_buf.shape).astype(BF)
    for copy in adv_leave:
        copy.start()
    for copy in both:
        copy.wait()
    out = pltpu.make_async_copy(weight_buf, weight_ref, weight_sems.at[2])
    out.start()
    for slot in range(slots):
        arrive[slot].wait()
        leave[slot].start()
    out.wait()
    for copy in adv_leave + leave:
        copy.wait()


def order(destinations, hidden, adv, key_weight, value_weight):
    rows, width = hidden.shape
    depth, kv_width = key_weight.shape
    slots = rows // SLOT
    anywhere = pl.BlockSpec(memory_space=pl.ANY)
    return pl.pallas_call(
        order_kernel,
        in_specs=[
            pl.BlockSpec(memory_space=pltpu.SMEM),
            anywhere,
            pl.BlockSpec(memory_space=pltpu.VMEM),
            anywhere,
            anywhere,
        ],
        out_specs=[anywhere] * 2,
        out_shape=[
            jax.ShapeDtypeStruct((rows, width + LANES), BF),
            jax.ShapeDtypeStruct((depth, 2 * kv_width), BF),
        ],
        scratch_shapes=[
            pltpu.VMEM((slots, SLOT, width), BF),
            pltpu.VMEM((rows, LANES), BF),
            pltpu.VMEM((depth, 2 * kv_width), BF),
            pltpu.SemaphoreType.DMA((slots,)),
            pltpu.SemaphoreType.DMA((slots,)),
            pltpu.SemaphoreType.DMA((slots,)),
            pltpu.SemaphoreType.DMA((3,)),
        ],
        compiler_params=params(),
        cost_estimate=cost(0, 2 * rows * width),
    )(destinations, hidden, adv, key_weight, value_weight)


def place_rows(lengths_ref, keep_ref, dest_ref, offsets_ref, place, mask, empty):
    rows = place.shape[0]
    dp_count, fsdp_count, slots = lengths_ref.shape
    dp_index, group = dp_fsdp()

    def of_group(ref):
        picked = lax.broadcasted_iota(jnp.int32, (dp_count, fsdp_count, slots), 1) == group
        return jnp.sum(jnp.where(picked, ref[...], 0), axis=1)

    keep = keep_ref[...]
    same = lax.broadcasted_iota(jnp.int32, (dp_count, dp_count), 0) == lax.broadcasted_iota(
        jnp.int32, (dp_count, dp_count), 1
    )
    picked = lax.broadcasted_iota(jnp.int32, keep.shape, 0) == group
    keep_row = jnp.sum(jnp.where(picked, keep, 0), axis=0, keepdims=True)
    keep_column = jnp.sum(jnp.where(same, keep_row, 0), axis=1, keepdims=True)
    kept = lengths_ref[0] * keep[:, 0:1]
    for source in range(1, dp_count):
        kept += lengths_ref[source] * keep[:, source : source + 1]
    count = jnp.sum(kept.astype(F32))
    kept = of_group(lengths_ref) * keep_column
    incoming = (of_group(dest_ref) == dp_index) & (kept > 0)
    offset = jnp.sum(jnp.where(incoming, of_group(offsets_ref), 0), axis=1, keepdims=True)
    length = jnp.sum(jnp.where(incoming, kept, 0), axis=1, keepdims=True)

    offset_row = jnp.sum(jnp.where(same, offset, 0), axis=0, keepdims=True)
    length_row = jnp.sum(jnp.where(same, length, 0), axis=0, keepdims=True)
    source = lax.broadcasted_iota(jnp.int32, (rows, dp_count), 1)
    relative = lax.broadcasted_iota(jnp.int32, (rows, dp_count), 0) - offset_row
    inside = (relative >= 0) & (relative < length_row)
    origin = jnp.sum(
        jnp.where(inside, source * SLOT + relative + 1, 0), axis=1, keepdims=True
    )
    origin = origin - 1
    filled = origin >= 0
    position = jnp.where(filled, lax.rem(origin, SLOT), 0)
    wide = lax.broadcasted_iota(jnp.int32, (rows, rows), 1)
    place[...] = jnp.where(wide == origin, 1.0, 0.0).astype(BF)

    for block, (first, size, window) in enumerate(row_blocks(rows)):
        width = mask.shape[2]
        across = first + lax.rem(lax.broadcasted_iota(jnp.int32, (dp_count, width), 1), size)
        relative = across - offset
        inside = (relative >= 0) & (relative < length)
        reach = jnp.sum(jnp.where(inside, relative + 1, 0), axis=0, keepdims=True)
        row = across[0:1]
        seen = window - SLOT + lax.broadcasted_iota(jnp.int32, (WINDOW, width), 0)
        visible = (seen > row - reach) & (seen <= row)
        mask[block] = jnp.where(visible, 1.0, 0.0)
        empty[block] = jnp.where(reach > 0, 0.0, 1.0)
    return count, position


def attend_kernel(
    lengths_ref,
    keep_ref,
    dest_ref,
    offsets_ref,
    got_ref,
    weight_ref,
    query_ref,
    upstream_ref,
    ratio_ref,
    cos_table_ref,
    sin_table_ref,
    tables_ref,
    out_ref,
    kv_grad_ref,
    rows_buf,
    weight_buf,
    adv_buf,
    sems,
    acc_ref,
    kv_ref,
    kv_pad,
    key_grad,
    value_grad,
    coef_ref,
    place_ref,
    mask_ref,
    empty_ref,
    cos_ref,
    sin_ref,
):
    head = pl.program_id(0)
    rows = query_ref.shape[0]
    kv_width = acc_ref.shape[1] // 2
    blocks, _, depth = rows_buf.shape

    def arrival(k):
        here = pl.ds(pl.multiple_of(k * depth, depth), depth)
        return (
            pltpu.make_async_copy(got_ref.at[:, here], rows_buf.at[k], sems.at[0, k]),
            pltpu.make_async_copy(weight_ref.at[here, :], weight_buf.at[k], sems.at[1, k]),
        )

    def adv_arrival():
        here = pl.ds(blocks * depth, LANES)
        return pltpu.make_async_copy(got_ref.at[:, here], adv_buf, sems.at[0, blocks])

    @pl.when(head == 0)
    def _():
        adv_arrival().start()
        for k in range(AHEAD):
            for copy in arrival(k):
                copy.start()

    @pl.when(head == 0)
    def _():
        count, position = place_rows(
            lengths_ref, keep_ref, dest_ref, offsets_ref, place_ref, mask_ref, empty_ref
        )
        at = lax.broadcasted_iota(jnp.int32, (rows, HD), 1) == position
        at = jnp.where(at, 1.0, 0.0).astype(BF)
        looked_up = jnp.dot(at, tables_ref[...], preferred_element_type=F32)
        for ref, first in ((cos_ref, 0), (sin_ref, 3 * HD)):
            parts = [looked_up[:, first + i * HD : first + (i + 1) * HD] for i in range(3)]
            ref[...] = parts[0] + (parts[1] + parts[2])
        adv_arrival().wait()
        adv = jnp.dot(place_ref[...], adv_buf[...], preferred_element_type=F32)
        ratio = column_of(ratio_ref)
        clipped = (adv > 0) & (ratio > clip_high) | (adv < 0) & (ratio < clip_low)
        coef_ref[...] = jnp.where(clipped, 0.0, adv * ratio) * (-loss_scale / count)

    @pl.when(head == 0)
    def _():
        acc_ref[...] = jnp.zeros_like(acc_ref)

        @pl.loop(0, blocks)
        def _(k):
            for copy in arrival(k):
                copy.wait()

            @pl.when(k + AHEAD < blocks)
            def _():
                for copy in arrival(k + AHEAD):
                    copy.start()

            acc_ref[...] += jnp.dot(rows_buf[k], weight_buf[k], preferred_element_type=F32)

        for slot in range(rows // SLOT):
            here = pl.ds(slot * SLOT, SLOT)
            cosine, sine = cos_table_ref[...], sin_table_ref[...]
            for head in range(kv_width // HD):
                columns = pl.ds(head * HD, HD)
                key = acc_ref[here, columns]
                turned = key * cosine + pltpu.roll(key, HD // 2, 1) * sine
                kv_ref[here, columns] = turned.astype(BF)
            values = pl.ds(kv_width, kv_width)
            kv_ref[here, values] = acc_ref[here, values].astype(BF)
        kv_pad[pl.ds(0, SLOT), :] = jnp.zeros((SLOT, 2 * kv_width), BF)
        kv_pad[pl.ds(SLOT, rows), :] = jnp.dot(
            place_ref[...], kv_ref[...], preferred_element_type=F32
        ).astype(BF)

    attend_head(
        head,
        query_ref,
        upstream_ref,
        out_ref,
        kv_grad_ref,
        kv_pad,
        key_grad,
        value_grad,
        coef_ref,
        place_ref,
        mask_ref,
        empty_ref,
        cos_ref,
        sin_ref,
    )


def attend_head(
    head,
    query_ref,
    upstream_ref,
    out_ref,
    kv_grad_ref,
    kv_pad,
    key_grad,
    value_grad,
    coef_ref,
    place_ref,
    mask_ref,
    empty_ref,
    cos_ref,
    sin_ref,
):
    rows = query_ref.shape[0]
    group = query_ref.shape[1] // HD
    kv_width = kv_pad.shape[1] // 2
    scale = 1.0 / math.sqrt(HD)
    body = pl.ds(SLOT, rows)
    key_columns = pl.ds(pl.multiple_of(head * HD, HD), HD)
    value_columns = pl.ds(pl.multiple_of(kv_width + head * HD, HD), HD)
    across = (((1,), (1,)), ((), ()))
    along = (((0,), (0,)), ((), ()))
    key_grad[...] = jnp.zeros_like(key_grad)
    value_grad[...] = jnp.zeros_like(value_grad)
    for block, (first, size, window) in enumerate(row_blocks(rows)):
        here = pl.ds(first, size)
        span = pl.ds(window, WINDOW)
        coef = coef_ref[here, :]
        many = pl.ds(0, group * size)
        allowed = mask_ref[block, :, many] > 0.0
        empty = empty_ref[block, :, many]
        query = jnp.concatenate(
            [query_ref[here, pl.ds(g * HD, HD)] for g in range(group)], axis=0
        )
        grad = jnp.concatenate(
            [
                (coef * upstream_ref[here, pl.ds(g * HD, HD)].astype(F32)).astype(BF)
                for g in range(group)
            ],
            axis=0,
        )
        key = kv_pad[span, key_columns]
        value = kv_pad[span, value_columns]
        scores = lax.dot_general(key, query, across, preferred_element_type=F32) * scale
        raw = jnp.where(allowed, jnp.exp(scores), 0.0)
        normed = raw * (1.0 / (jnp.sum(raw, axis=0, keepdims=True) + empty))
        normed_low = normed.astype(BF)
        output = lax.dot_general(normed_low, value, along, preferred_element_type=F32).astype(BF)
        for g in range(group):
            out_ref[here, pl.ds(g * HD, HD)] = output[g * size : (g + 1) * size]
        grad_normed = lax.dot_general(value, grad, across, preferred_element_type=F32)
        delta = jnp.sum(normed * grad_normed, axis=0, keepdims=True)
        grad_scores = (normed * (grad_normed - delta) * scale).astype(BF)
        key_grad[span, :] += jnp.dot(grad_scores, query, preferred_element_type=F32)
        value_grad[span, :] += jnp.dot(normed_low, grad, preferred_element_type=F32)
    turned = key_grad[body, :]
    key_back = turned * cos_ref[...] - pltpu.roll(turned, HD // 2, 1) * sin_ref[...]
    both = jnp.concatenate([key_back.astype(BF), value_grad[body, :].astype(BF)], axis=1)
    kv_grad_ref[...] = lax.dot_general(
        both, place_ref[...], along, preferred_element_type=F32
    ).astype(BF)


def attend(plan, got, weights, queries, upstream, ratios):
    rows = got.shape[0]
    width, kv_columns = weights.shape
    heads = kv_columns // (2 * HD)
    query_width = queries.shape[1] // heads
    depth = width // DEPTH_BLOCKS
    blocks, most = len(row_blocks(rows)), WINDOW - SLOT
    anywhere = pl.BlockSpec(memory_space=pl.ANY)
    tables = [jnp.asarray(table) for table in slot_tables() + (lookup_tables(),)]
    whole = lambda array: pl.BlockSpec(array.shape, lambda k: (0,) * array.ndim)
    return pl.pallas_call(
        attend_kernel,
        grid=(heads,),
        in_specs=[whole(array) for array in plan]
        + [
            anywhere,
            anywhere,
            pl.BlockSpec((rows, query_width), lambda h: (0, h)),
            pl.BlockSpec((rows, query_width), lambda h: (0, h)),
            whole(ratios),
            whole(tables[0]),
            whole(tables[1]),
            whole(tables[2]),
        ],
        out_specs=[
            pl.BlockSpec((rows, query_width), lambda h: (0, h)),
            pl.BlockSpec((2 * HD, rows), lambda h: (h, 0)),
        ],
        out_shape=[
            jax.ShapeDtypeStruct(queries.shape, BF),
            jax.ShapeDtypeStruct((kv_columns, rows), BF),
        ],
        scratch_shapes=[
            pltpu.VMEM((DEPTH_BLOCKS, rows, depth), BF),
            pltpu.VMEM((DEPTH_BLOCKS, depth, kv_columns), BF),
            pltpu.VMEM((rows, LANES), BF),
            pltpu.SemaphoreType.DMA((2, DEPTH_BLOCKS + 1)),
            pltpu.VMEM((rows, kv_columns), F32),
            pltpu.VMEM((rows, kv_columns), BF),
            pltpu.VMEM((rows + SLOT, kv_columns), BF),
            pltpu.VMEM((rows + SLOT, HD), F32),
            pltpu.VMEM((rows + SLOT, HD), F32),
            pltpu.VMEM((rows, LANES), F32),
            pltpu.VMEM((rows, rows), BF),
            pltpu.VMEM((blocks, WINDOW, query_width // HD * most), F32),
            pltpu.VMEM((blocks, 1, query_width // HD * most), F32),
            pltpu.VMEM((rows, HD), F32),
            pltpu.VMEM((rows, HD), F32),
        ],
        compiler_params=params(),
        cost_estimate=cost(
            2 * rows * width * kv_columns + 10 * rows * queries.shape[1] * HD,
            rows * width + width * kv_columns + 3 * rows * queries.shape[1],
        ),
    )(*plan, got, weights, queries, upstream, ratios, *tables)


def grad_kernel(
    own_ref,
    other_ref,
    got_ref,
    sibling_ref,
    first_ref,
    rest_ref,
    own_buf,
    other_buf,
    mine_buf,
    sibling_buf,
    first_buf,
    rest_buf,
    sems,
    in_sems,
    out_sems,
):
    piece = mine_buf.shape[2] // 2
    split = first_buf.shape[2]
    blocks = [lax.rem(lax.axis_index("x") + k, RING) for k in range(RING)]
    own = pltpu.make_async_copy(own_ref, own_buf, sems.at[0])
    other = pltpu.make_async_copy(other_ref, other_buf, sems.at[1])

    def arrival(source, target, k, row):
        start = (2 * blocks[k] + lax.axis_index("core")) * piece
        here = pl.ds(pl.multiple_of(start, LANES), piece)
        there = pl.ds((k % 2) * piece, piece)
        return pltpu.make_async_copy(
            source.at[:, here], target.at[k // 2, :, there], in_sems.at[row, k]
        )

    mine = [arrival(got_ref, mine_buf, k, 0) for k in range(RING)]
    sibling = [arrival(sibling_ref, sibling_buf, k, 1) for k in range(RING)]
    early = [own, mine[0], mine[1]]
    late = [[other, sibling[0], sibling[1]], [mine[2], mine[3], sibling[2], sibling[3]]]
    for copy in early + late[0]:
        copy.start()
    for copy in early:
        copy.wait()
    for copy in late[1]:
        copy.start()
    leave = []
    for half in range(2):
        for part in range(ROW_PARTS):
            count = own_buf.shape[0] // ROW_PARTS
            rows = pl.ds(part * count, count)
            product = jnp.dot(own_buf[rows, :], mine_buf[half], preferred_element_type=F32)
            if half == 0 and part == 0:
                for copy in late[0]:
                    copy.wait()
            product += jnp.dot(other_buf[rows, :], sibling_buf[half], preferred_element_type=F32)
            product = product.astype(BF)
            places = rest_buf.shape[1] // ROW_PARTS
            there = pl.ds(part * places, places)
            for k in (2 * half, 2 * half + 1):
                columns = slice((k % 2) * piece, (k % 2 + 1) * piece)
                first_buf[k, rows, :] = product[:, columns][:, :split]
                rest_buf[k, there] = product[:, columns][:, split:].reshape(
                    (places,) + rest_buf.shape[2:]
                )
                pair = (
                    pltpu.make_async_copy(
                        first_buf.at[k, rows], first_ref.at[blocks[k], rows], out_sems.at[0, k, part]
                    ),
                    pltpu.make_async_copy(
                        rest_buf.at[k, there],
                        rest_ref.at[there, blocks[k]],
                        out_sems.at[1, k, part],
                    ),
                )
                for copy in pair:
                    copy.start()
                    leave.append(copy)
        if half == 0:
            for copy in late[1]:
                copy.wait()
    for copy in leave:
        copy.wait()


def grad_parts(own, other, got, sibling, width, places):
    columns, rows = own.shape
    piece = width // (2 * RING)
    split = piece // 5 * SPLIT
    size = columns // places
    anywhere = pl.BlockSpec(memory_space=pl.ANY)
    return pl.pallas_call(
        grad_kernel,
        in_specs=[anywhere] * 4,
        out_specs=[anywhere] * 2,
        out_shape=[
            jax.ShapeDtypeStruct((RING, columns, split), BF),
            jax.ShapeDtypeStruct((places, RING, size, piece - split), BF),
        ],
        scratch_shapes=[
            pltpu.VMEM((columns, rows), BF),
            pltpu.VMEM((columns, rows), BF),
            pltpu.VMEM((2, rows, 2 * piece), BF),
            pltpu.VMEM((2, rows, 2 * piece), BF),
            pltpu.VMEM((RING, columns, split), BF),
            pltpu.VMEM((RING, places, size, piece - split), BF),
            pltpu.SemaphoreType.DMA((2,)),
            pltpu.SemaphoreType.DMA((2, RING)),
            pltpu.SemaphoreType.DMA((2, RING, ROW_PARTS)),
        ],
        compiler_params=params(20 * 1024 * 1024),
        cost_estimate=cost(
            4 * rows * columns * RING * piece, RING * piece * (2 * rows + columns)
        ),
    )(own, other, got, sibling)


def finish_kernel(spread_ref, key_ref, value_ref):
    places, size, _ = spread_ref.shape
    per_head = HD // size
    for i in range(places // per_head):
        rows = [spread_ref[i * per_head + j].astype(F32) for j in range(per_head)]
        out_ref = value_ref if i % 2 else key_ref
        out_ref[:, pl.ds(i // 2 * HD, HD)] = jnp.concatenate(rows, axis=0).T


def finish(spread, kv_width):
    columns = spread.shape[2]
    return pl.pallas_call(
        finish_kernel,
        out_shape=[jax.ShapeDtypeStruct((columns, kv_width), F32)] * 2,
        compiler_params=params(),
        cost_estimate=cost(0, 3 * spread.size),
    )(spread)


def summed(parts):
    return jnp.sum(parts.astype(F32), axis=0)


def swap_cores(value):
    return lax.ppermute(value, "core", [(0, 1), (1, 0)])


def exchange(value, axis):
    return lax.all_to_all(value, axis, split_axis=0, concat_axis=0, tiled=True)


def on_device(
    hidden,
    advantages,
    queries,
    upstream,
    ratios,
    key_weight,
    value_weight,
    lengths,
    keep_flags,
    destinations,
    offsets,
):
    dp_count = lengths.shape[0]
    rows_here, model_width = hidden.shape
    kv_width = key_weight.shape[1]
    adv = advantages.reshape(rows_here // LANES, LANES)
    sent, weights = order(destinations, hidden, adv, key_weight, value_weight)
    weights = lax.all_gather(weights, FSDP, axis=0, tiled=True)
    got = exchange(sent.reshape(dp_count, SLOT, sent.shape[1]), DP).reshape(sent.shape)
    sibling = swap_cores(got)
    plan = (lengths, keep_flags, destinations, offsets)
    ratios = ratios.reshape(rows_here // LANES, LANES)
    attention, own = attend(plan, got, weights, queries, upstream, ratios)
    other = swap_cores(own)

    first, rest = grad_parts(own, other, got, sibling, model_width, dp_count)
    first = lax.psum_scatter(
        first.reshape(-1, first.shape[2]), "x", scatter_dimension=0, tiled=True
    )
    rest = summed(exchange(summed(exchange(rest, DP)).astype(BF), "x"))
    first, rest = lax.optimization_barrier((first, rest))
    first = exchange(first.reshape(dp_count, -1, first.shape[1]), DP)
    share = jnp.concatenate([summed(first), rest], axis=1).astype(BF)
    spread = exchange(jnp.broadcast_to(share[None], (dp_count,) + share.shape), DP)
    grad_key, grad_value = finish(spread, kv_width)
    return (attention, grad_key, grad_value)


def solution(mesh):
    chips = {"y": RING, "z": RING, "x": RING, "core": 2}
    fine = Mesh(mesh.devices.reshape(tuple(chips.values())), tuple(chips))
    in_specs = (
        P(ALL, None),
        P(ALL),
        P(ALL, None),
        P(ALL, None),
        P(ALL),
        P(FSDP, None),
        P(FSDP, None),
        P(),
        P(),
        P(),
        P(),
    )
    out_specs = (P(ALL, None), P(FSDP, None), P(FSDP, None))
    return jax.shard_map(
        on_device, mesh=fine, in_specs=in_specs, out_specs=out_specs, check_vma=False
    )
```

```python
import math

import jax
import jax.numpy as jnp
import ml_dtypes
import numpy as np
from jax import lax
from jax.experimental import pallas as pl
from jax.experimental.pallas import tpu as pltpu
from jax.sharding import Mesh
from jax.sharding import PartitionSpec as P

HD = 128
SLOT = 32
RING = 4
ROW_PARTS = 1
WINDOW = 160
SPLIT = 3
VMEM_LIMIT = 56 * 1024 * 1024

rope_base = 1000000.0
loss_scale = 256.0
clip_low = 0.8
clip_high = 1.28

DP = ("y", "z")
FSDP = ("x", "core")
ALL = DP + FSDP
BF = jnp.bfloat16
F32 = jnp.float32
LANES = 128
DEPTH_BLOCKS = 5
AHEAD = 3


def row_blocks(rows):
    step = WINDOW - SLOT
    blocks = []
    for first in range(0, rows, step):
        size = min(step, rows - first)
        blocks.append((first, size, min(first, rows + SLOT - WINDOW)))
    return blocks


def slot_tables():
    frequency = rope_base ** (-(np.arange(HD // 2) * (2.0 / HD)))
    angle = np.arange(SLOT)[:, None] * frequency[None, :]
    cosine, sine = np.cos(angle), np.sin(angle)
    return (
        np.concatenate([cosine, cosine], axis=1).astype(np.float32),
        np.concatenate([-sine, sine], axis=1).astype(np.float32),
    )


def lookup_tables():
    terms = []
    for table in slot_tables():
        left = table
        for _ in range(3):
            term = left.astype(ml_dtypes.bfloat16)
            left = left - term.astype(np.float32)
            terms.append(term)
    return np.pad(np.concatenate(terms, axis=1), ((0, HD - SLOT), (0, 0)))


def params(limit=VMEM_LIMIT):
    return pltpu.CompilerParams(vmem_limit_bytes=limit)


def cost(flops, count):
    return pl.CostEstimate(flops=int(flops), bytes_accessed=int(2 * count), transcendentals=0)


def dp_fsdp():
    dp_index = lax.axis_index("y") * RING + lax.axis_index("z")
    return dp_index, lax.axis_index("x") * 2 + lax.axis_index("core")


def column_of(row_ref):
    same = lax.broadcasted_iota(jnp.int32, (LANES, LANES), 0) == lax.broadcasted_iota(
        jnp.int32, (LANES, LANES), 1
    )
    parts = []
    for i in range(row_ref.shape[0]):
        row = row_ref[i : i + 1, :].astype(F32)
        parts.append(jnp.sum(jnp.where(same, row, 0.0), axis=1, keepdims=True))
    return jnp.concatenate(parts, axis=0)


def order_kernel(
    dest_ref,
    hidden_ref,
    adv_ref,
    key_ref,
    value_ref,
    sent_ref,
    weight_ref,
    rows_buf,
    adv_buf,
    weight_buf,
    in_sems,
    out_sems,
    adv_sems,
    weight_sems,
):
    dp_index, group = dp_fsdp()
    width = hidden_ref.shape[1]
    kv_width = key_ref.shape[1]
    slots = hidden_ref.shape[0] // SLOT
    both = [
        pltpu.make_async_copy(
            ref, weight_buf.at[:, pl.ds(i * kv_width, kv_width)], weight_sems.at[i]
        )
        for i, ref in enumerate((key_ref, value_ref))
    ]
    arrive, leave, adv_leave = [], [], []
    for slot in range(slots):
        here = pl.ds(slot * SLOT, SLOT)
        there = pl.ds(pl.multiple_of(dest_ref[dp_index, group, slot] * SLOT, SLOT), SLOT)
        arrive.append(
            pltpu.make_async_copy(hidden_ref.at[here, :], rows_buf.at[slot], in_sems.at[slot])
        )
        leave.append(
            pltpu.make_async_copy(
                rows_buf.at[slot], sent_ref.at[there, pl.ds(0, width)], out_sems.at[slot]
            )
        )
        adv_leave.append(
            pltpu.make_async_copy(
                adv_buf.at[here, :], sent_ref.at[there, pl.ds(width, LANES)], adv_sems.at[slot]
            )
        )
    for copy in both + arrive:
        copy.start()
    adv_buf[...] = jnp.broadcast_to(column_of(adv_ref), adv_buf.shape).astype(BF)
    for copy in adv_leave:
        copy.start()
    for copy in both:
        copy.wait()
    out = pltpu.make_async_copy(weight_buf, weight_ref, weight_sems.at[2])
    out.start()
    for slot in range(slots):
        arrive[slot].wait()
        leave[slot].start()
    out.wait()
    for copy in adv_leave + leave:
        copy.wait()


def order(destinations, hidden, adv, key_weight, value_weight):
    rows, width = hidden.shape
    depth, kv_width = key_weight.shape
    slots = rows // SLOT
    anywhere = pl.BlockSpec(memory_space=pl.ANY)
    return pl.pallas_call(
        order_kernel,
        in_specs=[
            pl.BlockSpec(memory_space=pltpu.SMEM),
            anywhere,
            pl.BlockSpec(memory_space=pltpu.VMEM),
            anywhere,
            anywhere,
        ],
        out_specs=[anywhere] * 2,
        out_shape=[
            jax.ShapeDtypeStruct((rows, width + LANES), BF),
            jax.ShapeDtypeStruct((depth, 2 * kv_width), BF),
        ],
        scratch_shapes=[
            pltpu.VMEM((slots, SLOT, width), BF),
            pltpu.VMEM((rows, LANES), BF),
            pltpu.VMEM((depth, 2 * kv_width), BF),
            pltpu.SemaphoreType.DMA((slots,)),
            pltpu.SemaphoreType.DMA((slots,)),
            pltpu.SemaphoreType.DMA((slots,)),
            pltpu.SemaphoreType.DMA((3,)),
        ],
        compiler_params=params(),
        cost_estimate=cost(0, 2 * rows * width),
    )(destinations, hidden, adv, key_weight, value_weight)


def place_rows(lengths_ref, keep_ref, dest_ref, offsets_ref, place, mask, empty):
    rows = place.shape[0]
    dp_count, fsdp_count, slots = lengths_ref.shape
    dp_index, group = dp_fsdp()

    def of_group(ref):
        picked = lax.broadcasted_iota(jnp.int32, (dp_count, fsdp_count, slots), 1) == group
        return jnp.sum(jnp.where(picked, ref[...], 0), axis=1)

    keep = keep_ref[...]
    same = lax.broadcasted_iota(jnp.int32, (dp_count, dp_count), 0) == lax.broadcasted_iota(
        jnp.int32, (dp_count, dp_count), 1
    )
    picked = lax.broadcasted_iota(jnp.int32, keep.shape, 0) == group
    keep_row = jnp.sum(jnp.where(picked, keep, 0), axis=0, keepdims=True)
    keep_column = jnp.sum(jnp.where(same, keep_row, 0), axis=1, keepdims=True)
    kept = lengths_ref[0] * keep[:, 0:1]
    for source in range(1, dp_count):
        kept += lengths_ref[source] * keep[:, source : source + 1]
    count = jnp.sum(kept.astype(F32))
    kept = of_group(lengths_ref) * keep_column
    incoming = (of_group(dest_ref) == dp_index) & (kept > 0)
    offset = jnp.sum(jnp.where(incoming, of_group(offsets_ref), 0), axis=1, keepdims=True)
    length = jnp.sum(jnp.where(incoming, kept, 0), axis=1, keepdims=True)

    offset_row = jnp.sum(jnp.where(same, offset, 0), axis=0, keepdims=True)
    length_row = jnp.sum(jnp.where(same, length, 0), axis=0, keepdims=True)
    source = lax.broadcasted_iota(jnp.int32, (rows, dp_count), 1)
    relative = lax.broadcasted_iota(jnp.int32, (rows, dp_count), 0) - offset_row
    inside = (relative >= 0) & (relative < length_row)
    origin = jnp.sum(
        jnp.where(inside, source * SLOT + relative + 1, 0), axis=1, keepdims=True
    )
    origin = origin - 1
    filled = origin >= 0
    position = jnp.where(filled, lax.rem(origin, SLOT), 0)
    wide = lax.broadcasted_iota(jnp.int32, (rows, rows), 1)
    place[...] = jnp.where(wide == origin, 1.0, 0.0).astype(BF)

    for block, (first, size, window) in enumerate(row_blocks(rows)):
        width = mask.shape[2]
        across = first + lax.rem(lax.broadcasted_iota(jnp.int32, (dp_count, width), 1), size)
        relative = across - offset
        inside = (relative >= 0) & (relative < length)
        reach = jnp.sum(jnp.where(inside, relative + 1, 0), axis=0, keepdims=True)
        row = across[0:1]
        seen = window - SLOT + lax.broadcasted_iota(jnp.int32, (WINDOW, width), 0)
        visible = (seen > row - reach) & (seen <= row)
        mask[block] = jnp.where(visible, 1.0, 0.0)
        empty[block] = jnp.where(reach > 0, 0.0, 1.0)
    return count, position


def attend_kernel(
    lengths_ref,
    keep_ref,
    dest_ref,
    offsets_ref,
    got_ref,
    weight_ref,
    query_ref,
    upstream_ref,
    ratio_ref,
    cos_table_ref,
    sin_table_ref,
    tables_ref,
    out_ref,
    kv_grad_ref,
    rows_buf,
    weight_buf,
    adv_buf,
    sems,
    acc_ref,
    kv_ref,
    kv_pad,
    key_grad,
    value_grad,
    coef_ref,
    place_ref,
    mask_ref,
    empty_ref,
    cos_ref,
    sin_ref,
):
    head = pl.program_id(0)
    rows = query_ref.shape[0]
    kv_width = acc_ref.shape[1] // 2
    blocks, _, depth = rows_buf.shape

    def arrival(k):
        here = pl.ds(pl.multiple_of(k * depth, depth), depth)
        return (
            pltpu.make_async_copy(got_ref.at[:, here], rows_buf.at[k], sems.at[0, k]),
            pltpu.make_async_copy(weight_ref.at[here, :], weight_buf.at[k], sems.at[1, k]),
        )

    def adv_arrival():
        here = pl.ds(blocks * depth, LANES)
        return pltpu.make_async_copy(got_ref.at[:, here], adv_buf, sems.at[0, blocks])

    @pl.when(head == 0)
    def _():
        adv_arrival().start()
        for k in range(AHEAD):
            for copy in arrival(k):
                copy.start()

    @pl.when(head == 0)
    def _():
        count, position = place_rows(
            lengths_ref, keep_ref, dest_ref, offsets_ref, place_ref, mask_ref, empty_ref
        )
        at = lax.broadcasted_iota(jnp.int32, (rows, HD), 1) == position
        at = jnp.where(at, 1.0, 0.0).astype(BF)
        looked_up = jnp.dot(at, tables_ref[...], preferred_element_type=F32)
        for ref, first in ((cos_ref, 0), (sin_ref, 3 * HD)):
            parts = [looked_up[:, first + i * HD : first + (i + 1) * HD] for i in range(3)]
            ref[...] = parts[0] + (parts[1] + parts[2])
        adv_arrival().wait()
        adv = jnp.dot(place_ref[...], adv_buf[...], preferred_element_type=F32)
        ratio = column_of(ratio_ref)
        clipped = (adv > 0) & (ratio > clip_high) | (adv < 0) & (ratio < clip_low)
        coef_ref[...] = jnp.where(clipped, 0.0, adv * ratio) * (-loss_scale / count)

    @pl.when(head == 0)
    def _():
        acc_ref[...] = jnp.zeros_like(acc_ref)

        @pl.loop(0, blocks)
        def _(k):
            for copy in arrival(k):
                copy.wait()

            @pl.when(k + AHEAD < blocks)
            def _():
                for copy in arrival(k + AHEAD):
                    copy.start()

            acc_ref[...] += jnp.dot(rows_buf[k], weight_buf[k], preferred_element_type=F32)

        for slot in range(rows // SLOT):
            here = pl.ds(slot * SLOT, SLOT)
            cosine, sine = cos_table_ref[...], sin_table_ref[...]
            for head in range(kv_width // HD):
                columns = pl.ds(head * HD, HD)
                key = acc_ref[here, columns]
                turned = key * cosine + pltpu.roll(key, HD // 2, 1) * sine
                kv_ref[here, columns] = turned.astype(BF)
            values = pl.ds(kv_width, kv_width)
            kv_ref[here, values] = acc_ref[here, values].astype(BF)
        kv_pad[pl.ds(0, SLOT), :] = jnp.zeros((SLOT, 2 * kv_width), BF)
        kv_pad[pl.ds(SLOT, rows), :] = jnp.dot(
            place_ref[...], kv_ref[...], preferred_element_type=F32
        ).astype(BF)

    attend_head(
        head,
        query_ref,
        upstream_ref,
        out_ref,
        kv_grad_ref,
        kv_pad,
        key_grad,
        value_grad,
        coef_ref,
        place_ref,
        mask_ref,
        empty_ref,
        cos_ref,
        sin_ref,
    )


def attend_head(
    head,
    query_ref,
    upstream_ref,
    out_ref,
    kv_grad_ref,
    kv_pad,
    key_grad,
    value_grad,
    coef_ref,
    place_ref,
    mask_ref,
    empty_ref,
    cos_ref,
    sin_ref,
):
    rows = query_ref.shape[0]
    group = query_ref.shape[1] // HD
    kv_width = kv_pad.shape[1] // 2
    scale = 1.0 / math.sqrt(HD)
    body = pl.ds(SLOT, rows)
    key_columns = pl.ds(pl.multiple_of(head * HD, HD), HD)
    value_columns = pl.ds(pl.multiple_of(kv_width + head * HD, HD), HD)
    across = (((1,), (1,)), ((), ()))
    along = (((0,), (0,)), ((), ()))
    key_grad[...] = jnp.zeros_like(key_grad)
    value_grad[...] = jnp.zeros_like(value_grad)
    for block, (first, size, window) in enumerate(row_blocks(rows)):
        here = pl.ds(first, size)
        span = pl.ds(window, WINDOW)
        coef = coef_ref[here, :]
        many = pl.ds(0, group * size)
        allowed = mask_ref[block, :, many] > 0.0
        empty = empty_ref[block, :, many]
        query = jnp.concatenate(
            [query_ref[here, pl.ds(g * HD, HD)] for g in range(group)], axis=0
        )
        grad = jnp.concatenate(
            [
                (coef * upstream_ref[here, pl.ds(g * HD, HD)].astype(F32)).astype(BF)
                for g in range(group)
            ],
            axis=0,
        )
        key = kv_pad[span, key_columns]
        value = kv_pad[span, value_columns]
        scores = lax.dot_general(key, query, across, preferred_element_type=F32) * scale
        raw = jnp.where(allowed, jnp.exp(scores), 0.0)
        normed = raw * (1.0 / (jnp.sum(raw, axis=0, keepdims=True) + empty))
        normed_low = normed.astype(BF)
        output = lax.dot_general(normed_low, value, along, preferred_element_type=F32).astype(BF)
        for g in range(group):
            out_ref[here, pl.ds(g * HD, HD)] = output[g * size : (g + 1) * size]
        grad_normed = lax.dot_general(value, grad, across, preferred_element_type=F32)
        delta = jnp.sum(normed * grad_normed, axis=0, keepdims=True)
        grad_scores = (normed * (grad_normed - delta) * scale).astype(BF)
        key_grad[span, :] += jnp.dot(grad_scores, query, preferred_element_type=F32)
        value_grad[span, :] += jnp.dot(normed_low, grad, preferred_element_type=F32)
    turned = key_grad[body, :]
    key_back = turned * cos_ref[...] - pltpu.roll(turned, HD // 2, 1) * sin_ref[...]
    both = jnp.concatenate([key_back.astype(BF), value_grad[body, :].astype(BF)], axis=1)
    kv_grad_ref[...] = lax.dot_general(
        both, place_ref[...], along, preferred_element_type=F32
    ).astype(BF)


def attend(plan, got, weights, queries, upstream, ratios):
    rows = got.shape[0]
    width, kv_columns = weights.shape
    heads = kv_columns // (2 * HD)
    query_width = queries.shape[1] // heads
    depth = width // DEPTH_BLOCKS
    blocks, most = len(row_blocks(rows)), WINDOW - SLOT
    anywhere = pl.BlockSpec(memory_space=pl.ANY)
    tables = [jnp.asarray(table) for table in slot_tables() + (lookup_tables(),)]
    whole = lambda array: pl.BlockSpec(array.shape, lambda k: (0,) * array.ndim)
    return pl.pallas_call(
        attend_kernel,
        grid=(heads,),
        in_specs=[whole(array) for array in plan]
        + [
            anywhere,
            anywhere,
            pl.BlockSpec((rows, query_width), lambda h: (0, h)),
            pl.BlockSpec((rows, query_width), lambda h: (0, h)),
            whole(ratios),
            whole(tables[0]),
            whole(tables[1]),
            whole(tables[2]),
        ],
        out_specs=[
            pl.BlockSpec((rows, query_width), lambda h: (0, h)),
            pl.BlockSpec((2 * HD, rows), lambda h: (h, 0)),
        ],
        out_shape=[
            jax.ShapeDtypeStruct(queries.shape, BF),
            jax.ShapeDtypeStruct((kv_columns, rows), BF),
        ],
        scratch_shapes=[
            pltpu.VMEM((DEPTH_BLOCKS, rows, depth), BF),
            pltpu.VMEM((DEPTH_BLOCKS, depth, kv_columns), BF),
            pltpu.VMEM((rows, LANES), BF),
            pltpu.SemaphoreType.DMA((2, DEPTH_BLOCKS + 1)),
            pltpu.VMEM((rows, kv_columns), F32),
            pltpu.VMEM((rows, kv_columns), BF),
            pltpu.VMEM((rows + SLOT, kv_columns), BF),
            pltpu.VMEM((rows + SLOT, HD), F32),
            pltpu.VMEM((rows + SLOT, HD), F32),
            pltpu.VMEM((rows, LANES), F32),
            pltpu.VMEM((rows, rows), BF),
            pltpu.VMEM((blocks, WINDOW, query_width // HD * most), F32),
            pltpu.VMEM((blocks, 1, query_width // HD * most), F32),
            pltpu.VMEM((rows, HD), F32),
            pltpu.VMEM((rows, HD), F32),
        ],
        compiler_params=params(),
        cost_estimate=cost(
            2 * rows * width * kv_columns + 10 * rows * queries.shape[1] * HD,
            rows * width + width * kv_columns + 3 * rows * queries.shape[1],
        ),
    )(*plan, got, weights, queries, upstream, ratios, *tables)


def grad_kernel(
    own_ref,
    other_ref,
    got_ref,
    sibling_ref,
    first_ref,
    rest_ref,
    own_buf,
    other_buf,
    mine_buf,
    sibling_buf,
    first_buf,
    rest_buf,
    sems,
    in_sems,
    out_sems,
):
    piece = mine_buf.shape[2] // 2
    split = first_buf.shape[2]
    blocks = [lax.rem(lax.axis_index("x") + k, RING) for k in range(RING)]
    own = pltpu.make_async_copy(own_ref, own_buf, sems.at[0])
    other = pltpu.make_async_copy(other_ref, other_buf, sems.at[1])

    def arrival(source, target, k, row):
        start = (2 * blocks[k] + lax.axis_index("core")) * piece
        here = pl.ds(pl.multiple_of(start, LANES), piece)
        there = pl.ds((k % 2) * piece, piece)
        return pltpu.make_async_copy(
            source.at[:, here], target.at[k // 2, :, there], in_sems.at[row, k]
        )

    mine = [arrival(got_ref, mine_buf, k, 0) for k in range(RING)]
    sibling = [arrival(sibling_ref, sibling_buf, k, 1) for k in range(RING)]
    early = [own, mine[0], mine[1]]
    late = [[other, sibling[0], sibling[1]], [mine[2], mine[3], sibling[2], sibling[3]]]
    for copy in early + late[0]:
        copy.start()
    for copy in early:
        copy.wait()
    for copy in late[1]:
        copy.start()
    leave = []
    for half in range(2):
        for part in range(ROW_PARTS):
            count = own_buf.shape[0] // ROW_PARTS
            rows = pl.ds(part * count, count)
            product = jnp.dot(own_buf[rows, :], mine_buf[half], preferred_element_type=F32)
            if half == 0 and part == 0:
                for copy in late[0]:
                    copy.wait()
            product += jnp.dot(other_buf[rows, :], sibling_buf[half], preferred_element_type=F32)
            product = product.astype(BF)
            places = rest_buf.shape[1] // ROW_PARTS
            there = pl.ds(part * places, places)
            for k in (2 * half, 2 * half + 1):
                columns = slice((k % 2) * piece, (k % 2 + 1) * piece)
                first_buf[k, rows, :] = product[:, columns][:, :split]
                rest_buf[k, there] = product[:, columns][:, split:].reshape(
                    (places,) + rest_buf.shape[2:]
                )
                pair = (
                    pltpu.make_async_copy(
                        first_buf.at[k, rows], first_ref.at[blocks[k], rows], out_sems.at[0, k, part]
                    ),
                    pltpu.make_async_copy(
                        rest_buf.at[k, there],
                        rest_ref.at[there, blocks[k]],
                        out_sems.at[1, k, part],
                    ),
                )
                for copy in pair:
                    copy.start()
                    leave.append(copy)
        if half == 0:
            for copy in late[1]:
                copy.wait()
    for copy in leave:
        copy.wait()


def grad_parts(own, other, got, sibling, width, places):
    columns, rows = own.shape
    piece = width // (2 * RING)
    split = piece // 5 * SPLIT
    size = columns // places
    anywhere = pl.BlockSpec(memory_space=pl.ANY)
    in_hbm = pl.BlockSpec(memory_space=pltpu.HBM)
    return pl.pallas_call(
        grad_kernel,
        in_specs=[in_hbm, anywhere, in_hbm, in_hbm],
        out_specs=[anywhere] * 2,
        out_shape=[
            jax.ShapeDtypeStruct((RING, columns, split), BF),
            jax.ShapeDtypeStruct((places, RING, size, piece - split), BF),
        ],
        scratch_shapes=[
            pltpu.VMEM((columns, rows), BF),
            pltpu.VMEM((columns, rows), BF),
            pltpu.VMEM((2, rows, 2 * piece), BF),
            pltpu.VMEM((2, rows, 2 * piece), BF),
            pltpu.VMEM((RING, columns, split), BF),
            pltpu.VMEM((RING, places, size, piece - split), BF),
            pltpu.SemaphoreType.DMA((2,)),
            pltpu.SemaphoreType.DMA((2, RING)),
            pltpu.SemaphoreType.DMA((2, RING, ROW_PARTS)),
        ],
        compiler_params=params(20 * 1024 * 1024),
        cost_estimate=cost(
            4 * rows * columns * RING * piece, RING * piece * (2 * rows + columns)
        ),
    )(
        pltpu.with_memory_space_constraint(own, pltpu.HBM),
        other,
        pltpu.with_memory_space_constraint(got, pltpu.HBM),
        pltpu.with_memory_space_constraint(sibling, pltpu.HBM),
    )


def finish_kernel(spread_ref, key_ref, value_ref, key_buf, value_buf, sems):
    places, size, columns = spread_ref.shape
    per_head = HD // size
    leave = []
    for tile in range(columns // LANES):
        here = pl.ds(tile * LANES, LANES)
        for i in range(places // per_head):
            rows = [spread_ref[i * per_head + j, :, here].astype(F32) for j in range(per_head)]
            buf = value_buf if i % 2 else key_buf
            buf[here, pl.ds(i // 2 * HD, HD)] = jnp.concatenate(rows, axis=0).T
        for i, (buf, out_ref) in enumerate(((key_buf, key_ref), (value_buf, value_ref))):
            copy = pltpu.make_async_copy(buf.at[here, :], out_ref.at[here, :], sems.at[i, tile])
            copy.start()
            leave.append(copy)
    for copy in leave:
        copy.wait()


def finish(spread, kv_width):
    columns = spread.shape[2]
    anywhere = pl.BlockSpec(memory_space=pl.ANY)
    return pl.pallas_call(
        finish_kernel,
        in_specs=[pl.BlockSpec(memory_space=pltpu.VMEM)],
        out_specs=[anywhere, anywhere],
        out_shape=[jax.ShapeDtypeStruct((columns, kv_width), F32)] * 2,
        scratch_shapes=[
            pltpu.VMEM((columns, kv_width), F32),
            pltpu.VMEM((columns, kv_width), F32),
            pltpu.SemaphoreType.DMA((2, columns // LANES)),
        ],
        compiler_params=params(),
        cost_estimate=cost(0, 3 * spread.size),
    )(spread)


def summed(parts):
    return jnp.sum(parts.astype(F32), axis=0)


def swap_cores(value):
    return lax.ppermute(value, "core", [(0, 1), (1, 0)])


def exchange(value, axis):
    return lax.all_to_all(value, axis, split_axis=0, concat_axis=0, tiled=True)


def on_device(
    hidden,
    advantages,
    queries,
    upstream,
    ratios,
    key_weight,
    value_weight,
    lengths,
    keep_flags,
    destinations,
    offsets,
):
    dp_count = lengths.shape[0]
    rows_here, model_width = hidden.shape
    kv_width = key_weight.shape[1]
    adv = advantages.reshape(rows_here // LANES, LANES)
    sent, weights = order(destinations, hidden, adv, key_weight, value_weight)
    weights = lax.all_gather(weights, FSDP, axis=0, tiled=True)
    got = exchange(sent.reshape(dp_count, SLOT, sent.shape[1]), DP).reshape(sent.shape)
    sibling = swap_cores(got)
    plan = (lengths, keep_flags, destinations, offsets)
    ratios = ratios.reshape(rows_here // LANES, LANES)
    attention, own = attend(plan, got, weights, queries, upstream, ratios)
    other = swap_cores(own)

    first, rest = grad_parts(own, other, got, sibling, model_width, dp_count)
    first = lax.psum_scatter(
        first.reshape(-1, first.shape[2]), "x", scatter_dimension=0, tiled=True
    )
    rest = summed(exchange(summed(exchange(rest, DP)).astype(BF), "x"))
    first, rest = lax.optimization_barrier((first, rest))
    first = exchange(first.reshape(dp_count, -1, first.shape[1]), DP)
    share = jnp.concatenate([summed(first), rest], axis=1).astype(BF)
    spread = exchange(jnp.broadcast_to(share[None], (dp_count,) + share.shape), DP)
    grad_key, grad_value = finish(spread, kv_width)
    return (attention, grad_key, grad_value)


def solution(mesh):
    chips = {"y": RING, "z": RING, "x": RING, "core": 2}
    fine = Mesh(mesh.devices.reshape(tuple(chips.values())), tuple(chips))
    in_specs = (
        P(ALL, None),
        P(ALL),
        P(ALL, None),
        P(ALL, None),
        P(ALL),
        P(FSDP, None),
        P(FSDP, None),
        P(),
        P(),
        P(),
        P(),
    )
    out_specs = (P(ALL, None), P(FSDP, None), P(FSDP, None))
    return jax.shard_map(
        on_device, mesh=fine, in_specs=in_specs, out_specs=out_specs, check_vma=False
    )
```

```python
import math

import jax
import jax.numpy as jnp
import ml_dtypes
import numpy as np
from jax import lax
from jax.experimental import pallas as pl
from jax.experimental.pallas import tpu as pltpu
from jax.sharding import Mesh
from jax.sharding import PartitionSpec as P

HD = 128
SLOT = 32
RING = 4
ROW_PARTS = 2
WINDOW = 160
SPLIT = 3
VMEM_LIMIT = 56 * 1024 * 1024

rope_base = 1000000.0
loss_scale = 256.0
clip_low = 0.8
clip_high = 1.28

DP = ("y", "z")
FSDP = ("x", "core")
ALL = DP + FSDP
BF = jnp.bfloat16
F32 = jnp.float32
LANES = 128
DEPTH_BLOCKS = 5
AHEAD = 3


def row_blocks(rows):
    step = WINDOW - SLOT
    blocks = []
    for first in range(0, rows, step):
        size = min(step, rows - first)
        blocks.append((first, size, min(first, rows + SLOT - WINDOW)))
    return blocks


def slot_tables():
    frequency = rope_base ** (-(np.arange(HD // 2) * (2.0 / HD)))
    angle = np.arange(SLOT)[:, None] * frequency[None, :]
    cosine, sine = np.cos(angle), np.sin(angle)
    return (
        np.concatenate([cosine, cosine], axis=1).astype(np.float32),
        np.concatenate([-sine, sine], axis=1).astype(np.float32),
    )


def lookup_tables():
    terms = []
    for table in slot_tables():
        left = table
        for _ in range(3):
            term = left.astype(ml_dtypes.bfloat16)
            left = left - term.astype(np.float32)
            terms.append(term)
    return np.pad(np.concatenate(terms, axis=1), ((0, HD - SLOT), (0, 0)))


def params(limit=VMEM_LIMIT):
    return pltpu.CompilerParams(vmem_limit_bytes=limit)


def cost(flops, count):
    return pl.CostEstimate(flops=int(flops), bytes_accessed=int(2 * count), transcendentals=0)


def dp_fsdp():
    dp_index = lax.axis_index("y") * RING + lax.axis_index("z")
    return dp_index, lax.axis_index("x") * 2 + lax.axis_index("core")


def column_of(row_ref):
    same = lax.broadcasted_iota(jnp.int32, (LANES, LANES), 0) == lax.broadcasted_iota(
        jnp.int32, (LANES, LANES), 1
    )
    parts = []
    for i in range(row_ref.shape[0]):
        row = row_ref[i : i + 1, :].astype(F32)
        parts.append(jnp.sum(jnp.where(same, row, 0.0), axis=1, keepdims=True))
    return jnp.concatenate(parts, axis=0)


def order_kernel(
    dest_ref,
    hidden_ref,
    adv_ref,
    key_ref,
    value_ref,
    sent_ref,
    weight_ref,
    rows_buf,
    adv_buf,
    weight_buf,
    in_sems,
    out_sems,
    adv_sems,
    weight_sems,
):
    dp_index, group = dp_fsdp()
    width = hidden_ref.shape[1]
    kv_width = key_ref.shape[1]
    slots = hidden_ref.shape[0] // SLOT
    both = [
        pltpu.make_async_copy(
            ref, weight_buf.at[:, pl.ds(i * kv_width, kv_width)], weight_sems.at[i]
        )
        for i, ref in enumerate((key_ref, value_ref))
    ]
    arrive, leave, adv_leave = [], [], []
    for slot in range(slots):
        here = pl.ds(slot * SLOT, SLOT)
        there = pl.ds(pl.multiple_of(dest_ref[dp_index, group, slot] * SLOT, SLOT), SLOT)
        arrive.append(
            pltpu.make_async_copy(hidden_ref.at[here, :], rows_buf.at[slot], in_sems.at[slot])
        )
        leave.append(
            pltpu.make_async_copy(
                rows_buf.at[slot], sent_ref.at[there, pl.ds(0, width)], out_sems.at[slot]
            )
        )
        adv_leave.append(
            pltpu.make_async_copy(
                adv_buf.at[here, :], sent_ref.at[there, pl.ds(width, LANES)], adv_sems.at[slot]
            )
        )
    for copy in both + arrive:
        copy.start()
    adv_buf[...] = jnp.broadcast_to(column_of(adv_ref), adv_buf.shape).astype(BF)
    for copy in adv_leave:
        copy.start()
    for copy in both:
        copy.wait()
    out = pltpu.make_async_copy(weight_buf, weight_ref, weight_sems.at[2])
    out.start()
    for slot in range(slots):
        arrive[slot].wait()
        leave[slot].start()
    out.wait()
    for copy in adv_leave + leave:
        copy.wait()


def order(destinations, hidden, adv, key_weight, value_weight):
    rows, width = hidden.shape
    depth, kv_width = key_weight.shape
    slots = rows // SLOT
    anywhere = pl.BlockSpec(memory_space=pl.ANY)
    return pl.pallas_call(
        order_kernel,
        in_specs=[
            pl.BlockSpec(memory_space=pltpu.SMEM),
            anywhere,
            pl.BlockSpec(memory_space=pltpu.VMEM),
            anywhere,
            anywhere,
        ],
        out_specs=[anywhere] * 2,
        out_shape=[
            jax.ShapeDtypeStruct((rows, width + LANES), BF),
            jax.ShapeDtypeStruct((depth, 2 * kv_width), BF),
        ],
        scratch_shapes=[
            pltpu.VMEM((slots, SLOT, width), BF),
            pltpu.VMEM((rows, LANES), BF),
            pltpu.VMEM((depth, 2 * kv_width), BF),
            pltpu.SemaphoreType.DMA((slots,)),
            pltpu.SemaphoreType.DMA((slots,)),
            pltpu.SemaphoreType.DMA((slots,)),
            pltpu.SemaphoreType.DMA((3,)),
        ],
        compiler_params=params(),
        cost_estimate=cost(0, 2 * rows * width),
    )(destinations, hidden, adv, key_weight, value_weight)


def place_rows(lengths_ref, keep_ref, dest_ref, offsets_ref, place, mask, empty):
    rows = place.shape[0]
    dp_count, fsdp_count, slots = lengths_ref.shape
    dp_index, group = dp_fsdp()

    def of_group(ref):
        picked = lax.broadcasted_iota(jnp.int32, (dp_count, fsdp_count, slots), 1) == group
        return jnp.sum(jnp.where(picked, ref[...], 0), axis=1)

    keep = keep_ref[...]
    same = lax.broadcasted_iota(jnp.int32, (dp_count, dp_count), 0) == lax.broadcasted_iota(
        jnp.int32, (dp_count, dp_count), 1
    )
    picked = lax.broadcasted_iota(jnp.int32, keep.shape, 0) == group
    keep_row = jnp.sum(jnp.where(picked, keep, 0), axis=0, keepdims=True)
    keep_column = jnp.sum(jnp.where(same, keep_row, 0), axis=1, keepdims=True)
    kept = lengths_ref[0] * keep[:, 0:1]
    for source in range(1, dp_count):
        kept += lengths_ref[source] * keep[:, source : source + 1]
    count = jnp.sum(kept.astype(F32))
    kept = of_group(lengths_ref) * keep_column
    incoming = (of_group(dest_ref) == dp_index) & (kept > 0)
    offset = jnp.sum(jnp.where(incoming, of_group(offsets_ref), 0), axis=1, keepdims=True)
    length = jnp.sum(jnp.where(incoming, kept, 0), axis=1, keepdims=True)

    offset_row = jnp.sum(jnp.where(same, offset, 0), axis=0, keepdims=True)
    length_row = jnp.sum(jnp.where(same, length, 0), axis=0, keepdims=True)
    source = lax.broadcasted_iota(jnp.int32, (rows, dp_count), 1)
    relative = lax.broadcasted_iota(jnp.int32, (rows, dp_count), 0) - offset_row
    inside = (relative >= 0) & (relative < length_row)
    origin = jnp.sum(
        jnp.where(inside, source * SLOT + relative + 1, 0), axis=1, keepdims=True
    )
    origin = origin - 1
    filled = origin >= 0
    position = jnp.where(filled, lax.rem(origin, SLOT), 0)
    wide = lax.broadcasted_iota(jnp.int32, (rows, rows), 1)
    place[...] = jnp.where(wide == origin, 1.0, 0.0).astype(BF)

    for block, (first, size, window) in enumerate(row_blocks(rows)):
        width = mask.shape[2]
        across = first + lax.rem(lax.broadcasted_iota(jnp.int32, (dp_count, width), 1), size)
        relative = across - offset
        inside = (relative >= 0) & (relative < length)
        reach = jnp.sum(jnp.where(inside, relative + 1, 0), axis=0, keepdims=True)
        row = across[0:1]
        seen = window - SLOT + lax.broadcasted_iota(jnp.int32, (WINDOW, width), 0)
        visible = (seen > row - reach) & (seen <= row)
        mask[block] = jnp.where(visible, 1.0, 0.0)
        empty[block] = jnp.where(reach > 0, 0.0, 1.0)
    return count, position


def attend_kernel(
    lengths_ref,
    keep_ref,
    dest_ref,
    offsets_ref,
    got_ref,
    weight_ref,
    query_ref,
    upstream_ref,
    ratio_ref,
    cos_table_ref,
    sin_table_ref,
    tables_ref,
    out_ref,
    kv_grad_ref,
    rows_buf,
    weight_buf,
    adv_buf,
    sems,
    acc_ref,
    kv_ref,
    kv_pad,
    key_grad,
    value_grad,
    coef_ref,
    place_ref,
    mask_ref,
    empty_ref,
    cos_ref,
    sin_ref,
):
    head = pl.program_id(0)
    rows = query_ref.shape[0]
    kv_width = acc_ref.shape[1] // 2
    blocks, _, depth = rows_buf.shape

    def arrival(k):
        here = pl.ds(pl.multiple_of(k * depth, depth), depth)
        return (
            pltpu.make_async_copy(got_ref.at[:, here], rows_buf.at[k], sems.at[0, k]),
            pltpu.make_async_copy(weight_ref.at[here, :], weight_buf.at[k], sems.at[1, k]),
        )

    def adv_arrival():
        here = pl.ds(blocks * depth, LANES)
        return pltpu.make_async_copy(got_ref.at[:, here], adv_buf, sems.at[0, blocks])

    @pl.when(head == 0)
    def _():
        adv_arrival().start()
        for k in range(AHEAD):
            for copy in arrival(k):
                copy.start()

    @pl.when(head == 0)
    def _():
        count, position = place_rows(
            lengths_ref, keep_ref, dest_ref, offsets_ref, place_ref, mask_ref, empty_ref
        )
        at = lax.broadcasted_iota(jnp.int32, (rows, HD), 1) == position
        at = jnp.where(at, 1.0, 0.0).astype(BF)
        looked_up = jnp.dot(at, tables_ref[...], preferred_element_type=F32)
        for ref, first in ((cos_ref, 0), (sin_ref, 3 * HD)):
            parts = [looked_up[:, first + i * HD : first + (i + 1) * HD] for i in range(3)]
            ref[...] = parts[0] + (parts[1] + parts[2])
        adv_arrival().wait()
        adv = jnp.dot(place_ref[...], adv_buf[...], preferred_element_type=F32)
        ratio = column_of(ratio_ref)
        clipped = (adv > 0) & (ratio > clip_high) | (adv < 0) & (ratio < clip_low)
        coef_ref[...] = jnp.where(clipped, 0.0, adv * ratio) * (-loss_scale / count)

    @pl.when(head == 0)
    def _():
        acc_ref[...] = jnp.zeros_like(acc_ref)

        @pl.loop(0, blocks)
        def _(k):
            for copy in arrival(k):
                copy.wait()

            @pl.when(k + AHEAD < blocks)
            def _():
                for copy in arrival(k + AHEAD):
                    copy.start()

            acc_ref[...] += jnp.dot(rows_buf[k], weight_buf[k], preferred_element_type=F32)

        for slot in range(rows // SLOT):
            here = pl.ds(slot * SLOT, SLOT)
            cosine, sine = cos_table_ref[...], sin_table_ref[...]
            for head in range(kv_width // HD):
                columns = pl.ds(head * HD, HD)
                key = acc_ref[here, columns]
                turned = key * cosine + pltpu.roll(key, HD // 2, 1) * sine
                kv_ref[here, columns] = turned.astype(BF)
            values = pl.ds(kv_width, kv_width)
            kv_ref[here, values] = acc_ref[here, values].astype(BF)
        kv_pad[pl.ds(0, SLOT), :] = jnp.zeros((SLOT, 2 * kv_width), BF)
        kv_pad[pl.ds(SLOT, rows), :] = jnp.dot(
            place_ref[...], kv_ref[...], preferred_element_type=F32
        ).astype(BF)

    attend_head(
        head,
        query_ref,
        upstream_ref,
        out_ref,
        kv_grad_ref,
        kv_pad,
        key_grad,
        value_grad,
        coef_ref,
        place_ref,
        mask_ref,
        empty_ref,
        cos_ref,
        sin_ref,
    )


def attend_head(
    head,
    query_ref,
    upstream_ref,
    out_ref,
    kv_grad_ref,
    kv_pad,
    key_grad,
    value_grad,
    coef_ref,
    place_ref,
    mask_ref,
    empty_ref,
    cos_ref,
    sin_ref,
):
    rows = query_ref.shape[0]
    group = query_ref.shape[1] // HD
    kv_width = kv_pad.shape[1] // 2
    scale = 1.0 / math.sqrt(HD)
    body = pl.ds(SLOT, rows)
    key_columns = pl.ds(pl.multiple_of(head * HD, HD), HD)
    value_columns = pl.ds(pl.multiple_of(kv_width + head * HD, HD), HD)
    across = (((1,), (1,)), ((), ()))
    along = (((0,), (0,)), ((), ()))
    key_grad[...] = jnp.zeros_like(key_grad)
    value_grad[...] = jnp.zeros_like(value_grad)
    for block, (first, size, window) in enumerate(row_blocks(rows)):
        here = pl.ds(first, size)
        span = pl.ds(window, WINDOW)
        coef = coef_ref[here, :]
        many = pl.ds(0, group * size)
        allowed = mask_ref[block, :, many] > 0.0
        empty = empty_ref[block, :, many]
        query = jnp.concatenate(
            [query_ref[here, pl.ds(g * HD, HD)] for g in range(group)], axis=0
        )
        grad = jnp.concatenate(
            [
                (coef * upstream_ref[here, pl.ds(g * HD, HD)].astype(F32)).astype(BF)
                for g in range(group)
            ],
            axis=0,
        )
        key = kv_pad[span, key_columns]
        value = kv_pad[span, value_columns]
        scores = lax.dot_general(key, query, across, preferred_element_type=F32) * scale
        raw = jnp.where(allowed, jnp.exp(scores), 0.0)
        normed = raw * (1.0 / (jnp.sum(raw, axis=0, keepdims=True) + empty))
        normed_low = normed.astype(BF)
        output = lax.dot_general(normed_low, value, along, preferred_element_type=F32).astype(BF)
        for g in range(group):
            out_ref[here, pl.ds(g * HD, HD)] = output[g * size : (g + 1) * size]
        grad_normed = lax.dot_general(value, grad, across, preferred_element_type=F32)
        delta = jnp.sum(normed * grad_normed, axis=0, keepdims=True)
        grad_scores = (normed * (grad_normed - delta) * scale).astype(BF)
        key_grad[span, :] += jnp.dot(grad_scores, query, preferred_element_type=F32)
        value_grad[span, :] += jnp.dot(normed_low, grad, preferred_element_type=F32)
    turned = key_grad[body, :]
    key_back = turned * cos_ref[...] - pltpu.roll(turned, HD // 2, 1) * sin_ref[...]
    both = jnp.concatenate([key_back.astype(BF), value_grad[body, :].astype(BF)], axis=1)
    kv_grad_ref[...] = lax.dot_general(
        both, place_ref[...], along, preferred_element_type=F32
    ).astype(BF)


def attend(plan, got, weights, queries, upstream, ratios):
    rows = got.shape[0]
    width, kv_columns = weights.shape
    heads = kv_columns // (2 * HD)
    query_width = queries.shape[1] // heads
    depth = width // DEPTH_BLOCKS
    blocks, most = len(row_blocks(rows)), WINDOW - SLOT
    anywhere = pl.BlockSpec(memory_space=pl.ANY)
    tables = [jnp.asarray(table) for table in slot_tables() + (lookup_tables(),)]
    whole = lambda array: pl.BlockSpec(array.shape, lambda k: (0,) * array.ndim)
    return pl.pallas_call(
        attend_kernel,
        grid=(heads,),
        in_specs=[whole(array) for array in plan]
        + [
            anywhere,
            anywhere,
            pl.BlockSpec((rows, query_width), lambda h: (0, h)),
            pl.BlockSpec((rows, query_width), lambda h: (0, h)),
            whole(ratios),
            whole(tables[0]),
            whole(tables[1]),
            whole(tables[2]),
        ],
        out_specs=[
            pl.BlockSpec((rows, query_width), lambda h: (0, h)),
            pl.BlockSpec((2 * HD, rows), lambda h: (h, 0)),
        ],
        out_shape=[
            jax.ShapeDtypeStruct(queries.shape, BF),
            jax.ShapeDtypeStruct((kv_columns, rows), BF),
        ],
        scratch_shapes=[
            pltpu.VMEM((DEPTH_BLOCKS, rows, depth), BF),
            pltpu.VMEM((DEPTH_BLOCKS, depth, kv_columns), BF),
            pltpu.VMEM((rows, LANES), BF),
            pltpu.SemaphoreType.DMA((2, DEPTH_BLOCKS + 1)),
            pltpu.VMEM((rows, kv_columns), F32),
            pltpu.VMEM((rows, kv_columns), BF),
            pltpu.VMEM((rows + SLOT, kv_columns), BF),
            pltpu.VMEM((rows + SLOT, HD), F32),
            pltpu.VMEM((rows + SLOT, HD), F32),
            pltpu.VMEM((rows, LANES), F32),
            pltpu.VMEM((rows, rows), BF),
            pltpu.VMEM((blocks, WINDOW, query_width // HD * most), F32),
            pltpu.VMEM((blocks, 1, query_width // HD * most), F32),
            pltpu.VMEM((rows, HD), F32),
            pltpu.VMEM((rows, HD), F32),
        ],
        compiler_params=params(),
        cost_estimate=cost(
            2 * rows * width * kv_columns + 10 * rows * queries.shape[1] * HD,
            rows * width + width * kv_columns + 3 * rows * queries.shape[1],
        ),
    )(*plan, got, weights, queries, upstream, ratios, *tables)


def grad_kernel(
    own_ref,
    other_ref,
    got_ref,
    sibling_ref,
    first_ref,
    rest_ref,
    own_buf,
    other_buf,
    mine_buf,
    sibling_buf,
    first_buf,
    rest_buf,
    sems,
    in_sems,
    out_sems,
):
    piece = mine_buf.shape[2] // 2
    split = first_buf.shape[2]
    blocks = [lax.rem(lax.axis_index("x") + k, RING) for k in range(RING)]
    own = pltpu.make_async_copy(own_ref, own_buf, sems.at[0])
    other = pltpu.make_async_copy(other_ref, other_buf, sems.at[1])

    def arrival(source, target, k, row):
        start = (2 * blocks[k] + lax.axis_index("core")) * piece
        here = pl.ds(pl.multiple_of(start, LANES), piece)
        there = pl.ds((k % 2) * piece, piece)
        return pltpu.make_async_copy(
            source.at[:, here], target.at[k // 2, :, there], in_sems.at[row, k]
        )

    mine = [arrival(got_ref, mine_buf, k, 0) for k in range(RING)]
    sibling = [arrival(sibling_ref, sibling_buf, k, 1) for k in range(RING)]
    early = [own, mine[0], mine[1]]
    late = [[other, sibling[0], sibling[1]], [mine[2], mine[3], sibling[2], sibling[3]]]
    for copy in early + late[0]:
        copy.start()
    for copy in early:
        copy.wait()
    for copy in late[1]:
        copy.start()
    leave = []
    for half in range(2):
        for part in range(ROW_PARTS):
            count = own_buf.shape[0] // ROW_PARTS
            rows = pl.ds(part * count, count)
            product = jnp.dot(own_buf[rows, :], mine_buf[half], preferred_element_type=F32)
            if half == 0 and part == 0:
                for copy in late[0]:
                    copy.wait()
            product += jnp.dot(other_buf[rows, :], sibling_buf[half], preferred_element_type=F32)
            product = product.astype(BF)
            places = rest_buf.shape[1] // ROW_PARTS
            there = pl.ds(part * places, places)
            for k in (2 * half, 2 * half + 1):
                columns = slice((k % 2) * piece, (k % 2 + 1) * piece)
                first_buf[k, rows, :] = product[:, columns][:, :split]
                rest_buf[k, there] = product[:, columns][:, split:].reshape(
                    (places,) + rest_buf.shape[2:]
                )
                pair = (
                    pltpu.make_async_copy(
                        first_buf.at[k, rows], first_ref.at[blocks[k], rows], out_sems.at[0, k, part]
                    ),
                    pltpu.make_async_copy(
                        rest_buf.at[k, there],
                        rest_ref.at[there, blocks[k]],
                        out_sems.at[1, k, part],
                    ),
                )
                for copy in pair:
                    copy.start()
                    leave.append(copy)
        if half == 0:
            for copy in late[1]:
                copy.wait()
    for copy in leave:
        copy.wait()


def grad_parts(own, other, got, sibling, width, places):
    columns, rows = own.shape
    piece = width // (2 * RING)
    split = piece // 5 * SPLIT
    size = columns // places
    anywhere = pl.BlockSpec(memory_space=pl.ANY)
    in_hbm = pl.BlockSpec(memory_space=pltpu.HBM)
    return pl.pallas_call(
        grad_kernel,
        in_specs=[in_hbm, anywhere, in_hbm, in_hbm],
        out_specs=[anywhere] * 2,
        out_shape=[
            jax.ShapeDtypeStruct((RING, columns, split), BF),
            jax.ShapeDtypeStruct((places, RING, size, piece - split), BF),
        ],
        scratch_shapes=[
            pltpu.VMEM((columns, rows), BF),
            pltpu.VMEM((columns, rows), BF),
            pltpu.VMEM((2, rows, 2 * piece), BF),
            pltpu.VMEM((2, rows, 2 * piece), BF),
            pltpu.VMEM((RING, columns, split), BF),
            pltpu.VMEM((RING, places, size, piece - split), BF),
            pltpu.SemaphoreType.DMA((2,)),
            pltpu.SemaphoreType.DMA((2, RING)),
            pltpu.SemaphoreType.DMA((2, RING, ROW_PARTS)),
        ],
        compiler_params=params(20 * 1024 * 1024),
        cost_estimate=cost(
            4 * rows * columns * RING * piece, RING * piece * (2 * rows + columns)
        ),
    )(
        pltpu.with_memory_space_constraint(own, pltpu.HBM),
        other,
        pltpu.with_memory_space_constraint(got, pltpu.HBM),
        pltpu.with_memory_space_constraint(sibling, pltpu.HBM),
    )


def finish_kernel(spread_ref, key_ref, value_ref, key_buf, value_buf, sems):
    places, size, columns = spread_ref.shape
    per_head = HD // size
    leave = []
    for tile in range(columns // LANES):
        here = pl.ds(tile * LANES, LANES)
        for i in range(places // per_head):
            rows = [spread_ref[i * per_head + j, :, here].astype(F32) for j in range(per_head)]
            buf = value_buf if i % 2 else key_buf
            buf[here, pl.ds(i // 2 * HD, HD)] = jnp.concatenate(rows, axis=0).T
        for i, (buf, out_ref) in enumerate(((key_buf, key_ref), (value_buf, value_ref))):
            copy = pltpu.make_async_copy(buf.at[here, :], out_ref.at[here, :], sems.at[i, tile])
            copy.start()
            leave.append(copy)
    for copy in leave:
        copy.wait()


def finish(spread, kv_width):
    columns = spread.shape[2]
    anywhere = pl.BlockSpec(memory_space=pl.ANY)
    return pl.pallas_call(
        finish_kernel,
        in_specs=[pl.BlockSpec(memory_space=pltpu.VMEM)],
        out_specs=[anywhere, anywhere],
        out_shape=[jax.ShapeDtypeStruct((columns, kv_width), F32)] * 2,
        scratch_shapes=[
            pltpu.VMEM((columns, kv_width), F32),
            pltpu.VMEM((columns, kv_width), F32),
            pltpu.SemaphoreType.DMA((2, columns // LANES)),
        ],
        compiler_params=params(),
        cost_estimate=cost(0, 3 * spread.size),
    )(spread)


def summed(parts):
    return jnp.sum(parts.astype(F32), axis=0)


def swap_cores(value):
    return lax.ppermute(value, "core", [(0, 1), (1, 0)])


def exchange(value, axis):
    return lax.all_to_all(value, axis, split_axis=0, concat_axis=0, tiled=True)


def on_device(
    hidden,
    advantages,
    queries,
    upstream,
    ratios,
    key_weight,
    value_weight,
    lengths,
    keep_flags,
    destinations,
    offsets,
):
    dp_count = lengths.shape[0]
    rows_here, model_width = hidden.shape
    kv_width = key_weight.shape[1]
    adv = advantages.reshape(rows_here // LANES, LANES)
    sent, weights = order(destinations, hidden, adv, key_weight, value_weight)
    weights = lax.all_gather(weights, FSDP, axis=0, tiled=True)
    got = exchange(sent.reshape(dp_count, SLOT, sent.shape[1]), DP).reshape(sent.shape)
    sibling = swap_cores(got)
    plan = (lengths, keep_flags, destinations, offsets)
    ratios = ratios.reshape(rows_here // LANES, LANES)
    attention, own = attend(plan, got, weights, queries, upstream, ratios)
    other = swap_cores(own)

    first, rest = grad_parts(own, other, got, sibling, model_width, dp_count)
    first = lax.psum_scatter(
        first.reshape(-1, first.shape[2]), "x", scatter_dimension=0, tiled=True
    )
    rest = summed(exchange(summed(exchange(rest, DP)).astype(BF), "x"))
    first, rest = lax.optimization_barrier((first, rest))
    first = exchange(first.reshape(dp_count, -1, first.shape[1]), DP)
    share = jnp.concatenate([summed(first), rest], axis=1).astype(BF)
    spread = exchange(jnp.broadcast_to(share[None], (dp_count,) + share.shape), DP)
    grad_key, grad_value = finish(spread, kv_width)
    return (attention, grad_key, grad_value)


def solution(mesh):
    chips = {"y": RING, "z": RING, "x": RING, "core": 2}
    fine = Mesh(mesh.devices.reshape(tuple(chips.values())), tuple(chips))
    in_specs = (
        P(ALL, None),
        P(ALL),
        P(ALL, None),
        P(ALL, None),
        P(ALL),
        P(FSDP, None),
        P(FSDP, None),
        P(),
        P(),
        P(),
        P(),
    )
    out_specs = (P(ALL, None), P(FSDP, None), P(FSDP, None))
    return jax.shard_map(
        on_device, mesh=fine, in_specs=in_specs, out_specs=out_specs, check_vma=False
    )
```
